128 devices in a mesh: member: 8 (over y, z_lo), space: 16 (over z_hi, x, core).
Axes of the slice: x: 4, y: 4, z: 4 (z_hi: 2, z_lo: 2; z = z_hi * 2 + z_lo), core: 2. Of those that a mesh axis runs over, the one named last changes fastest.
Arguments:
- tokens: bfloat16 [16, 2048, 1024], P('member', 'space'), may hold values from -6 to 6
- w_qkv: bfloat16 [1024, 3072], replicated, may hold values from -0.1875 to 0.1875
- w_out: bfloat16 [1024, 1024], replicated, may hold values from -1.5 to 1.5
- w_hidden: bfloat16 [1024, 1024], replicated, may hold values from -0.1875 to 0.1875
- decoder_readout_matrix: bfloat16 [1024, 128], replicated, may hold values from -0.1875 to 0.1875
- edge_token: int32 [16384, 3], P('space'), may hold values from 0 to 2047, as said below
- edge_weight: float32 [16384, 3], P('space'), may hold values from 0.2 to 1
- truth_state: float32 [16384, 128], P('space'), may hold values from -6 to 6
- area: float32 [16384], P('space'), may hold values from 0.3 to 3
Outputs:
- grad_tokens: bfloat16 [16, 2048, 1024], P('member', 'space')
- grad_qkv_w: float32 [1024, 3072], P(('member', 'space'))
- grad_out_w: float32 [1024, 1024], P(('member', 'space'))
- grad_hidden_w: float32 [1024, 1024], P(('member', 'space'))
- decoder_readout_derivative: float32 [1024, 128], P(('member', 'space'))
The draws below stay inside these ranges and needn't reach their ends.
Inputs may be any that keep to these rules, and one draw needn't show every extreme that they name: edge_token[c, e] // 128 == c // 1024: a cell's edges reach tokens of its own block.
All inputs are finite; a program needn't handle non-finite values.
Results may differ from the reference program's by a relative error of at most 0.017.
Values may be sent and summed in bfloat16 or wider, within the bound.
A program may use at most 192 MiB of HBM per device.

```python
import math
import jax
import jax.numpy as jnp
from jax import lax

D = 1024
HEADS = 16
VARS = 128
NE = 3
TOK_DEV = 128
CELLS_DEV = 1024
HALF = 64
MEMBERS = 16
TOKENS = 2048
NCELLS = 16384


def draw_edge_token(key, part):
    key = jax.random.fold_in(key, 7)
    cell_ids = jnp.arange(NCELLS, dtype=jnp.int32)
    cell_block = cell_ids // CELLS_DEV
    cell_local = cell_ids % CELLS_DEV
    nearest = cell_local * TOK_DEV // CELLS_DEV
    jitter = jax.random.randint(key, (NCELLS, NE), -4, 5, dtype=jnp.int32)
    jitter = jitter.at[:, 0].set(0)
    token_local = jnp.clip(nearest[:, None] + jitter, 0, TOK_DEV - 1)
    return (cell_block[:, None] * TOK_DEV + token_local).astype(jnp.int32)


def with_spikes(array, key, source, target, parts, factor):
    owner, partner = [(jnp.arange(array.shape[dim]) // (array.shape[dim] // parts)).reshape([-1 if axis == dim else 1 for axis in range(array.ndim)]) for dim in (source, target)]
    chosen = jax.random.permutation(key, parts)[partner]
    strong = (owner == chosen) | (owner == (partner + parts // 2) % parts)
    return jnp.where(strong, factor * array, array)


def steps_of(rng, dims, pieces, least, largest):
    factor_of, own = 1.0, jax.random.fold_in(rng, 6)
    for position, blocks in pieces:
        heights = jnp.exp(jax.random.uniform(jax.random.fold_in(own, position), (blocks,), jnp.float32, least / len(pieces), largest / len(pieces)))
        factor_of = factor_of * jnp.repeat(heights, dims[position] // blocks).reshape([-1 if axis == position else 1 for axis in range(len(dims))])
    return factor_of


def scatter_about(stream_key, extent, spread, most, cuts=(), held_as=jnp.bfloat16):
    values = jax.random.normal(stream_key, extent, jnp.float32) * spread
    if len(cuts) > 0:
        values = steps_of(stream_key, extent, cuts, -0.22, 0.18) * values
    return jnp.clip(values, min=-most, max=most).astype(held_as)


def noise_with(own_key, shape, deviation, most, pieces, heavy, held_as=jnp.bfloat16):
    array = deviation * jax.random.normal(own_key, shape, jnp.float32)
    if pieces:
        array = array * steps_of(own_key, shape, pieces, -0.22, 0.18)
    return jnp.clip(with_spikes(array, jax.random.fold_in(own_key, 3), *heavy), -most, most).astype(held_as)


def setup_inputs(seed: int = 0) -> dict:
    key_of = jax.random.split(jax.random.key(seed), 10)
    tokens = noise_with(key_of[0], (MEMBERS, TOKENS, D), 1.0, 6.0, ((0, 8), (1, 16)), (1, 2, 16, 2.0))
    w_qkv = scatter_about(key_of[1], (D, 3 * D), D ** -0.5, 0.1875)
    w_out = scatter_about(key_of[2], (D, D), (D // 64) ** -0.5, 1.5)
    w_hidden = scatter_about(key_of[3], (D, D), D ** -0.5, 0.1875)
    decoder_readout_matrix = scatter_about(key_of[4], (D, VARS), D ** -0.5, 0.1875)
    edge_token = draw_edge_token(jax.random.fold_in(key_of[9], 71), 0)
    edge_weight = jnp.clip(0.2 + 0.8 * jax.random.uniform(key_of[6], (NCELLS, NE), jnp.float32) ** steps_of(key_of[6], (NCELLS, NE), ((0, 16),), -0.2, 0.2), 0.2, 1.0)
    truth_state = scatter_about(key_of[7], (NCELLS, VARS), 1.0, 6.0, ((0, 16),), jnp.float32)
    area = jnp.clip(jnp.exp(math.log(3.0) - 2.3025851 * jax.random.uniform(key_of[8], (NCELLS,), jnp.float32) ** steps_of(key_of[8], (NCELLS,), ((0, 16),), -0.2, 0.2)), 0.3, 3.0)
    return {"tokens": tokens, "w_qkv": w_qkv, "w_out": w_out, "w_hidden": w_hidden, "decoder_readout_matrix": decoder_readout_matrix, "edge_token": edge_token, "edge_weight": edge_weight, "truth_state": truth_state, "area": area}


EPS = 1e-05
ALPHA = 0.95
DELTA = 0.1

def norm_stats(values):
    wide = values.astype(jnp.float32)
    centre = wide - lax.optimization_barrier(jnp.mean(wide, axis=-1, keepdims=True))
    inverse = lax.rsqrt(lax.optimization_barrier(jnp.mean(centre * centre, axis=-1, keepdims=True)) + EPS)
    return (centre * inverse, inverse)

def norm_back(objective_derivative, normal_hat, inverse):
    first = lax.optimization_barrier(jnp.mean(objective_derivative, axis=-1, keepdims=True))
    second = lax.optimization_barrier(jnp.mean(objective_derivative * normal_hat, axis=-1, keepdims=True))
    return inverse * (objective_derivative - first - normal_hat * second)

def criterion_derivative(diff):
    return diff / jnp.sqrt(diff * diff + DELTA * DELTA)

def window_mask(row_count, reach, first_row, token_count):
    query_pos = jnp.arange(row_count, dtype=jnp.int32)[:, None]
    key_pos = jnp.arange(row_count + 2 * reach, dtype=jnp.int32)[None, :]
    global_key = first_row - reach + key_pos
    inside = (key_pos >= query_pos) & (key_pos <= query_pos + 2 * reach)
    inside = inside & (global_key >= 0) & (global_key < token_count)
    return inside.astype(jnp.float32)

def split_heads(queries, extended, head_count):
    member_dev, row_count, feature_count = queries.shape
    head_dim = feature_count // head_count
    query_h = queries.reshape(member_dev, row_count, head_count, head_dim).astype(jnp.float32)
    key_h = extended[..., :feature_count].reshape(member_dev, -1, head_count, head_dim).astype(jnp.float32)
    value_h = extended[..., feature_count:].reshape(member_dev, -1, head_count, head_dim).astype(jnp.float32)
    return (query_h, key_h, value_h, head_dim)

def attend(queries, extended, window, head_count):
    member_dev, row_count, feature_count = queries.shape
    query_h, key_h, value_h, head_dim = split_heads(queries, extended, head_count)
    scores = jnp.einsum('mahd,mrhd->mhar', query_h, key_h) / math.sqrt(head_dim)
    expo = jnp.exp(scores) * window
    probs = expo / lax.optimization_barrier(jnp.sum(expo, axis=-1, keepdims=True))
    probs_b = probs.astype(jnp.bfloat16)
    result = jnp.einsum('mhar,mrhd->mahd', probs_b.astype(jnp.float32), value_h)
    return (result.astype(jnp.bfloat16).reshape(member_dev, row_count, feature_count), probs, probs_b)

def attend_back(queries, extended, probs, probs_b, grad_att, head_count):
    member_dev, row_count, feature_count = queries.shape
    query_h, key_h, value_h, head_dim = split_heads(queries, extended, head_count)
    grad_h = grad_att.reshape(member_dev, row_count, head_count, head_dim).astype(jnp.float32)
    dprob = jnp.einsum('mahd,mrhd->mhar', grad_h, value_h)
    inner = lax.optimization_barrier(jnp.sum(probs * dprob, axis=-1, keepdims=True))
    dscore = (probs * (dprob - inner) / math.sqrt(head_dim)).astype(jnp.bfloat16).astype(jnp.float32)
    grad_q = jnp.einsum('mhar,mrhd->mahd', dscore, key_h).reshape(member_dev, row_count, feature_count)
    grad_k = jnp.einsum('mhar,mahd->mrhd', dscore, query_h).reshape(member_dev, -1, feature_count)
    grad_v = jnp.einsum('mhar,mahd->mrhd', probs_b.astype(jnp.float32), grad_h).reshape(member_dev, -1, feature_count)
    return (grad_q, jnp.concatenate([grad_k, grad_v], axis=-1))

def unblock(stacked):
    block_count, member_dev, row_count, feature_count = stacked.shape
    return jnp.transpose(stacked, (1, 0, 2, 3)).reshape(member_dev, block_count * row_count, feature_count)

def reference(tokens, w_qkv, w_out, w_hidden, decoder_readout_matrix, edge_token, edge_weight, truth_state, area):
    sample_number, token_count, feature_count = tokens.shape
    location_number = truth_state.shape[0]
    normal_hat, inverse = norm_stats(tokens)
    normed = normal_hat.astype(jnp.bfloat16)
    flat_normed = normed.reshape(-1, feature_count)
    qkv = jnp.dot(flat_normed, w_qkv, preferred_element_type=jnp.float32).astype(jnp.bfloat16)
    qkv = qkv.reshape(sample_number, token_count, 3 * feature_count)
    queries = qkv[..., :feature_count]
    keyvals = jnp.pad(qkv[..., feature_count:], ((0, 0), (HALF, HALF), (0, 0)))
    block_ids = jnp.arange(token_count // TOK_DEV, dtype=jnp.int32)

    def block_inputs(block):
        first_row = (block * TOK_DEV).astype(jnp.int32)
        query_block = lax.dynamic_slice_in_dim(queries, first_row, TOK_DEV, 1)
        key_block = lax.dynamic_slice_in_dim(keyvals, first_row, TOK_DEV + 2 * HALF, 1)
        return (first_row, query_block, key_block, window_mask(TOK_DEV, HALF, first_row, token_count))

    def forward_block(block):
        first_row, query_block, key_block, window = block_inputs(block)
        return attend(query_block, key_block, window, HEADS)[0]
    attended = unblock(lax.map(forward_block, block_ids))
    flat_att = attended.reshape(-1, feature_count)
    states = tokens.astype(jnp.float32) + jnp.dot(flat_att, w_out, preferred_element_type=jnp.float32).reshape(tokens.shape)
    states = states.astype(jnp.bfloat16)
    agg = jnp.zeros((sample_number, location_number, feature_count), jnp.float32)
    for edge_slot in range(edge_token.shape[1]):
        agg = agg + edge_weight[:, edge_slot][None, :, None] * states[:, edge_token[:, edge_slot]].astype(jnp.float32)
    agg_b = agg.astype(jnp.bfloat16).reshape(-1, feature_count)
    pre = jnp.dot(agg_b, w_hidden, preferred_element_type=jnp.float32)
    hidden_state_entries = jax.nn.gelu(pre, approximate=False).astype(jnp.bfloat16)
    sample_prediction = jnp.dot(hidden_state_entries, decoder_readout_matrix, preferred_element_type=jnp.float32).reshape(sample_number, location_number, -1)
    objective_multiplier = math.sqrt(sample_number / location_number)
    eps_fair = (1.0 - ALPHA) / sample_number
    diagonal_contribution = criterion_derivative(sample_prediction - truth_state[None])
    sample_dispersion = lax.map(lambda lone_sample: lax.optimization_barrier(jnp.sum(criterion_derivative(lone_sample[None] - sample_prediction), axis=0)), sample_prediction)
    objective_derivative = objective_multiplier * area[None, :, None] * (diagonal_contribution / sample_number - (1.0 - eps_fair) / (sample_number * (sample_number - 1)) * sample_dispersion)
    prediction_derivative = objective_derivative.astype(jnp.bfloat16).reshape(-1, sample_prediction.shape[2])
    decoder_readout_derivative = jnp.dot(hidden_state_entries.T, prediction_derivative, preferred_element_type=jnp.float32)
    hidden_state_derivative = jnp.dot(prediction_derivative, decoder_readout_matrix.T, preferred_element_type=jnp.float32)
    unused, gelu_back = jax.vjp(lambda inner_pre: jax.nn.gelu(inner_pre, approximate=False), pre)
    grad_pre = gelu_back(hidden_state_derivative)[0].astype(jnp.bfloat16)
    grad_hidden_w = jnp.dot(agg_b.T, grad_pre, preferred_element_type=jnp.float32)
    grad_agg = jnp.dot(grad_pre, w_hidden.T, preferred_element_type=jnp.float32).reshape(sample_number, location_number, feature_count)
    grad_states = jnp.zeros(tokens.shape, jnp.float32)
    for edge_slot in range(edge_token.shape[1]):
        grad_states = grad_states.at[:, edge_token[:, edge_slot]].add(edge_weight[:, edge_slot][None, :, None] * grad_agg)
    flat_gs = grad_states.astype(jnp.bfloat16).reshape(-1, feature_count)
    grad_out_w = jnp.dot(flat_att.T, flat_gs, preferred_element_type=jnp.float32)
    grad_att = jnp.dot(flat_gs, w_out.T, preferred_element_type=jnp.float32).astype(jnp.bfloat16).reshape(tokens.shape)

    def backward_block(block):
        first_row, query_block, key_block, window = block_inputs(block)
        unused_out, probs, probs_b = attend(query_block, key_block, window, HEADS)
        grad_block = lax.dynamic_slice_in_dim(grad_att, first_row, TOK_DEV, 1)
        return attend_back(query_block, key_block, probs, probs_b, grad_block, HEADS)
    grad_q_blocks, grad_kv_blocks = lax.map(backward_block, block_ids)
    middle = grad_kv_blocks[:, :, HALF:HALF + TOK_DEV]
    lower_part = grad_kv_blocks[:, :, :HALF]
    upper_part = grad_kv_blocks[:, :, HALF + TOK_DEV:]
    lower_next = jnp.concatenate([lower_part[1:], jnp.zeros_like(lower_part[:1])], axis=0)
    upper_prev = jnp.concatenate([jnp.zeros_like(upper_part[:1]), upper_part[:-1]], axis=0)
    middle = middle.at[:, :, TOK_DEV - HALF:].add(lower_next)
    middle = middle.at[:, :, :HALF].add(upper_prev)
    grad_qkv = jnp.concatenate([unblock(grad_q_blocks), unblock(middle)], axis=-1).astype(jnp.bfloat16)
    grad_qkv = grad_qkv.reshape(-1, 3 * feature_count)
    grad_qkv_w = jnp.dot(flat_normed.T, grad_qkv, preferred_element_type=jnp.float32)
    grad_normed = jnp.dot(grad_qkv, w_qkv.T, preferred_element_type=jnp.float32).reshape(tokens.shape)
    grad_tokens = (grad_states + norm_back(grad_normed, normal_hat, inverse)).astype(jnp.bfloat16)
    return (grad_tokens, grad_qkv_w, grad_out_w, grad_hidden_w, decoder_readout_derivative)
```

```python
import functools
import math

import jax
import jax.numpy as jnp
from jax import lax
from jax.experimental import pallas as pl
from jax.experimental.pallas import tpu as pltpu
from jax.sharding import PartitionSpec as P

HEADS = 16


EPS = 1e-05
ALPHA = 0.95
DELTA = 0.1


MESH = pl.DeviceIdType.MESH


class Place:
    def __init__(self):
        member, space = lax.axis_index("member"), lax.axis_index("space")
        self.member, self.space = member, space
        self.y, z_lo = member // 2, member % 2
        z_hi = space // 8
        self.x, self.core = (space // 2) % 4, space % 2
        self.z = z_hi * 2 + z_lo
        self.partner = (member, space + 1 - 2 * self.core)

    def ring(self, axis):
        return {"x": self.x, "y": self.y, "z": self.z}[axis]

    def device(self, axis, j):
        if axis == "x":
            return (self.member, (self.space // 8) * 8 + j * 2 + self.core)
        if axis == "y":
            return (j * 2 + self.member % 2, self.space)
        return ((self.member // 2) * 2 + j % 2, (j // 2) * 8 + self.space % 8)

    def neighbours(self):
        found = []
        for axis in "xyz":
            i = self.ring(axis)
            found += [self.device(axis, (i + 1) % 4), self.device(axis, (i + 3) % 4)]
        return found


def entry_barrier(devices):
    barrier = pltpu.get_barrier_semaphore()
    for device in devices:
        pl.semaphore_signal(barrier, inc=1, device_id=device, device_id_type=MESH)
    pl.semaphore_wait(barrier, len(devices))


ORDERS = (
    (
        ("x", (4, 2, 2), lambda j, r: (*r, j)),
        ("y", (2, 2), lambda j, r: (j, *r)),
        ("z", (), lambda j, r: (j % 2, j // 2)),
    ),
    (
        ("y", (2, 2, 4), lambda j, r: (j, *r)),
        ("z", (4,), lambda j, r: (j % 2, j // 2, *r)),
        ("x", (), lambda j, r: (j,)),
    ),
    (
        ("z", (4, 4), lambda j, r: (r[0], j % 2, j // 2, r[1])),
        ("x", (4,), lambda j, r: (r[0], j)),
        ("y", (), lambda j, r: (j,)),
    ),
)
FULL = (4, 2, 2, 4)


def first_columns(width):
    return width // 128 // 2 * 128


def sum_scratch(width):
    low = first_columns(width)
    shapes = []
    for order in ORDERS:
        for phase, (_, rest, _) in enumerate(order):
            for columns in (width, width, low, width - low):
                shapes.append(pltpu.VMEM((*rest, 16, columns), jnp.bfloat16))
            if phase < 2:
                shapes.append(pltpu.VMEM((*rest, 16, width), jnp.bfloat16))
    return shapes + [pltpu.SemaphoreType.DMA((54,)), pltpu.SemaphoreType.DMA((54,))]


def over(dims, body):
    if len(dims) <= 1:
        body((slice(None),) * len(dims))
        return
    count = math.prod(dims[:-1])

    def step(n, carry):
        index = []
        for size in reversed(dims[:-1]):
            index.insert(0, lax.rem(n, size))
            n = n // size
        body((*index, slice(None)))
        return carry

    lax.fori_loop(0, count, step, 0)


class RingSum:
    def __init__(self, place, width, parts, scratch, finish):
        self.place, self.width, self.low = place, width, first_columns(width)
        scratch = list(scratch)
        self.recv, self.send = scratch.pop(), scratch.pop()
        self.slots = []
        for _ in range(3):
            self.slots.append([])
            for phase in range(3):
                count = 5 if phase < 2 else 4
                self.slots[-1].append(scratch[:count])
                scratch = scratch[count:]
        self.data = [[part] for part in parts]
        for part in range(3):
            self.data[part] += [self.slots[part][phase][4] for phase in range(2)]
        self.finish = finish
        self.copies = {}

    def copy(self, part, phase, message, source, target, device):
        sem = (part * 3 + phase) * 6 + message
        made = pltpu.make_async_remote_copy(
            src_ref=source, dst_ref=target, send_sem=self.send.at[sem], recv_sem=self.recv.at[sem],
            device_id=device, device_id_type=MESH,
        )
        made.start()
        self.copies[part, phase, message] = made

    def view(self, part, phase, j, low):
        _, rest, at = ORDERS[part][phase]
        columns = pl.ds(0, self.low) if low else pl.ds(self.low, self.width - self.low)
        return self.data[part][phase].at[(*at(j, (slice(None),) * len(rest)), slice(None), columns)]

    def around(self, part, phase):
        axis = ORDERS[part][phase][0]
        i = self.place.ring(axis)
        right, left = (i + 1) % 4, (i + 3) % 4
        return i, right, left, (i + 2) % 4, self.place.device(axis, right), self.place.device(axis, left)

    def open(self, part, phase):
        _, right, left, opposite, to_right, to_left = self.around(part, phase)
        from_left, from_right, relay_left, relay_right = self.slots[part][phase][:4]
        low, high = pl.ds(0, self.low), pl.ds(self.low, self.width - self.low)
        self.copy(part, phase, 0, self.view(part, phase, opposite, True), relay_left, to_right)
        self.copy(part, phase, 1, self.view(part, phase, opposite, False), relay_right, to_left)
        self.copy(part, phase, 2, self.view(part, phase, right, False), from_left.at[..., high], to_right)
        self.copy(part, phase, 3, self.view(part, phase, left, True), from_right.at[..., low], to_left)

    def relay(self, part, phase):
        _, right, left, _, to_right, to_left = self.around(part, phase)
        _, rest, at = ORDERS[part][phase]
        from_left, from_right, relay_left, relay_right = self.slots[part][phase][:4]
        low, high = pl.ds(0, self.low), pl.ds(self.low, self.width - self.low)
        data = self.data[part][phase]
        for message, j, columns, relayed in ((0, right, low, relay_left), (1, left, high, relay_right)):
            self.copies[part, phase, message].wait_recv()

            def add(r, j=j, columns=columns, relayed=relayed):
                here = (*at(j, r), slice(None), columns)
                there = (*r, slice(None), slice(None))
                both = data[here].astype(jnp.float32) + relayed[there].astype(jnp.float32)
                data[here] = both.astype(jnp.bfloat16)

            over(rest, add)
            if message == 0:
                self.copy(part, phase, 4, self.view(part, phase, right, True), from_left.at[..., low], to_right)
            else:
                self.copy(part, phase, 5, self.view(part, phase, left, False), from_right.at[..., high], to_left)

    def close(self, part, phase):
        i = self.around(part, phase)[0]
        _, rest, at = ORDERS[part][phase]
        from_left, from_right = self.slots[part][phase][:2]
        data = self.data[part][phase]
        for message in (2, 3, 4, 5):
            self.copies[part, phase, message].wait_recv()

        def add(r):
            there = (*r, slice(None), slice(None))
            total = data[(*at(i, r), slice(None), slice(None))].astype(jnp.float32)
            total = total + from_left[there].astype(jnp.float32) + from_right[there].astype(jnp.float32)
            if phase < 2:
                self.data[part][phase + 1][there] = total.astype(jnp.bfloat16)
            else:
                self.finish(part, total)

        over(rest, add)

    def run(self):
        for phase in range(3):
            for part in range(3):
                self.open(part, phase)
            for part in range(3):
                self.relay(part, phase)
            for part in range(3):
                self.close(part, phase)

    def drain(self):
        for made in self.copies.values():
            made.wait_send()


def weight_sum_kernel(width, g_ref, out_ref, acc, partner_part, final, pair_sems, final_sems, *scratch):
    place = Place()
    entry_barrier([place.partner, *place.neighbours()])
    core = place.core
    swaps = []
    for part in range(3):
        swap = pltpu.make_async_remote_copy(
            src_ref=g_ref.at[1 - core, part], dst_ref=partner_part.at[part],
            send_sem=pair_sems.at[0, part], recv_sem=pair_sems.at[1, part],
            device_id=place.partner, device_id_type=MESH,
        )
        swap.start()
        swaps.append(swap)

    def finish(part, total):
        final[part] = total.reshape(2, 8, width)

    sums = RingSum(place, width, [acc.at[part] for part in range(3)], scratch, finish)
    for part in range(3):
        swaps[part].wait_recv()

        def add(r, part=part):
            here = (part, *r, slice(None), slice(None))
            both = g_ref[(core, *here)].astype(jnp.float32) + partner_part[here].astype(jnp.float32)
            acc[here] = both.astype(jnp.bfloat16)

        over(FULL, add)
        sums.open(part, 0)
    for phase in range(3):
        if phase:
            for part in range(3):
                sums.open(part, phase)
        for part in range(3):
            sums.relay(part, phase)
        for part in range(3):
            sums.close(part, phase)
    last = pltpu.make_async_remote_copy(
        src_ref=final.at[:, 1 - core], dst_ref=out_ref.at[core],
        send_sem=final_sems.at[0], recv_sem=final_sems.at[1],
        device_id=place.partner, device_id_type=MESH,
    )
    last.start()
    out_ref[core] = final[:, core]
    last.wait()
    for swap in swaps:
        swap.wait_send()
    sums.drain()


def weight_sum(g):
    width = g.shape[-1]
    whole = pltpu.VMEM((3, *FULL, 16, width), jnp.bfloat16)
    return pl.pallas_call(
        functools.partial(weight_sum_kernel, width),
        out_shape=jax.ShapeDtypeStruct((2, 3, 8, width), jnp.float32),
        in_specs=[pl.BlockSpec(memory_space=pltpu.VMEM)],
        out_specs=pl.BlockSpec(memory_space=pltpu.VMEM),
        scratch_shapes=[
            whole, whole, pltpu.VMEM((3, 2, 8, width), jnp.float32),
            pltpu.SemaphoreType.DMA((2, 3)), pltpu.SemaphoreType.DMA((2,)), *sum_scratch(width),
        ],
        compiler_params=pltpu.CompilerParams(
            collective_id=0, has_side_effects=True, vmem_limit_bytes=58 * 2**20
        ),
    )(g.reshape(2, 3, *FULL, 16, width))


def extended_2(array, sides, width):
    for axis, dim in sides:
        count, length = (lax.axis_size(axis), array.shape[dim])
        up = [(i, (i + 1) % count) for i in range(count - 1)]
        down = [(j, i) for i, j in up]
        last = lax.slice_in_dim(array, length - width, length, axis=dim)
        initial = lax.slice_in_dim(array, 0, width, axis=dim)
        before = lax.ppermute(last, axis, up)
        after = lax.ppermute(initial, axis, down)
        array = jnp.concatenate([before, array, after], axis=dim)
    return array


def passed_along(value, axis, steps):
    count = lax.axis_size(axis)
    initial, last = (max(0, -steps), min(count, count - steps))
    return lax.ppermute(value, axis, [(source, source + steps) for source in range(initial, last)])


def norm_stats(values):
    wide = values.astype(jnp.float32)
    centre = wide - jnp.mean(wide, axis=-1, keepdims=True)
    inverse = lax.rsqrt(jnp.mean(centre * centre, axis=-1, keepdims=True) + EPS)
    return (centre * inverse, inverse)


def norm_back(objective_derivative, normal_hat, inverse):
    first = jnp.mean(objective_derivative, axis=-1, keepdims=True)
    second = jnp.mean(objective_derivative * normal_hat, axis=-1, keepdims=True)
    return inverse * (objective_derivative - first - normal_hat * second)


def criterion_derivative(diff):
    return diff / jnp.sqrt(diff * diff + DELTA * DELTA)


def window_mask(row_count, reach, first_row, token_count):
    query_pos = jnp.arange(row_count, dtype=jnp.int32)[:, None]
    key_pos = jnp.arange(row_count + 2 * reach, dtype=jnp.int32)[None, :]
    global_key = first_row - reach + key_pos
    inside = (key_pos >= query_pos) & (key_pos <= query_pos + 2 * reach)
    inside = inside & (global_key >= 0) & (global_key < token_count)
    return inside.astype(jnp.float32)


def split_heads(queries, extended, head_count):
    member_dev, row_count, feature_count = queries.shape
    head_dim = feature_count // head_count
    query_h = queries.reshape(member_dev, row_count, head_count, head_dim)
    key_h = extended[..., :feature_count].reshape(member_dev, -1, head_count, head_dim)
    value_h = extended[..., feature_count:].reshape(member_dev, -1, head_count, head_dim)
    return (query_h, key_h, value_h, head_dim)


def attend(queries, extended, window, head_count):
    member_dev, row_count, feature_count = queries.shape
    query_h, key_h, value_h, head_dim = split_heads(queries, extended, head_count)
    scores = jnp.einsum(
        "mahd,mrhd->mhar", query_h, key_h, preferred_element_type=jnp.float32
    ) / math.sqrt(head_dim)
    expo = jnp.exp(scores) * window
    probs = expo / jnp.sum(expo, axis=-1, keepdims=True)
    probs_b = probs.astype(jnp.bfloat16)
    result = jnp.einsum("mhar,mrhd->mahd", probs_b, value_h, preferred_element_type=jnp.float32)
    return (
        result.astype(jnp.bfloat16).reshape(member_dev, row_count, feature_count),
        probs,
        probs_b,
    )


def attend_back(queries, extended, probs, probs_b, grad_att, head_count):
    member_dev, row_count, feature_count = queries.shape
    query_h, key_h, value_h, head_dim = split_heads(queries, extended, head_count)
    grad_h = grad_att.reshape(member_dev, row_count, head_count, head_dim)
    dprob = jnp.einsum("mahd,mrhd->mhar", grad_h, value_h, preferred_element_type=jnp.float32)
    inner = jnp.sum(probs * dprob, axis=-1, keepdims=True)
    dscore = (probs * (dprob - inner) / math.sqrt(head_dim)).astype(jnp.bfloat16)
    grad_q = jnp.einsum("mhar,mrhd->mahd", dscore, key_h, preferred_element_type=jnp.float32)
    grad_k = jnp.einsum("mhar,mahd->mrhd", dscore, query_h, preferred_element_type=jnp.float32)
    grad_v = jnp.einsum("mhar,mahd->mrhd", probs_b, grad_h, preferred_element_type=jnp.float32)
    grad_q = grad_q.reshape(member_dev, row_count, feature_count)
    grad_k = grad_k.reshape(member_dev, -1, feature_count)
    grad_v = grad_v.reshape(member_dev, -1, feature_count)
    return (grad_q, jnp.concatenate([grad_k, grad_v], axis=-1))


def derivative_by_sample(
    sample_prediction, measured_truth, surface_portion_coefficient, objective_multiplier
):
    sample_number = sample_prediction.shape[0]
    eps_fair = (1.0 - ALPHA) / sample_number
    diagonal_contribution = criterion_derivative(sample_prediction - measured_truth[None])
    sample_dispersion = jnp.sum(
        criterion_derivative(sample_prediction[:, None] - sample_prediction[None, :]), axis=1
    )
    objective_derivative = (
        objective_multiplier
        * surface_portion_coefficient[None, :, None]
        * (
            diagonal_contribution / sample_number
            - (1.0 - eps_fair) / (sample_number * (sample_number - 1)) * sample_dispersion
        )
    )
    return objective_derivative.astype(jnp.bfloat16)


def edge_operator(token_local, edge_weight, row_count):
    places = jnp.arange(row_count, dtype=jnp.int32)[None, :]
    matrix = jnp.zeros((token_local.shape[0], row_count), jnp.float32)
    for slot in range(token_local.shape[1]):
        matrix = matrix + jnp.where(
            token_local[:, slot][:, None] == places, edge_weight[:, slot][:, None], 0.0
        )
    high = matrix.astype(jnp.bfloat16)
    low = (matrix - high.astype(jnp.float32)).astype(jnp.bfloat16)
    return jnp.concatenate([high, low], axis=1)


def doubled(values):
    rounded = values.astype(jnp.bfloat16)
    return jnp.concatenate([rounded, rounded], axis=1)


def on_device(
    tokens,
    w_qkv,
    w_out,
    w_hidden,
    decoder_readout_matrix,
    edge_token,
    edge_weight,
    truth_state,
    area,
):
    member_dev, row_count, feature_count = tokens.shape
    reach = row_count // 2
    space_count = lax.axis_size("space")
    first_row = lax.axis_index("space") * row_count
    token_count = row_count * space_count
    normal_hat, inverse = norm_stats(tokens)
    normed = normal_hat.astype(jnp.bfloat16)
    flat_normed = normed.reshape(-1, feature_count)
    qkv = jnp.dot(flat_normed, w_qkv, preferred_element_type=jnp.float32).astype(jnp.bfloat16)
    qkv = qkv.reshape(member_dev, row_count, 3 * feature_count)
    queries = qkv[..., :feature_count]
    extended = extended_2(qkv[..., feature_count:], (("space", 1),), reach)
    window = window_mask(row_count, reach, first_row, token_count)
    attended, probs, probs_b = attend(queries, extended, window, HEADS)
    flat_att = attended.reshape(-1, feature_count)
    states = tokens.astype(jnp.float32) + jnp.dot(
        flat_att, w_out, preferred_element_type=jnp.float32
    ).reshape(tokens.shape)
    states = states.astype(jnp.bfloat16)
    location_number = edge_token.shape[0]
    edges = edge_operator(edge_token - first_row, edge_weight, row_count)
    hidden = jnp.dot(
        states.reshape(-1, feature_count), w_hidden, preferred_element_type=jnp.float32
    ).reshape(tokens.shape)
    pre = jnp.einsum(
        "ct,mtk->mck", edges, doubled(hidden), preferred_element_type=jnp.float32
    ).reshape(-1, feature_count)
    hidden_state_entries = jax.nn.gelu(pre, approximate=False).astype(jnp.bfloat16)
    sample_prediction = jnp.dot(
        hidden_state_entries, decoder_readout_matrix, preferred_element_type=jnp.float32
    ).reshape(member_dev, location_number, -1)
    every_member_output = lax.all_to_all(
        sample_prediction.astype(jnp.bfloat16), "member", split_axis=1, concat_axis=0, tiled=True
    ).astype(sample_prediction.dtype)
    cell_piece = every_member_output.shape[1]
    cell_first = lax.axis_index("member") * cell_piece
    measured_truth = lax.dynamic_slice_in_dim(truth_state, cell_first, cell_piece, 0)
    surface_portion_coefficient = lax.dynamic_slice_in_dim(area, cell_first, cell_piece, 0)
    objective_multiplier = math.sqrt(every_member_output.shape[0] / (location_number * space_count))
    grad_members = derivative_by_sample(
        every_member_output, measured_truth, surface_portion_coefficient, objective_multiplier
    )
    prediction_derivative = lax.all_to_all(
        grad_members, "member", split_axis=0, concat_axis=1, tiled=True
    ).reshape(-1, sample_prediction.shape[2])
    decoder_readout_derivative = jnp.einsum(
        "du,de->ue", hidden_state_entries, prediction_derivative, preferred_element_type=jnp.float32
    )
    hidden_state_derivative = jnp.einsum(
        "hv,bv->hb",
        prediction_derivative,
        decoder_readout_matrix,
        preferred_element_type=jnp.float32,
    )
    unused, gelu_back = jax.vjp(lambda inner_pre: jax.nn.gelu(inner_pre, approximate=False), pre)
    grad_pre = gelu_back(hidden_state_derivative)[0].astype(jnp.bfloat16)
    gathered = jnp.einsum(
        "ct,mck->mtk",
        edges,
        grad_pre.reshape(member_dev, location_number, feature_count),
        preferred_element_type=jnp.float32,
    )
    gathered = (gathered[:, :row_count] + gathered[:, row_count:]).reshape(-1, feature_count)
    gathered_hi = gathered.astype(jnp.bfloat16)
    gathered_lo = (gathered - gathered_hi.astype(jnp.float32)).astype(jnp.bfloat16)
    grad_hidden_w = jnp.einsum(
        "rk,rj->kj", states.reshape(-1, feature_count), gathered_hi, preferred_element_type=jnp.float32
    )
    grad_states = jnp.einsum(
        "rj,kj->rk", gathered_hi, w_hidden, preferred_element_type=jnp.float32
    ) + jnp.einsum("rj,kj->rk", gathered_lo, w_hidden, preferred_element_type=jnp.float32)
    grad_states = grad_states.reshape(tokens.shape)
    flat_gs = grad_states.astype(jnp.bfloat16).reshape(-1, feature_count)
    grad_out_w = jnp.einsum("rk,rj->kj", flat_att, flat_gs, preferred_element_type=jnp.float32)
    grad_att = jnp.einsum("rj,kj->rk", flat_gs, w_out, preferred_element_type=jnp.float32)
    grad_att = grad_att.astype(jnp.bfloat16).reshape(tokens.shape)
    grad_q, grad_kv_ext = attend_back(queries, extended, probs, probs_b, grad_att, HEADS)
    lower_part = grad_kv_ext[:, :reach]
    upper_part = grad_kv_ext[:, reach + row_count :]
    from_above = passed_along(lower_part.astype(jnp.bfloat16), "space", -1).astype(lower_part.dtype)
    from_below = passed_along(upper_part.astype(jnp.bfloat16), "space", 1).astype(upper_part.dtype)
    grad_kv = grad_kv_ext[:, reach : reach + row_count]
    grad_kv = grad_kv.at[:, row_count - reach :].add(from_above)
    grad_kv = grad_kv.at[:, :reach].add(from_below)
    grad_qkv = (
        jnp.concatenate([grad_q, grad_kv], axis=-1)
        .astype(jnp.bfloat16)
        .reshape(-1, 3 * feature_count)
    )
    grad_qkv_w = jnp.einsum("rk,rj->kj", flat_normed, grad_qkv, preferred_element_type=jnp.float32)
    grad_normed = jnp.einsum(
        "rj,kj->rk", grad_qkv, w_qkv, preferred_element_type=jnp.float32
    ).reshape(tokens.shape)
    grad_tokens = (grad_states + norm_back(grad_normed, normal_hat, inverse)).astype(jnp.bfloat16)
    rows = feature_count

    def halves(g):
        return g.astype(jnp.bfloat16).reshape(rows, 2, -1)

    readout = jnp.stack([decoder_readout_derivative, jnp.zeros_like(decoder_readout_derivative)], axis=1)
    pieces = (grad_qkv_w, grad_out_w, grad_hidden_w, readout.reshape(rows, -1))
    whole = jnp.concatenate([halves(g) for g in pieces], axis=-1)
    whole = jnp.transpose(whole.reshape(rows, 2, 3, -1), (1, 2, 0, 3))
    total = jnp.transpose(weight_sum(whole), (2, 0, 1, 3)).reshape(8, 2, -1)
    reduced, at = [], 0
    for g in pieces:
        width = g.shape[1] // 2
        reduced.append(total[:, :, at : at + width].reshape(8, -1))
        at += width
    reduced[3] = reduced[3][:, : decoder_readout_derivative.shape[1]]
    return (grad_tokens, reduced[0], reduced[1], reduced[2], reduced[3])


def solution(mesh):
    in_specs = (
        P("member", "space", None),
        P(),
        P(),
        P(),
        P(),
        P("space", None),
        P("space", None),
        P("space", None),
        P("space"),
    )
    out_specs = (
        P("member", "space", None),
        P(("member", "space"), None),
        P(("member", "space"), None),
        P(("member", "space"), None),
        P(("member", "space"), None),
    )
    return jax.shard_map(
        on_device, mesh=mesh, in_specs=in_specs, out_specs=out_specs, check_vma=False
    )
```

```python
import functools
import math

import jax
import jax.numpy as jnp
from jax import lax
from jax.experimental import pallas as pl
from jax.experimental.pallas import tpu as pltpu
from jax.sharding import PartitionSpec as P

HEADS = 16


EPS = 1e-05
ALPHA = 0.95
DELTA = 0.1


MESH = pl.DeviceIdType.MESH


class Place:
    def __init__(self):
        member, space = lax.axis_index("member"), lax.axis_index("space")
        self.member, self.space = member, space
        self.y, z_lo = member // 2, member % 2
        z_hi = space // 8
        self.x, self.core = (space // 2) % 4, space % 2
        self.z = z_hi * 2 + z_lo
        self.partner = (member, space + 1 - 2 * self.core)

    def ring(self, axis):
        return {"x": self.x, "y": self.y, "z": self.z}[axis]

    def device(self, axis, j):
        if axis == "x":
            return (self.member, (self.space // 8) * 8 + j * 2 + self.core)
        if axis == "y":
            return (j * 2 + self.member % 2, self.space)
        return ((self.member // 2) * 2 + j % 2, (j // 2) * 8 + self.space % 8)

    def neighbours(self):
        found = []
        for axis in "xyz":
            i = self.ring(axis)
            found += [self.device(axis, (i + 1) % 4), self.device(axis, (i + 3) % 4)]
        return found


def entry_barrier(devices):
    barrier = pltpu.get_barrier_semaphore()
    for device in devices:
        pl.semaphore_signal(barrier, inc=1, device_id=device, device_id_type=MESH)
    pl.semaphore_wait(barrier, len(devices))


ORDERS = (
    (
        ("x", (4, 2, 2), lambda j, r: (*r, j)),
        ("y", (2, 2), lambda j, r: (j, *r)),
        ("z", (), lambda j, r: (j % 2, j // 2)),
    ),
    (
        ("y", (2, 2, 4), lambda j, r: (j, *r)),
        ("z", (4,), lambda j, r: (j % 2, j // 2, *r)),
        ("x", (), lambda j, r: (j,)),
    ),
    (
        ("z", (4, 4), lambda j, r: (r[0], j % 2, j // 2, r[1])),
        ("x", (4,), lambda j, r: (r[0], j)),
        ("y", (), lambda j, r: (j,)),
    ),
)
FULL = (4, 2, 2, 4)


def first_columns(width):
    return width // 128 // 2 * 128


def sum_scratch(width):
    low = first_columns(width)
    shapes = []
    for order in ORDERS:
        for phase, (_, rest, _) in enumerate(order):
            for columns in (width, width, low, width - low):
                shapes.append(pltpu.VMEM((*rest, 16, columns), jnp.bfloat16))
            if phase < 2:
                shapes.append(pltpu.VMEM((*rest, 16, width), jnp.bfloat16))
    return shapes + [pltpu.SemaphoreType.DMA((54,)), pltpu.SemaphoreType.DMA((54,))]


def over(dims, body):
    if len(dims) <= 1:
        body((slice(None),) * len(dims))
        return
    count = math.prod(dims[:-1])

    def step(n, carry):
        index = []
        for size in reversed(dims[:-1]):
            index.insert(0, lax.rem(n, size))
            n = n // size
        body((*index, slice(None)))
        return carry

    lax.fori_loop(0, count, step, 0)


class RingSum:
    def __init__(self, place, width, parts, scratch, finish):
        self.place, self.width, self.low = place, width, first_columns(width)
        scratch = list(scratch)
        self.recv, self.send = scratch.pop(), scratch.pop()
        self.slots = []
        for _ in range(3):
            self.slots.append([])
            for phase in range(3):
                count = 5 if phase < 2 else 4
                self.slots[-1].append(scratch[:count])
                scratch = scratch[count:]
        self.data = [[part] for part in parts]
        for part in range(3):
            self.data[part] += [self.slots[part][phase][4] for phase in range(2)]
        self.finish = finish
        self.copies = {}

    def copy(self, part, phase, message, source, target, device):
        sem = (part * 3 + phase) * 6 + message
        made = pltpu.make_async_remote_copy(
            src_ref=source, dst_ref=target, send_sem=self.send.at[sem], recv_sem=self.recv.at[sem],
            device_id=device, device_id_type=MESH,
        )
        made.start()
        self.copies[part, phase, message] = made

    def view(self, part, phase, j, low):
        _, rest, at = ORDERS[part][phase]
        columns = pl.ds(0, self.low) if low else pl.ds(self.low, self.width - self.low)
        return self.data[part][phase].at[(*at(j, (slice(None),) * len(rest)), slice(None), columns)]

    def around(self, part, phase):
        axis = ORDERS[part][phase][0]
        i = self.place.ring(axis)
        right, left = (i + 1) % 4, (i + 3) % 4
        return i, right, left, (i + 2) % 4, self.place.device(axis, right), self.place.device(axis, left)

    def open(self, part, phase):
        _, right, left, opposite, to_right, to_left = self.around(part, phase)
        from_left, from_right, relay_left, relay_right = self.slots[part][phase][:4]
        low, high = pl.ds(0, self.low), pl.ds(self.low, self.width - self.low)
        self.copy(part, phase, 0, self.view(part, phase, opposite, True), relay_left, to_right)
        self.copy(part, phase, 1, self.view(part, phase, opposite, False), relay_right, to_left)
        self.copy(part, phase, 2, self.view(part, phase, right, False), from_left.at[..., high], to_right)
        self.copy(part, phase, 3, self.view(part, phase, left, True), from_right.at[..., low], to_left)

    def relay(self, part, phase):
        _, right, left, _, to_right, to_left = self.around(part, phase)
        _, rest, at = ORDERS[part][phase]
        from_left, from_right, relay_left, relay_right = self.slots[part][phase][:4]
        low, high = pl.ds(0, self.low), pl.ds(self.low, self.width - self.low)
        data = self.data[part][phase]
        for message, j, columns, relayed in ((0, right, low, relay_left), (1, left, high, relay_right)):
            self.copies[part, phase, message].wait_recv()

            def add(r, j=j, columns=columns, relayed=relayed):
                here = (*at(j, r), slice(None), columns)
                there = (*r, slice(None), slice(None))
                both = data[here].astype(jnp.float32) + relayed[there].astype(jnp.float32)
                data[here] = both.astype(jnp.bfloat16)

            over(rest, add)
            if message == 0:
                self.copy(part, phase, 4, self.view(part, phase, right, True), from_left.at[..., low], to_right)
            else:
                self.copy(part, phase, 5, self.view(part, phase, left, False), from_right.at[..., high], to_left)

    def close(self, part, phase):
        i = self.around(part, phase)[0]
        _, rest, at = ORDERS[part][phase]
        from_left, from_right = self.slots[part][phase][:2]
        data = self.data[part][phase]
        for message in (2, 3, 4, 5):
            self.copies[part, phase, message].wait_recv()

        def add(r):
            there = (*r, slice(None), slice(None))
            total = data[(*at(i, r), slice(None), slice(None))].astype(jnp.float32)
            total = total + from_left[there].astype(jnp.float32) + from_right[there].astype(jnp.float32)
            if phase < 2:
                self.data[part][phase + 1][there] = total.astype(jnp.bfloat16)
            else:
                self.finish(part, total)

        over(rest, add)

    def steps(self):
        for phase in range(3):
            for part in range(3):
                self.relay(part, phase)
                yield
            for part in range(3):
                self.close(part, phase)
                if phase < 2:
                    self.open(part, phase + 1)
                yield

    def drain(self):
        for made in self.copies.values():
            made.wait_send()


NT = (((1,), (1,)), ((), ()))
TN = (((0,), (0,)), ((), ()))


def dot_nn(a, b):
    return jnp.dot(a, b, preferred_element_type=jnp.float32)


def dot_nt(a, b):
    return lax.dot_general(a, b, NT, preferred_element_type=jnp.float32)


def dot_tn(a, b):
    return lax.dot_general(a, b, TN, preferred_element_type=jnp.float32)


def gelu_both(x):
    bell = jnp.exp(-0.5 * (x * x))
    t = 1.0 / (1.0 + (0.3275911 / math.sqrt(2.0)) * jnp.abs(x))
    poly = t * (
        0.5 * 0.254829592
        + t * (-0.5 * 0.284496736 + t * (0.5 * 1.421413741 + t * (-0.5 * 1.453152027 + t * (0.5 * 1.061405429))))
    )
    tail = poly * bell
    share = jnp.where(x >= 0.0, 1.0 - tail, tail)
    return x * share, share + x * (bell * (1.0 / math.sqrt(2.0 * math.pi)))


def decoder_kernel(
    hid_ref, edges_ref, edges_t_ref, readout_ref, truth_ref, area_ref, gathered_ref, readout_grad_ref,
    active, slope, sent, held, sent_back, held_back, turned, send, recv, send_back, recv_back,
):
    member, space = lax.axis_index("member"), lax.axis_index("space")
    others = [lax.rem(member + k, 8) for k in range(1, 8)]
    entry_barrier([(other, space) for other in others])
    home = member // 2

    def give(source, target, send_sem, recv_sem, to):
        return pltpu.make_async_remote_copy(
            src_ref=source.at[to], dst_ref=target.at[member], send_sem=send_sem.at[to],
            recv_sem=recv_sem.at[member], device_id=(to, space), device_id_type=MESH,
        )

    def take(target, send_sem, recv_sem, source):
        return pltpu.make_async_remote_copy(
            src_ref=target.at[source], dst_ref=target.at[source], send_sem=send_sem.at[source],
            recv_sem=recv_sem.at[source], device_id=(source, space), device_id_type=MESH,
        )

    for n in range(4):
        group = lax.rem(home + 1 + n, 4)
        edges = edges_ref[group]

        def forward(b, carry, group=group, edges=edges):
            hid = hid_ref[b]
            twice = jnp.concatenate([hid, hid], axis=0)
            forecast = jnp.zeros((256, 128), jnp.float32)
            for part in range(4):
                columns = slice(part * 256, part * 256 + 256)
                value, derivative = gelu_both(dot_nn(edges, twice[:, columns]))
                value = value.astype(jnp.bfloat16)
                active[b, group, :, columns] = value
                slope[b, group, :, columns] = derivative
                forecast = forecast + dot_nn(value, readout_ref[columns, :])
            sent[2 * group, b] = forecast[:128].astype(jnp.bfloat16)
            sent[2 * group + 1, b] = forecast[128:].astype(jnp.bfloat16)
            return carry

        lax.fori_loop(0, 2, forward, 0)
        if n < 3:
            give(sent, held, send, recv, 2 * group).start()
            give(sent, held, send, recv, 2 * group + 1).start()
        else:
            give(sent, held, send, recv, 2 * group + 1 - lax.rem(member, 2)).start()
            held[member] = sent[member]
    for other in others:
        take(held, send, recv, other).wait_recv()

    multiplier = math.sqrt(16 / 16384)
    eps_fair = (1.0 - ALPHA) / 16

    def score(block, carry):
        rows = pl.ds(pl.multiple_of(block * 16, 16), 16)
        whole = [held[m // 2, m % 2, rows, :].astype(jnp.float32) for m in range(16)]
        truth, area = truth_ref[rows, :], area_ref[rows, :]
        found = [[] for _ in range(16)]
        for half in (slice(0, 8), slice(8, 16)):
            values = [value[half] for value in whole]
            spread = [None] * 16
            for j in range(16):
                for k in range(j + 1, 16):
                    d = values[j] - values[k]
                    s = d * lax.rsqrt(d * d + DELTA * DELTA)
                    spread[j] = s if spread[j] is None else spread[j] + s
                    spread[k] = -s if spread[k] is None else spread[k] - s
            for j in range(16):
                d = values[j] - truth[half]
                s = d * lax.rsqrt(d * d + DELTA * DELTA)
                found[j].append(
                    multiplier * area[half] * (s / 16 - (1.0 - eps_fair) / (16 * 15) * spread[j])
                )
        for j in range(16):
            sent_back[j // 2, j % 2, rows, :] = jnp.concatenate(found[j], axis=0).astype(jnp.bfloat16)
        return carry

    lax.fori_loop(0, 8, score, 0)
    for other in others:
        give(sent_back, held_back, send_back, recv_back, other).start()
    held_back[member] = sent_back[member]

    gathered_ref[...] = jnp.zeros_like(gathered_ref)
    turned[...] = jnp.zeros_like(turned)
    for n in range(4):
        group = lax.rem(home + n, 4)
        if n == 0:
            take(held_back, send_back, recv_back, 2 * group + 1 - lax.rem(member, 2)).wait_recv()
        else:
            take(held_back, send_back, recv_back, 2 * group).wait_recv()
            take(held_back, send_back, recv_back, 2 * group + 1).wait_recv()
        edges_t = edges_t_ref[group]

        def backward(b, carry, group=group, edges_t=edges_t):
            grad = jnp.concatenate([held_back[2 * group, b], held_back[2 * group + 1, b]], axis=0)
            for part in range(4):
                columns = slice(part * 256, part * 256 + 256)
                hidden = dot_nt(grad, readout_ref[columns, :])
                grad_pre = (hidden * slope[b, group, :, columns]).astype(jnp.bfloat16)
                both = dot_nn(edges_t, grad_pre)
                gathered_ref[b, :, columns] += both[:128] + both[128:]
                turned[:, columns] += dot_tn(grad, active[b, group, :, columns])
            return carry

        lax.fori_loop(0, 2, backward, 0)
    readout_grad_ref[...] = turned[...].T.astype(jnp.bfloat16)
    for other in others:
        give(sent, held, send, recv, other).wait_send()
        give(sent_back, held_back, send_back, recv_back, other).wait_send()


def decoder(hidden, edges, readout, truth, area):
    dma = pltpu.SemaphoreType.DMA((8,))
    cells = pltpu.VMEM((8, 2, 128, 128), jnp.bfloat16)
    vmem = pl.BlockSpec(memory_space=pltpu.VMEM)
    return pl.pallas_call(
        decoder_kernel,
        out_shape=(
            jax.ShapeDtypeStruct((2, 128, 1024), jnp.float32),
            jax.ShapeDtypeStruct((1024, 128), jnp.bfloat16),
        ),
        in_specs=[vmem] * 6,
        out_specs=[vmem, vmem],
        scratch_shapes=[
            pltpu.VMEM((2, 4, 256, 1024), jnp.bfloat16), pltpu.VMEM((2, 4, 256, 1024), jnp.float32),
            cells, cells, cells, cells, pltpu.VMEM((128, 1024), jnp.float32), dma, dma, dma, dma,
        ],
        compiler_params=pltpu.CompilerParams(
            collective_id=1, has_side_effects=True, vmem_limit_bytes=56 * 2**20
        ),
    )(
        hidden,
        edges.reshape(4, 256, 256),
        jnp.transpose(edges.reshape(4, 256, 256), (0, 2, 1)),
        readout,
        truth,
        area.reshape(-1, 1),
    )


def backward_kernel(
    states_ref, gathered_ref, readout_grad_ref, att_ref, q_ref, kv_ref, normed_ref, tokens_ref,
    w_hidden_hbm, w_out_hbm, w_qkv_hbm, grad_tokens_ref, early_ref, late_ref, *scratch
):
    (
        w_hidden, w_out, w_qkv, states_2, att_2, normed_2, gather_b, gather_2, grad_s, grad_sb, grad_s2,
        grad_att, readout_2, window, grad_qkv, grad_qkv2, middle, lower, upper, from_above, from_below,
        early_data, late_data, early_final, late_final, load_sems, pair_sems, halo_sems, final_sems,
        *ring_scratch,
    ) = scratch
    early_scratch, late_scratch = ring_scratch[: len(ring_scratch) // 2], ring_scratch[len(ring_scratch) // 2 :]
    place = Place()
    member, space, core = place.member, place.space, place.core
    loads = []
    for i, (source, target) in enumerate(((w_hidden_hbm, w_hidden), (w_out_hbm, w_out), (w_qkv_hbm, w_qkv))):
        load = pltpu.make_async_copy(source, target, load_sems.at[i])
        load.start()
        loads.append(load)
    above, below = (member, lax.rem(space + 1, 16)), (member, lax.rem(space + 15, 16))
    entry_barrier([place.partner, above, below, *place.neighbours()])
    pairs = []

    def pair(source, target):
        i = len(pairs)
        made = pltpu.make_async_remote_copy(
            src_ref=source, dst_ref=target, send_sem=pair_sems.at[0, i], recv_sem=pair_sems.at[1, i],
            device_id=place.partner, device_id_type=MESH,
        )
        made.start()
        pairs.append(made)
        return made

    mine = pl.ds(pl.multiple_of(core * 512, 512), 512)
    other = pl.ds(pl.multiple_of((1 - core) * 512, 512), 512)
    states_here = pair(states_ref, states_2)
    high = gathered_ref[...].astype(jnp.bfloat16)
    gather_b[...] = high
    gather_here = pair(gather_b.at[:, other], gather_2)
    readout_here = pair(readout_grad_ref, readout_2)
    att_here = pair(att_ref, att_2)
    normed_here = pair(normed_ref, normed_2)

    row = lax.broadcasted_iota(jnp.int32, (256, 256), 0) % 128
    key = lax.broadcasted_iota(jnp.int32, (256, 256), 1)
    token = space * 128 - 64 + key
    inside = (key >= row) & (key <= row + 128) & (token >= 0) & (token < 2048)
    window[...] = jnp.where(inside, 1.0, 0.0)

    loads[0].wait()
    low = (gathered_ref[...] - high.astype(jnp.float32)).astype(jnp.bfloat16)
    for part in range(4):
        rows = slice(part * 256, part * 256 + 256)
        weights = w_hidden[rows, :]
        value = dot_nt(high, weights) + dot_nt(low, weights)
        grad_s[:, rows] = value
        grad_sb[:, rows] = value.astype(jnp.bfloat16)
    grad_s_here = pair(grad_sb.at[:, other], grad_s2)

    def early_tile(tile, y, value):
        columns = slice(tile % 3 * 128, tile % 3 * 128 + 128)
        early_data[tile // 3, y, :, :, :, :, columns] = value.astype(jnp.bfloat16).reshape(2, 2, 4, 16, 128)

    states_here.wait_recv()
    gather_here.wait_recv()
    for y in range(4):
        rows = slice(y * 256, y * 256 + 256)
        value = dot_tn(states_ref[:, rows], gather_b[:, mine]) + dot_tn(states_2[:, rows], gather_2[...])
        for tile in range(4):
            early_tile(tile, y, value[:, tile * 128 : tile * 128 + 128])
    readout_here.wait_recv()
    for y in range(4):
        rows = slice(y * 256, y * 256 + 256)
        early_tile(8, y, readout_grad_ref[rows, :].astype(jnp.float32) + readout_2[rows, :].astype(jnp.float32))
    att_here.wait_recv()
    grad_s_here.wait_recv()
    for y in range(4):
        rows = slice(y * 256, y * 256 + 256)
        value = dot_tn(att_ref[:, rows], grad_sb[:, mine]) + dot_tn(att_2[:, rows], grad_s2[...])
        for tile in range(4):
            early_tile(4 + tile, y, value[:, tile * 128 : tile * 128 + 128])

    def early_finish(part, total):
        early_final[part] = total.reshape(2, 8, 384)

    def late_finish(part, total):
        late_final[part] = total.reshape(2, 8, 512)

    early = RingSum(place, 384, [early_data.at[part] for part in range(3)], early_scratch, early_finish)
    late = RingSum(place, 512, [late_data.at[part] for part in range(3)], late_scratch, late_finish)
    for part in range(3):
        early.open(part, 0)
    early_steps = early.steps()

    loads[1].wait()
    for part in range(4):
        rows = slice(part * 256, part * 256 + 256)
        grad_att[:, rows] = dot_nt(grad_sb[...], w_out[rows, :]).astype(jnp.bfloat16)

    lane = lax.broadcasted_iota(jnp.int32, (128, 128), 1)
    first = lane < 64

    def stacked(value):
        zero = jnp.zeros_like(value)
        return jnp.concatenate([jnp.where(first, value, zero), jnp.where(first, zero, value)], axis=0)

    def attention(m, n, carry):
        start = pl.multiple_of(n * 128, 128)
        columns, values = pl.ds(start, 128), pl.ds(start + 1024, 128)
        token_rows = pl.ds(m * 128, 128)
        queries = stacked(q_ref[token_rows, columns])
        keys, vals = kv_ref[m, :, columns], kv_ref[m, :, values]
        grads = stacked(grad_att[token_rows, columns])
        expo = jnp.where(window[...] > 0.0, jnp.exp(dot_nt(queries, keys) * 0.125), 0.0)
        probs = expo / jnp.sum(expo, axis=-1, keepdims=True)
        probs_b = probs.astype(jnp.bfloat16)
        dprob = dot_nt(grads, vals)
        inner = jnp.sum(probs * dprob, axis=-1, keepdims=True)
        dscore = (probs * (dprob - inner) * 0.125).astype(jnp.bfloat16)
        grad_q = dot_nn(dscore, keys)
        grad_qkv[token_rows, columns] = jnp.where(first, grad_q[:128], grad_q[128:]).astype(jnp.bfloat16)
        for value, at in ((dot_tn(dscore, queries), columns), (dot_tn(probs_b, grads), values)):
            lower[m, :, at] = value[:64].astype(jnp.bfloat16)
            middle[token_rows, at] = value[64:192]
            upper[m, :, at] = value[192:].astype(jnp.bfloat16)
        return carry

    halos = []
    for m in range(2):
        for half in range(2):
            lax.fori_loop(half * 4, half * 4 + 4, functools.partial(attention, m), 0)
            for _ in range(4):
                next(early_steps, None)
        for side, (source, target, device) in enumerate(((lower, from_above, below), (upper, from_below, above))):
            made = pltpu.make_async_remote_copy(
                src_ref=source.at[m], dst_ref=target.at[m], send_sem=halo_sems.at[0, side, m],
                recv_sem=halo_sems.at[1, side, m], device_id=device, device_id_type=MESH,
            )
            made.start()
            halos.append(made)

    def swap(part):
        return pair(
            grad_qkv.at[:, pl.ds(pl.multiple_of(part * 1024 + (1 - core) * 512, 512), 512)], grad_qkv2.at[part]
        )

    def late_product(part):
        own = grad_qkv[:, pl.ds(pl.multiple_of(part * 1024 + core * 512, 512), 512)]
        for y in range(4):
            rows = slice(y * 256, y * 256 + 256)
            value = dot_tn(normed_ref[:, rows], own) + dot_tn(normed_2[:, rows], grad_qkv2[part])
            late_data[part, y] = value.astype(jnp.bfloat16).reshape(2, 2, 4, 16, 512)
        late.open(part, 0)

    swaps = [swap(0)]
    for _ in early_steps:
        pass
    for made in halos:
        made.wait_recv()
    for m in range(2):
        begin = m * 128
        for columns in (slice(0, 1024), slice(1024, 2048)):
            into = slice(columns.start + 1024, columns.stop + 1024)
            grad_qkv[begin : begin + 64, into] = (
                middle[begin : begin + 64, columns] + from_below[m, :, columns].astype(jnp.float32)
            ).astype(jnp.bfloat16)
            grad_qkv[begin + 64 : begin + 128, into] = (
                middle[begin + 64 : begin + 128, columns] + from_above[m, :, columns].astype(jnp.float32)
            ).astype(jnp.bfloat16)
    swaps += [swap(1), swap(2)]
    normed_here.wait_recv()
    for part in range(3):
        swaps[part].wait_recv()
        late_product(part)
    late_steps = late.steps()
    loads[2].wait()
    for part in range(4):
        rows = slice(part * 256, part * 256 + 256)
        middle[:, rows] = dot_nt(grad_qkv[...], w_qkv[rows, :])
        next(late_steps, None)
        next(late_steps, None)
    wide = tokens_ref[...].astype(jnp.float32)
    centre = wide - jnp.mean(wide, axis=-1, keepdims=True)
    inverse = lax.rsqrt(jnp.mean(centre * centre, axis=-1, keepdims=True) + EPS)
    back = norm_back(middle[:, :1024], centre * inverse, inverse)
    grad_tokens_ref[...] = (grad_s[...] + back).astype(jnp.bfloat16)
    for _ in late_steps:
        pass

    lasts = []
    for i, (final, out) in enumerate(((early_final, early_ref), (late_final, late_ref))):
        last = pltpu.make_async_remote_copy(
            src_ref=final.at[:, 1 - core], dst_ref=out.at[core], send_sem=final_sems.at[0, i],
            recv_sem=final_sems.at[1, i], device_id=place.partner, device_id_type=MESH,
        )
        last.start()
        lasts.append(last)
        out[core] = final[:, core]
    for last in lasts:
        last.wait()
    for made in pairs + halos:
        made.wait_send()
    early.drain()
    late.drain()


def backward(states, gathered, readout_grad, attended, queries, extended, normed, tokens, weights):
    vmem, anywhere = pl.BlockSpec(memory_space=pltpu.VMEM), pl.BlockSpec(memory_space=pl.ANY)

    def b16(*shape):
        return pltpu.VMEM(shape, jnp.bfloat16)

    def f32(*shape):
        return pltpu.VMEM(shape, jnp.float32)

    return pl.pallas_call(
        backward_kernel,
        out_shape=(
            jax.ShapeDtypeStruct((256, 1024), jnp.bfloat16),
            jax.ShapeDtypeStruct((2, 3, 8, 384), jnp.float32),
            jax.ShapeDtypeStruct((2, 3, 8, 512), jnp.float32),
        ),
        in_specs=[vmem] * 8 + [anywhere] * 3,
        out_specs=[vmem] * 3,
        scratch_shapes=[
            b16(1024, 1024), b16(1024, 1024), b16(1024, 3072), b16(256, 1024), b16(256, 1024), b16(256, 1024),
            b16(256, 1024), b16(256, 512), f32(256, 1024), b16(256, 1024), b16(256, 512),
            b16(256, 1024), b16(1024, 128), f32(256, 256), b16(256, 3072), b16(3, 256, 512), f32(256, 2048),
            b16(2, 64, 2048), b16(2, 64, 2048), b16(2, 64, 2048), b16(2, 64, 2048),
            b16(3, *FULL, 16, 384), b16(3, *FULL, 16, 512), f32(3, 2, 8, 384), f32(3, 2, 8, 512),
            pltpu.SemaphoreType.DMA((3,)), pltpu.SemaphoreType.DMA((2, 9)),
            pltpu.SemaphoreType.DMA((2, 2, 2)), pltpu.SemaphoreType.DMA((2, 2)),
            *sum_scratch(384), *sum_scratch(512),
        ],
        compiler_params=pltpu.CompilerParams(
            collective_id=0, has_side_effects=True, vmem_limit_bytes=58 * 2**20
        ),
    )(states, gathered, readout_grad, attended, queries, extended, normed, tokens, *weights)


def extended_2(array, sides, width):
    for axis, dim in sides:
        count, length = (lax.axis_size(axis), array.shape[dim])
        up = [(i, (i + 1) % count) for i in range(count - 1)]
        down = [(j, i) for i, j in up]
        last = lax.slice_in_dim(array, length - width, length, axis=dim)
        initial = lax.slice_in_dim(array, 0, width, axis=dim)
        before = lax.ppermute(last, axis, up)
        after = lax.ppermute(initial, axis, down)
        array = jnp.concatenate([before, array, after], axis=dim)
    return array


def norm_stats(values):
    wide = values.astype(jnp.float32)
    centre = wide - jnp.mean(wide, axis=-1, keepdims=True)
    inverse = lax.rsqrt(jnp.mean(centre * centre, axis=-1, keepdims=True) + EPS)
    return (centre * inverse, inverse)


def norm_back(objective_derivative, normal_hat, inverse):
    first = jnp.mean(objective_derivative, axis=-1, keepdims=True)
    second = jnp.mean(objective_derivative * normal_hat, axis=-1, keepdims=True)
    return inverse * (objective_derivative - first - normal_hat * second)


def window_mask(row_count, reach, first_row, token_count):
    query_pos = jnp.arange(row_count, dtype=jnp.int32)[:, None]
    key_pos = jnp.arange(row_count + 2 * reach, dtype=jnp.int32)[None, :]
    global_key = first_row - reach + key_pos
    inside = (key_pos >= query_pos) & (key_pos <= query_pos + 2 * reach)
    inside = inside & (global_key >= 0) & (global_key < token_count)
    return inside.astype(jnp.float32)


def split_heads(queries, extended, head_count):
    member_dev, row_count, feature_count = queries.shape
    head_dim = feature_count // head_count
    query_h = queries.reshape(member_dev, row_count, head_count, head_dim)
    key_h = extended[..., :feature_count].reshape(member_dev, -1, head_count, head_dim)
    value_h = extended[..., feature_count:].reshape(member_dev, -1, head_count, head_dim)
    return (query_h, key_h, value_h, head_dim)


def attend(queries, extended, window, head_count):
    member_dev, row_count, feature_count = queries.shape
    query_h, key_h, value_h, head_dim = split_heads(queries, extended, head_count)
    scores = jnp.einsum(
        "mahd,mrhd->mhar", query_h, key_h, preferred_element_type=jnp.float32
    ) / math.sqrt(head_dim)
    expo = jnp.exp(scores) * window
    probs = expo / jnp.sum(expo, axis=-1, keepdims=True)
    probs_b = probs.astype(jnp.bfloat16)
    result = jnp.einsum("mhar,mrhd->mahd", probs_b, value_h, preferred_element_type=jnp.float32)
    return (
        result.astype(jnp.bfloat16).reshape(member_dev, row_count, feature_count),
        probs,
        probs_b,
    )


def edge_operator(token_local, edge_weight, row_count):
    places = jnp.arange(row_count, dtype=jnp.int32)[None, :]
    matrix = jnp.zeros((token_local.shape[0], row_count), jnp.float32)
    for slot in range(token_local.shape[1]):
        matrix = matrix + jnp.where(
            token_local[:, slot][:, None] == places, edge_weight[:, slot][:, None], 0.0
        )
    high = matrix.astype(jnp.bfloat16)
    low = (matrix - high.astype(jnp.float32)).astype(jnp.bfloat16)
    return jnp.concatenate([high, low], axis=1)


def on_device(
    tokens,
    w_qkv,
    w_out,
    w_hidden,
    decoder_readout_matrix,
    edge_token,
    edge_weight,
    truth_state,
    area,
):
    member_dev, row_count, feature_count = tokens.shape
    reach = row_count // 2
    space_count = lax.axis_size("space")
    first_row = lax.axis_index("space") * row_count
    token_count = row_count * space_count
    normal_hat, inverse = norm_stats(tokens)
    normed = normal_hat.astype(jnp.bfloat16)
    flat_normed = normed.reshape(-1, feature_count)
    qkv = jnp.dot(flat_normed, w_qkv, preferred_element_type=jnp.float32).astype(jnp.bfloat16)
    qkv = qkv.reshape(member_dev, row_count, 3 * feature_count)
    queries = qkv[..., :feature_count]
    extended = extended_2(qkv[..., feature_count:], (("space", 1),), reach)
    window = window_mask(row_count, reach, first_row, token_count)
    attended, probs, probs_b = attend(queries, extended, window, HEADS)
    flat_att = attended.reshape(-1, feature_count)
    states = tokens.astype(jnp.float32) + jnp.dot(
        flat_att, w_out, preferred_element_type=jnp.float32
    ).reshape(tokens.shape)
    states = states.astype(jnp.bfloat16)
    location_number = edge_token.shape[0]
    edges = edge_operator(edge_token - first_row, edge_weight, row_count)
    hidden = jnp.dot(
        states.reshape(-1, feature_count), w_hidden, preferred_element_type=jnp.float32
    ).reshape(tokens.shape)
    cell_piece = location_number // lax.axis_size("member")
    cell_first = lax.axis_index("member") * cell_piece
    gathered, readout_grad = decoder(
        hidden.astype(jnp.bfloat16),
        edges,
        decoder_readout_matrix,
        lax.dynamic_slice_in_dim(truth_state, cell_first, cell_piece, 0),
        lax.dynamic_slice_in_dim(area, cell_first, cell_piece, 0),
    )
    grad_tokens, early, late = backward(
        states.reshape(-1, feature_count),
        gathered.reshape(-1, feature_count),
        readout_grad,
        flat_att,
        queries.reshape(-1, feature_count),
        extended,
        flat_normed,
        tokens.reshape(-1, feature_count),
        (w_hidden, w_out, w_qkv),
    )
    early = jnp.transpose(early, (2, 0, 1, 3)).reshape(8, 2, -1)
    late = jnp.transpose(late, (2, 1, 0, 3)).reshape(8, -1)
    return (
        grad_tokens.reshape(tokens.shape),
        late,
        early[:, :, 512:1024].reshape(8, -1),
        early[:, :, :512].reshape(8, -1),
        early[:, 0, 1024:],
    )


def solution(mesh):
    in_specs = (
        P("member", "space", None),
        P(),
        P(),
        P(),
        P(),
        P("space", None),
        P("space", None),
        P("space", None),
        P("space"),
    )
    out_specs = (
        P("member", "space", None),
        P(("member", "space"), None),
        P(("member", "space"), None),
        P(("member", "space"), None),
        P(("member", "space"), None),
    )
    return jax.shard_map(
        on_device, mesh=mesh, in_specs=in_specs, out_specs=out_specs, check_vma=False
    )
```

```python
import functools
import math
import types

import jax
import jax.numpy as jnp
from jax import lax
from jax.experimental import pallas as pl
from jax.experimental.pallas import tpu as pltpu
from jax.sharding import PartitionSpec as P

EPS = 1e-05
ALPHA = 0.95
DELTA = 0.1


MESH = pl.DeviceIdType.MESH


class Place:
    def __init__(self):
        member, space = lax.axis_index("member"), lax.axis_index("space")
        self.member, self.space = member, space
        self.y, z_lo = member // 2, member % 2
        z_hi = space // 8
        self.x, self.core = (space // 2) % 4, space % 2
        self.z = z_hi * 2 + z_lo
        self.partner = (member, space + 1 - 2 * self.core)

    def ring(self, axis):
        return {"x": self.x, "y": self.y, "z": self.z}[axis]

    def device(self, axis, j):
        if axis == "x":
            return (self.member, (self.space // 8) * 8 + j * 2 + self.core)
        if axis == "y":
            return (j * 2 + self.member % 2, self.space)
        return ((self.member // 2) * 2 + j % 2, (j // 2) * 8 + self.space % 8)

    def neighbours(self):
        found = []
        for axis in "xyz":
            i = self.ring(axis)
            found += [self.device(axis, (i + 1) % 4), self.device(axis, (i + 3) % 4)]
        return found


def entry_barrier(devices):
    barrier = pltpu.get_barrier_semaphore()
    for device in devices:
        pl.semaphore_signal(barrier, inc=1, device_id=device, device_id_type=MESH)
    pl.semaphore_wait(barrier, len(devices))


ORDERS = (
    (
        ("x", (4, 2, 2), lambda j, r: (*r, j)),
        ("y", (2, 2), lambda j, r: (j, *r)),
        ("z", (), lambda j, r: (j % 2, j // 2)),
    ),
    (
        ("y", (2, 2, 4), lambda j, r: (j, *r)),
        ("z", (4,), lambda j, r: (j % 2, j // 2, *r)),
        ("x", (), lambda j, r: (j,)),
    ),
    (
        ("z", (4, 4), lambda j, r: (r[0], j % 2, j // 2, r[1])),
        ("x", (4,), lambda j, r: (r[0], j)),
        ("y", (), lambda j, r: (j,)),
    ),
)
FULL = (4, 2, 2, 4)


def first_columns(width):
    return width // 128 // 2 * 128


def sum_scratch(width):
    low = first_columns(width)
    shapes = []
    for order in ORDERS:
        for phase, (_, rest, _) in enumerate(order):
            for columns in (width, width, low, width - low):
                shapes.append(pltpu.VMEM((*rest, 16, columns), jnp.bfloat16))
            if phase < 2:
                shapes.append(pltpu.VMEM((*rest, 16, width), jnp.bfloat16))
    return shapes + [pltpu.SemaphoreType.DMA((54,)), pltpu.SemaphoreType.DMA((54,))]


def over(dims, body):
    if len(dims) <= 1:
        body((slice(None),) * len(dims))
        return
    count = math.prod(dims[:-1])

    def step(n, carry):
        index = []
        for size in reversed(dims[:-1]):
            index.insert(0, lax.rem(n, size))
            n = n // size
        body((*index, slice(None)))
        return carry

    lax.fori_loop(0, count, step, 0)


class RingSum:
    def __init__(self, place, width, parts, scratch, finish):
        self.place, self.width, self.low = place, width, first_columns(width)
        scratch = list(scratch)
        self.recv, self.send = scratch.pop(), scratch.pop()
        self.slots = []
        for _ in range(3):
            self.slots.append([])
            for phase in range(3):
                count = 5 if phase < 2 else 4
                self.slots[-1].append(scratch[:count])
                scratch = scratch[count:]
        self.data = [[part] for part in parts]
        for part in range(3):
            self.data[part] += [self.slots[part][phase][4] for phase in range(2)]
        self.finish = finish
        self.copies = {}

    def copy(self, part, phase, message, source, target, device):
        sem = (part * 3 + phase) * 6 + message
        made = pltpu.make_async_remote_copy(
            src_ref=source, dst_ref=target, send_sem=self.send.at[sem], recv_sem=self.recv.at[sem],
            device_id=device, device_id_type=MESH,
        )
        made.start()
        self.copies[part, phase, message] = made

    def view(self, part, phase, j, low):
        _, rest, at = ORDERS[part][phase]
        columns = pl.ds(0, self.low) if low else pl.ds(self.low, self.width - self.low)
        return self.data[part][phase].at[(*at(j, (slice(None),) * len(rest)), slice(None), columns)]

    def around(self, part, phase):
        axis = ORDERS[part][phase][0]
        i = self.place.ring(axis)
        right, left = (i + 1) % 4, (i + 3) % 4
        return i, right, left, (i + 2) % 4, self.place.device(axis, right), self.place.device(axis, left)

    def open(self, part, phase):
        _, right, left, opposite, to_right, to_left = self.around(part, phase)
        from_left, from_right, relay_left, relay_right = self.slots[part][phase][:4]
        low, high = pl.ds(0, self.low), pl.ds(self.low, self.width - self.low)
        self.copy(part, phase, 0, self.view(part, phase, opposite, True), relay_left, to_right)
        self.copy(part, phase, 1, self.view(part, phase, opposite, False), relay_right, to_left)
        self.copy(part, phase, 2, self.view(part, phase, right, False), from_left.at[..., high], to_right)
        self.copy(part, phase, 3, self.view(part, phase, left, True), from_right.at[..., low], to_left)

    def relay(self, part, phase):
        _, right, left, _, to_right, to_left = self.around(part, phase)
        _, rest, at = ORDERS[part][phase]
        from_left, from_right, relay_left, relay_right = self.slots[part][phase][:4]
        low, high = pl.ds(0, self.low), pl.ds(self.low, self.width - self.low)
        data = self.data[part][phase]
        for message, j, columns, relayed in ((0, right, low, relay_left), (1, left, high, relay_right)):
            self.copies[part, phase, message].wait_recv()

            def add(r, j=j, columns=columns, relayed=relayed):
                here = (*at(j, r), slice(None), columns)
                there = (*r, slice(None), slice(None))
                both = data[here].astype(jnp.float32) + relayed[there].astype(jnp.float32)
                data[here] = both.astype(jnp.bfloat16)

            over(rest, add)
            if message == 0:
                self.copy(part, phase, 4, self.view(part, phase, right, True), from_left.at[..., low], to_right)
            else:
                self.copy(part, phase, 5, self.view(part, phase, left, False), from_right.at[..., high], to_left)

    def close(self, part, phase):
        i = self.around(part, phase)[0]
        _, rest, at = ORDERS[part][phase]
        from_left, from_right = self.slots[part][phase][:2]
        data = self.data[part][phase]
        for message in (2, 3, 4, 5):
            self.copies[part, phase, message].wait_recv()

        def add(r):
            there = (*r, slice(None), slice(None))
            total = data[(*at(i, r), slice(None), slice(None))].astype(jnp.float32)
            total = total + from_left[there].astype(jnp.float32) + from_right[there].astype(jnp.float32)
            if phase < 2:
                self.data[part][phase + 1][there] = total.astype(jnp.bfloat16)
            else:
                self.finish(part, total)

        over(rest, add)

    def steps(self):
        for phase in range(3):
            for part in range(3):
                self.relay(part, phase)
                yield
            for part in range(3):
                self.close(part, phase)
                if phase < 2:
                    self.open(part, phase + 1)
                yield

    def drain(self):
        for made in self.copies.values():
            made.wait_send()


NT = (((1,), (1,)), ((), ()))
TN = (((0,), (0,)), ((), ()))


def dot_nn(a, b):
    return jnp.dot(a, b, preferred_element_type=jnp.float32)


def dot_nt(a, b):
    return lax.dot_general(a, b, NT, preferred_element_type=jnp.float32)


def dot_tn(a, b):
    return lax.dot_general(a, b, TN, preferred_element_type=jnp.float32)


def gelu_both(x):
    bell = jnp.exp(-0.5 * (x * x))
    t = 1.0 / (1.0 + (0.3275911 / math.sqrt(2.0)) * jnp.abs(x))
    poly = t * (
        0.5 * 0.254829592
        + t * (-0.5 * 0.284496736 + t * (0.5 * 1.421413741 + t * (-0.5 * 1.453152027 + t * (0.5 * 1.061405429))))
    )
    tail = poly * bell
    share = jnp.where(x >= 0.0, 1.0 - tail, tail)
    return x * share, share + x * (bell * (1.0 / math.sqrt(2.0 * math.pi)))


def norm_back(objective_derivative, normal_hat, inverse):
    first = jnp.mean(objective_derivative, axis=-1, keepdims=True)
    second = jnp.mean(objective_derivative * normal_hat, axis=-1, keepdims=True)
    return inverse * (objective_derivative - first - normal_hat * second)


def normalised(values):
    wide = values.astype(jnp.float32)
    centre = wide - jnp.mean(wide, axis=-1, keepdims=True)
    inverse = lax.rsqrt(jnp.mean(centre * centre, axis=-1, keepdims=True) + EPS)
    return centre * inverse, inverse


def in_columns(count=4):
    return [slice(part * 256, part * 256 + 256) for part in range(count)]


def kernel(names, *refs):
    r = types.SimpleNamespace(**dict(zip(names, refs)))
    ring_scratch = refs[len(names) :]
    place = Place()
    member, space, core = place.member, place.space, place.core

    loads = [
        pltpu.make_async_copy(
            r.w_qkv_hbm.at[:, pl.ds(part * 1024, 1024)], r.w_qkv.at[:, pl.ds(part * 1024, 1024)], r.load_sems.at[part]
        )
        for part in range(3)
    ]
    loads.append(pltpu.make_async_copy(r.w_out_hbm, r.w_out, r.load_sems.at[3]))
    loads.append(pltpu.make_async_copy(r.w_hidden_hbm, r.w_hidden, r.load_sems.at[4]))
    loads.append(pltpu.make_async_copy(
        r.truth_hbm.at[pl.ds(pl.multiple_of(member * 128, 128), 128), :], r.truth, r.load_sems.at[5]
    ))
    for load in loads:
        load.start()

    above, below = (member, lax.rem(space + 1, 16)), (member, lax.rem(space + 15, 16))
    others = [lax.rem(member + k, 8) for k in range(1, 8)]
    entry_barrier([above, below, place.partner, *place.neighbours(), *[(other, space) for other in others]])
    sent_copies = []

    def push(source, target, sems, i, device):
        made = pltpu.make_async_remote_copy(
            src_ref=source, dst_ref=target, send_sem=sems.at[(0, *i)], recv_sem=sems.at[(1, *i)],
            device_id=device, device_id_type=MESH,
        )
        made.start()
        sent_copies.append(made)
        return made

    halo_tokens = []
    for m in range(2):
        halo_tokens.append(push(
            r.tokens.at[pl.ds(m * 128 + 64, 64)], r.halo.at[m, pl.ds(0, 64)], r.token_sems, (0, m), above
        ))
        halo_tokens.append(push(
            r.tokens.at[pl.ds(m * 128, 64)], r.halo.at[m, pl.ds(64, 64)], r.token_sems, (1, m), below
        ))

    pair_count = [0]

    def pair(source, target):
        pair_count[0] += 1
        return push(source, target, r.pair_sems, (pair_count[0] - 1,), place.partner)

    for block in range(4):
        rows = slice(block * 64, block * 64 + 64)
        r.normed[rows, :] = normalised(r.tokens[rows, :])[0].astype(jnp.bfloat16)
    normed_here = pair(r.normed, r.normed_2)
    loads[0].wait()
    for columns in in_columns():
        r.queries[:, columns] = dot_nn(r.normed[...], r.w_qkv[:, columns]).astype(jnp.bfloat16)

    row = lax.broadcasted_iota(jnp.int32, (256, 256), 0) % 128
    key = lax.broadcasted_iota(jnp.int32, (256, 256), 1)
    token = space * 128 - 64 + key
    inside = (key >= row) & (key <= row + 128) & (token >= 0) & (token < 2048)
    r.window[...] = jnp.where(inside, 1.0, 0.0)
    for group, columns in enumerate(in_columns()):
        local = r.edge_token[:, columns] - space * 128
        weight = r.edge_weight[:, columns]
        places = lax.broadcasted_iota(jnp.int32, (128, 256), 0)
        matrix = jnp.zeros((128, 256), jnp.float32)
        for slot in range(3):
            matrix = matrix + jnp.where(local[slot : slot + 1] == places, weight[slot : slot + 1], 0.0)
        high = matrix.astype(jnp.bfloat16)
        both = jnp.concatenate([high, (matrix - high.astype(jnp.float32)).astype(jnp.bfloat16)], axis=0)
        r.edges_t[group] = both
        r.edges[group] = both.T

    for made in halo_tokens:
        made.wait_recv()
    for m in range(2):
        r.halo[m] = normalised(r.halo[m])[0].astype(jnp.bfloat16)
    every = jnp.concatenate([r.normed[...], r.halo[0], r.halo[1]], axis=0)
    for part in range(2):
        loads[1 + part].wait()
        for n in range(4):
            at = slice(part * 1024 + n * 256, part * 1024 + n * 256 + 256)
            value = dot_nn(every, r.w_qkv[:, slice(at.start + 1024, at.stop + 1024)]).astype(jnp.bfloat16)
            for m in range(2):
                edge = 256 + m * 128
                r.kv[m, 0:64, at] = value[edge : edge + 64]
                r.kv[m, 64:192, at] = value[m * 128 : m * 128 + 128]
                r.kv[m, 192:256, at] = value[edge + 64 : edge + 128]

    first = lax.broadcasted_iota(jnp.int32, (128, 128), 1) < 64

    def stacked(value):
        zero = jnp.zeros_like(value)
        return jnp.concatenate([jnp.where(first, value, zero), jnp.where(first, zero, value)], axis=0)

    def attend(i, carry):
        m, n = i // 8, lax.rem(i, 8)
        start = pl.multiple_of(n * 128, 128)
        columns, values = pl.ds(start, 128), pl.ds(start + 1024, 128)
        token_rows = pl.ds(pl.multiple_of(m * 128, 128), 128)
        scores = dot_nt(stacked(r.queries[token_rows, columns]), r.kv[m, :, columns])
        expo = jnp.where(r.window[...] > 0.0, jnp.exp(scores * 0.125), 0.0)
        probs = expo / jnp.sum(expo, axis=-1, keepdims=True)
        r.probs[i] = probs
        result = dot_nn(probs.astype(jnp.bfloat16), r.kv[m, :, values])
        r.att[token_rows, columns] = jnp.where(first, result[:128], result[128:]).astype(jnp.bfloat16)
        return carry

    lax.fori_loop(0, 16, attend, 0, unroll=2)
    att_here = pair(r.att, r.att_2)
    loads[3].wait()
    for columns in in_columns():
        value = r.tokens[:, columns].astype(jnp.float32) + dot_nn(r.att[...], r.w_out[:, columns])
        r.states[:, columns] = value.astype(jnp.bfloat16)
    states_here = pair(r.states, r.states_2)
    loads[4].wait()
    for columns in in_columns():
        value = dot_nn(r.states[...], r.w_hidden[:, columns]).astype(jnp.bfloat16)
        for m in range(2):
            r.hidden[m, 0:128, columns] = value[m * 128 : m * 128 + 128]
            r.hidden[m, 128:256, columns] = value[m * 128 : m * 128 + 128]

    home = member // 2

    def give(source, target, i, to):
        return pltpu.make_async_remote_copy(
            src_ref=source.at[to], dst_ref=target.at[member], send_sem=r.member_sems.at[i, 0, to],
            recv_sem=r.member_sems.at[i, 1, member], device_id=(to, space), device_id_type=MESH,
        )

    def take(target, i, source):
        return pltpu.make_async_remote_copy(
            src_ref=target.at[source], dst_ref=target.at[source], send_sem=r.member_sems.at[i, 0, source],
            recv_sem=r.member_sems.at[i, 1, source], device_id=(source, space), device_id_type=MESH,
        )

    for n in range(4):
        group = lax.rem(home + 1 + n, 4)

        def forward(b, carry, group=group):
            forecast = jnp.zeros((256, 128), jnp.float32)
            for columns in in_columns():
                value, derivative = gelu_both(dot_nn(r.edges[group], r.hidden[b, :, columns]))
                value = value.astype(jnp.bfloat16)
                r.active[b, group, :, columns] = value
                r.slope[b, group, :, columns] = derivative.astype(jnp.bfloat16)
                forecast = forecast + dot_nn(value, r.readout[columns, :])
            r.sent[2 * group, b] = forecast[:128].astype(jnp.bfloat16)
            r.sent[2 * group + 1, b] = forecast[128:].astype(jnp.bfloat16)
            return carry

        lax.fori_loop(0, 2, forward, 0)
        if n < 3:
            give(r.sent, r.held, 0, 2 * group).start()
            give(r.sent, r.held, 0, 2 * group + 1).start()
        else:
            give(r.sent, r.held, 0, 2 * group + 1 - lax.rem(member, 2)).start()
            r.held[member] = r.sent[member]
    r.area_here[...] = jnp.broadcast_to(r.area[pl.ds(member, 1), :], (128, 128)).T
    loads[5].wait()
    for other in others:
        take(r.held, 0, other).wait_recv()

    multiplier = math.sqrt(16 / 16384)
    eps_fair = (1.0 - ALPHA) / 16

    def score(block, carry):
        rows = pl.ds(pl.multiple_of(block * 16, 16), 16)
        whole = [r.held[m // 2, m % 2, rows, :].astype(jnp.float32) for m in range(16)]
        truth, area = r.truth[rows, :], r.area_here[rows, :]
        found = [[] for _ in range(16)]
        for half in (slice(0, 8), slice(8, 16)):
            values = [value[half] for value in whole]
            spread = [None] * 16
            for j in range(16):
                for k in range(j + 1, 16):
                    d = values[j] - values[k]
                    s = d * lax.rsqrt(d * d + DELTA * DELTA)
                    spread[j] = s if spread[j] is None else spread[j] + s
                    spread[k] = -s if spread[k] is None else spread[k] - s
            for j in range(16):
                d = values[j] - truth[half]
                s = d * lax.rsqrt(d * d + DELTA * DELTA)
                found[j].append(
                    multiplier * area[half] * (s / 16 - (1.0 - eps_fair) / (16 * 15) * spread[j])
                )
        for j in range(16):
            r.sent_back[j // 2, j % 2, rows, :] = jnp.concatenate(found[j], axis=0).astype(jnp.bfloat16)
        return carry

    lax.fori_loop(0, 8, score, 0)
    for other in others:
        give(r.sent_back, r.held_back, 1, other).start()
    r.held_back[member] = r.sent_back[member]

    r.gathered[...] = jnp.zeros_like(r.gathered)
    r.turned[...] = jnp.zeros_like(r.turned)
    for n in range(4):
        group = lax.rem(home + n, 4)
        if n == 0:
            take(r.held_back, 1, 2 * group + 1 - lax.rem(member, 2)).wait_recv()
        else:
            take(r.held_back, 1, 2 * group).wait_recv()
            take(r.held_back, 1, 2 * group + 1).wait_recv()

        def backward(b, carry, group=group):
            grad = jnp.concatenate([r.held_back[2 * group, b], r.held_back[2 * group + 1, b]], axis=0)
            token_rows = pl.ds(pl.multiple_of(b * 128, 128), 128)
            for columns in in_columns():
                hidden = dot_nt(grad, r.readout[columns, :])
                grad_pre = (hidden * r.slope[b, group, :, columns].astype(jnp.float32)).astype(jnp.bfloat16)
                both = dot_nn(r.edges_t[group], grad_pre)
                r.gathered[token_rows, columns] += both[:128] + both[128:]
                r.turned[:, columns] += dot_tn(grad, r.active[b, group, :, columns])
            return carry

        lax.fori_loop(0, 2, backward, 0)

    mine = pl.ds(pl.multiple_of(core * 512, 512), 512)
    other_half = pl.ds(pl.multiple_of((1 - core) * 512, 512), 512)
    high = r.gathered[...].astype(jnp.bfloat16)
    r.gather_b[...] = high
    gather_here = pair(r.gather_b.at[:, other_half], r.gather_2)
    r.readout_grad[...] = r.turned[...].T.astype(jnp.bfloat16)
    readout_here = pair(r.readout_grad, r.readout_2)
    low = (r.gathered[...] - high.astype(jnp.float32)).astype(jnp.bfloat16)
    for rows in in_columns():
        weights = r.w_hidden[rows, :]
        value = dot_nt(high, weights) + dot_nt(low, weights)
        r.grad_s[:, rows] = value
        r.grad_sb[:, rows] = value.astype(jnp.bfloat16)
    grad_s_here = pair(r.grad_sb.at[:, other_half], r.grad_s2)

    def early_tile(tile, y, value):
        columns = slice(tile % 3 * 128, tile % 3 * 128 + 128)
        r.early_data[tile // 3, y, :, :, :, :, columns] = value.astype(jnp.bfloat16).reshape(2, 2, 4, 16, 128)

    states_here.wait_recv()
    gather_here.wait_recv()
    for y, rows in enumerate(in_columns()):
        value = dot_tn(r.states[:, rows], r.gather_b[:, mine]) + dot_tn(r.states_2[:, rows], r.gather_2[...])
        for tile in range(4):
            early_tile(tile, y, value[:, tile * 128 : tile * 128 + 128])
    readout_here.wait_recv()
    for y, rows in enumerate(in_columns()):
        early_tile(8, y, r.readout_grad[rows, :].astype(jnp.float32) + r.readout_2[rows, :].astype(jnp.float32))
    att_here.wait_recv()
    grad_s_here.wait_recv()
    for y, rows in enumerate(in_columns()):
        value = dot_tn(r.att[:, rows], r.grad_sb[:, mine]) + dot_tn(r.att_2[:, rows], r.grad_s2[...])
        for tile in range(4):
            early_tile(4 + tile, y, value[:, tile * 128 : tile * 128 + 128])

    def early_finish(part, total):
        r.early_final[:, :, part * 384 : part * 384 + 384] = total.reshape(2, 8, 384)

    def late_finish(part, total):
        r.late_final[:, :, part * 512 : part * 512 + 512] = total.reshape(2, 8, 512)

    split = len(ring_scratch) // 2
    early = RingSum(place, 384, [r.early_data.at[part] for part in range(3)], ring_scratch[:split], early_finish)
    late = RingSum(place, 512, [r.late_data.at[part] for part in range(3)], ring_scratch[split:], late_finish)
    for part in range(3):
        early.open(part, 0)
    early_steps = early.steps()

    for rows in in_columns():
        r.grad_att[:, rows] = dot_nt(r.grad_sb[...], r.w_out[rows, :]).astype(jnp.bfloat16)

    def attend_back(m, n, carry):
        start = pl.multiple_of(n * 128, 128)
        columns, values = pl.ds(start, 128), pl.ds(start + 1024, 128)
        token_rows = pl.ds(m * 128, 128)
        queries = stacked(r.queries[token_rows, columns])
        grads = stacked(r.grad_att[token_rows, columns])
        probs = r.probs[m * 8 + n]
        dprob = dot_nt(grads, r.kv[m, :, values])
        inner = jnp.sum(probs * dprob, axis=-1, keepdims=True)
        dscore = (probs * (dprob - inner) * 0.125).astype(jnp.bfloat16)
        grad_q = dot_nn(dscore, r.kv[m, :, columns])
        r.grad_qkv[token_rows, columns] = jnp.where(first, grad_q[:128], grad_q[128:]).astype(jnp.bfloat16)
        for value, at in (
            (dot_tn(dscore, queries), columns), (dot_tn(probs.astype(jnp.bfloat16), grads), values)
        ):
            r.lower[m, :, at] = value[:64].astype(jnp.bfloat16)
            r.middle[token_rows, at] = value[64:192]
            r.upper[m, :, at] = value[192:].astype(jnp.bfloat16)
        return carry

    halos = []
    for m in range(2):
        for half in range(2):
            lax.fori_loop(half * 4, half * 4 + 4, functools.partial(attend_back, m), 0, unroll=2)
            for _ in range(4):
                next(early_steps, None)
        halos.append(push(r.lower.at[m], r.from_above.at[m], r.halo_sems, (0, m), below))
        halos.append(push(r.upper.at[m], r.from_below.at[m], r.halo_sems, (1, m), above))

    def swap(part):
        at = pl.ds(pl.multiple_of(part * 1024 + (1 - core) * 512, 512), 512)
        return pair(r.grad_qkv.at[:, at], r.grad_qkv2.at[part])

    def late_product(part):
        own = r.grad_qkv[:, pl.ds(pl.multiple_of(part * 1024 + core * 512, 512), 512)]
        for y, rows in enumerate(in_columns()):
            value = dot_tn(r.normed[:, rows], own) + dot_tn(r.normed_2[:, rows], r.grad_qkv2[part])
            r.late_data[part, y] = value.astype(jnp.bfloat16).reshape(2, 2, 4, 16, 512)
        late.open(part, 0)

    swaps = [swap(0)]
    normed_here.wait_recv()
    swaps[0].wait_recv()
    late_product(0)
    for made in halos:
        made.wait_recv()
    for m in range(2):
        low_rows, high_rows = slice(m * 128, m * 128 + 64), slice(m * 128 + 64, m * 128 + 128)
        for part in range(2):
            at, into = slice(part * 1024, part * 1024 + 1024), slice(part * 1024 + 1024, part * 1024 + 2048)
            for rows, arrived in ((low_rows, r.from_below), (high_rows, r.from_above)):
                total = r.middle[rows, at] + arrived[m, :, at].astype(jnp.float32)
                r.grad_qkv[rows, into] = total.astype(jnp.bfloat16)
    swaps += [swap(1), swap(2)]
    for _ in early_steps:
        pass
    final_sums = [push(r.early_final.at[1 - core], r.early_other, r.final_sems, (0,), place.partner)]
    for part in (1, 2):
        swaps[part].wait_recv()
        late_product(part)
    late_steps = late.steps()
    for rows in in_columns():
        r.middle[:, rows] = dot_nt(r.grad_qkv[...], r.w_qkv[rows, :])
        next(late_steps, None)
        next(late_steps, None)
    for block in range(4):
        rows = slice(block * 64, block * 64 + 64)
        normal_hat, inverse = normalised(r.tokens[rows, :])
        back = norm_back(r.middle[rows, :1024], normal_hat, inverse)
        r.grad_tokens[rows, :] = (r.grad_s[rows, :] + back).astype(jnp.bfloat16)
    for _ in late_steps:
        pass
    final_sums.append(push(r.late_final.at[1 - core], r.late_other, r.final_sems, (1,), place.partner))

    yours = pl.ds(pl.multiple_of((1 - core) * 512, 512), 512)
    r.grad_hidden_w[:, mine] = r.early_final[core, :, :512]
    r.grad_out_w[:, mine] = r.early_final[core, :, 512:1024]
    r.grad_readout[...] = r.early_final[core, :, 1024:]
    final_sums[0].wait_recv()
    r.grad_hidden_w[:, yours] = r.early_other[:, :512]
    r.grad_out_w[:, yours] = r.early_other[:, 512:1024]
    final_sums[1].wait_recv()
    for part in range(3):
        at = slice(part * 512, part * 512 + 512)
        for half, rows in ((core, r.late_final[core, :, at]), (1 - core, r.late_other[:, at])):
            r.grad_qkv_w[:, pl.ds(pl.multiple_of(part * 1024 + half * 512, 512), 512)] = rows
    for made in sent_copies:
        made.wait_send()
    for other in others:
        give(r.sent, r.held, 0, other).wait_send()
        give(r.sent_back, r.held_back, 1, other).wait_send()
    early.drain()
    late.drain()


def on_device(
    tokens, w_qkv, w_out, w_hidden, decoder_readout_matrix, edge_token, edge_weight, truth_state, area
):
    vmem, anywhere = pl.BlockSpec(memory_space=pltpu.VMEM), pl.BlockSpec(memory_space=pl.ANY)
    dma = pltpu.SemaphoreType.DMA

    def b16(*shape):
        return pltpu.VMEM(shape, jnp.bfloat16)

    def f32(*shape):
        return pltpu.VMEM(shape, jnp.float32)

    inputs = {
        "tokens": (tokens.reshape(256, 1024), vmem),
        "w_qkv_hbm": (w_qkv, anywhere),
        "w_out_hbm": (w_out, anywhere),
        "w_hidden_hbm": (w_hidden, anywhere),
        "readout": (decoder_readout_matrix, vmem),
        "edge_token": (edge_token.T, vmem),
        "edge_weight": (edge_weight.T, vmem),
        "truth_hbm": (truth_state, anywhere),
        "area": (area.reshape(8, 128), vmem),
    }
    outputs = {
        "grad_tokens": jax.ShapeDtypeStruct((256, 1024), jnp.bfloat16),
        "grad_qkv_w": jax.ShapeDtypeStruct((8, 3072), jnp.float32),
        "grad_out_w": jax.ShapeDtypeStruct((8, 1024), jnp.float32),
        "grad_hidden_w": jax.ShapeDtypeStruct((8, 1024), jnp.float32),
        "grad_readout": jax.ShapeDtypeStruct((8, 128), jnp.float32),
    }
    scratch = {
        "w_qkv": b16(1024, 3072), "w_out": b16(1024, 1024), "w_hidden": b16(1024, 1024), "truth": f32(128, 128),
        "area_here": f32(128, 128), "halo": b16(2, 128, 1024), "normed": b16(256, 1024), "normed_2": b16(256, 1024),
        "queries": b16(256, 1024), "kv": b16(2, 256, 2048), "window": f32(256, 256), "probs": f32(16, 256, 256),
        "att": b16(256, 1024), "att_2": b16(256, 1024), "states": b16(256, 1024), "states_2": b16(256, 1024),
        "hidden": b16(2, 256, 1024), "edges": b16(4, 256, 256), "edges_t": b16(4, 256, 256),
        "active": b16(2, 4, 256, 1024), "slope": b16(2, 4, 256, 1024),
        "sent": b16(8, 2, 128, 128), "held": b16(8, 2, 128, 128),
        "sent_back": b16(8, 2, 128, 128), "held_back": b16(8, 2, 128, 128), "turned": f32(128, 1024),
        "gathered": f32(256, 1024), "gather_b": b16(256, 1024), "gather_2": b16(256, 512),
        "grad_s": f32(256, 1024), "grad_sb": b16(256, 1024), "grad_s2": b16(256, 512), "grad_att": b16(256, 1024),
        "readout_grad": b16(1024, 128), "readout_2": b16(1024, 128), "grad_qkv": b16(256, 3072),
        "grad_qkv2": b16(3, 256, 512), "middle": f32(256, 2048), "lower": b16(2, 64, 2048), "upper": b16(2, 64, 2048),
        "from_above": b16(2, 64, 2048), "from_below": b16(2, 64, 2048),
        "early_data": b16(3, *FULL, 16, 384), "late_data": b16(3, *FULL, 16, 512),
        "early_final": f32(2, 8, 1152), "late_final": f32(2, 8, 1536),
        "early_other": f32(8, 1152), "late_other": f32(8, 1536),
        "load_sems": dma((6,)), "token_sems": dma((2, 2, 2)), "pair_sems": dma((2, 9)), "halo_sems": dma((2, 2, 2)),
        "member_sems": dma((2, 2, 8)), "final_sems": dma((2, 2)),
    }
    names = [*inputs, *outputs, *scratch]
    results = pl.pallas_call(
        functools.partial(kernel, names),
        out_shape=tuple(outputs.values()),
        in_specs=[spec for _, spec in inputs.values()],
        out_specs=[vmem] * len(outputs),
        scratch_shapes=[*scratch.values(), *sum_scratch(384), *sum_scratch(512)],
        compiler_params=pltpu.CompilerParams(
            collective_id=0, has_side_effects=True, vmem_limit_bytes=62 * 2**20
        ),
    )(*[value for value, _ in inputs.values()])
    return (results[0].reshape(tokens.shape), *results[1:])


def solution(mesh):
    in_specs = (
        P("member", "space", None),
        P(),
        P(),
        P(),
        P(),
        P("space", None),
        P("space", None),
        P("space", None),
        P("space"),
    )
    out_specs = (
        P("member", "space", None),
        P(("member", "space"), None),
        P(("member", "space"), None),
        P(("member", "space"), None),
        P(("member", "space"), None),
    )
    return jax.shard_map(
        on_device, mesh=mesh, in_specs=in_specs, out_specs=out_specs, check_vma=False
    )
```

```python
import functools
import math
import types

import jax
import jax.numpy as jnp
from jax import lax
from jax.experimental import pallas as pl
from jax.experimental.pallas import tpu as pltpu
from jax.sharding import PartitionSpec as P

EPS = 1e-05
ALPHA = 0.95
DELTA = 0.1


MESH = pl.DeviceIdType.MESH


class Place:
    def __init__(self):
        member, space = lax.axis_index("member"), lax.axis_index("space")
        self.member, self.space = member, space
        self.y, z_lo = member // 2, member % 2
        z_hi = space // 8
        self.x, self.core = (space // 2) % 4, space % 2
        self.z = z_hi * 2 + z_lo
        self.partner = (member, space + 1 - 2 * self.core)

    def ring(self, axis):
        return {"x": self.x, "y": self.y, "z": self.z}[axis]

    def device(self, axis, j):
        if axis == "x":
            return (self.member, (self.space // 8) * 8 + j * 2 + self.core)
        if axis == "y":
            return (j * 2 + self.member % 2, self.space)
        return ((self.member // 2) * 2 + j % 2, (j // 2) * 8 + self.space % 8)

    def neighbours(self):
        found = []
        for axis in "xyz":
            i = self.ring(axis)
            found += [self.device(axis, (i + 1) % 4), self.device(axis, (i + 3) % 4)]
        return found


def entry_barrier(devices):
    barrier = pltpu.get_barrier_semaphore()
    for device in devices:
        pl.semaphore_signal(barrier, inc=1, device_id=device, device_id_type=MESH)
    pl.semaphore_wait(barrier, len(devices))


ORDERS = (
    (
        ("x", (4, 2, 2), lambda j, r: (*r, j)),
        ("y", (2, 2), lambda j, r: (j, *r)),
        ("z", (), lambda j, r: (j % 2, j // 2)),
    ),
    (
        ("y", (2, 2, 4), lambda j, r: (j, *r)),
        ("z", (4,), lambda j, r: (j % 2, j // 2, *r)),
        ("x", (), lambda j, r: (j,)),
    ),
    (
        ("z", (4, 4), lambda j, r: (r[0], j % 2, j // 2, r[1])),
        ("x", (4,), lambda j, r: (r[0], j)),
        ("y", (), lambda j, r: (j,)),
    ),
)
FULL = (4, 2, 2, 4)


def first_columns(width):
    return width // 128 // 2 * 128


def sum_scratch(width):
    low = first_columns(width)
    shapes = []
    for order in ORDERS:
        for phase, (_, rest, _) in enumerate(order):
            columns = (width, width, low, width - low) if phase == 0 else (width, width, width)
            for count in columns + (width,) * (phase < 2):
                shapes.append(pltpu.VMEM((*rest, 16, count), jnp.bfloat16))
    return shapes + [pltpu.SemaphoreType.DMA((54,)), pltpu.SemaphoreType.DMA((54,))]


def over(dims, body):
    if len(dims) <= 1:
        body((slice(None),) * len(dims))
        return
    count = math.prod(dims[:-1])

    def step(n, carry):
        index = []
        for size in reversed(dims[:-1]):
            index.insert(0, lax.rem(n, size))
            n = n // size
        body((*index, slice(None)))
        return carry

    lax.fori_loop(0, count, step, 0)


class RingSum:
    def __init__(self, place, width, parts, scratch, finish):
        self.place, self.width, self.low = place, width, first_columns(width)
        scratch = list(scratch)
        self.recv, self.send = scratch.pop(), scratch.pop()
        self.slots = []
        for _ in range(3):
            self.slots.append([])
            for phase in range(3):
                count = (5, 4, 3)[phase]
                self.slots[-1].append(scratch[:count])
                scratch = scratch[count:]
        self.data = [[part] for part in parts]
        for part in range(3):
            self.data[part] += [self.slots[part][0][4], self.slots[part][1][3]]
        self.finish = finish
        self.copies = {}

    def copy(self, part, phase, message, source, target, device):
        sem = (part * 3 + phase) * 6 + message
        made = pltpu.make_async_remote_copy(
            src_ref=source, dst_ref=target, send_sem=self.send.at[sem], recv_sem=self.recv.at[sem],
            device_id=device, device_id_type=MESH,
        )
        made.start()
        self.copies[part, phase, message] = made

    def view(self, part, phase, j, low):
        _, rest, at = ORDERS[part][phase]
        columns = pl.ds(0, self.low) if low else pl.ds(self.low, self.width - self.low)
        return self.data[part][phase].at[(*at(j, (slice(None),) * len(rest)), slice(None), columns)]

    def around(self, part, phase):
        axis = ORDERS[part][phase][0]
        i = self.place.ring(axis)
        right, left = (i + 1) % 4, (i + 3) % 4
        return i, right, left, (i + 2) % 4, self.place.device(axis, right), self.place.device(axis, left)

    def open(self, part, phase):
        _, right, left, opposite, to_right, to_left = self.around(part, phase)
        if phase:
            axis, rest, at = ORDERS[part][phase]
            across = self.place.device(axis, opposite)
            for message, (j, to) in enumerate(((opposite, across), (right, to_right), (left, to_left))):
                source = self.data[part][phase].at[(*at(j, (slice(None),) * len(rest)),)]
                self.copy(part, phase, message, source, self.slots[part][phase][message], to)
            return
        from_left, from_right, relay_left, relay_right = self.slots[part][phase][:4]
        low, high = pl.ds(0, self.low), pl.ds(self.low, self.width - self.low)
        self.copy(part, phase, 0, self.view(part, phase, opposite, True), relay_left, to_right)
        self.copy(part, phase, 1, self.view(part, phase, opposite, False), relay_right, to_left)
        self.copy(part, phase, 2, self.view(part, phase, right, False), from_left.at[..., high], to_right)
        self.copy(part, phase, 3, self.view(part, phase, left, True), from_right.at[..., low], to_left)

    def relay(self, part, phase):
        _, right, left, _, to_right, to_left = self.around(part, phase)
        _, rest, at = ORDERS[part][phase]
        from_left, from_right, relay_left, relay_right = self.slots[part][phase][:4]
        low, high = pl.ds(0, self.low), pl.ds(self.low, self.width - self.low)
        data = self.data[part][phase]
        for message, j, columns, relayed in ((0, right, low, relay_left), (1, left, high, relay_right)):
            self.copies[part, phase, message].wait_recv()

            def add(r, j=j, columns=columns, relayed=relayed):
                here = (*at(j, r), slice(None), columns)
                there = (*r, slice(None), slice(None))
                both = data[here].astype(jnp.float32) + relayed[there].astype(jnp.float32)
                data[here] = both.astype(jnp.bfloat16)

            over(rest, add)
            if message == 0:
                self.copy(part, phase, 4, self.view(part, phase, right, True), from_left.at[..., low], to_right)
            else:
                self.copy(part, phase, 5, self.view(part, phase, left, False), from_right.at[..., high], to_left)

    def close(self, part, phase):
        i = self.around(part, phase)[0]
        _, rest, at = ORDERS[part][phase]
        arrived = self.slots[part][phase][: 3 if phase else 2]
        data = self.data[part][phase]
        for message in (0, 1, 2) if phase else (2, 3, 4, 5):
            self.copies[part, phase, message].wait_recv()

        def add(r):
            there = (*r, slice(None), slice(None))
            total = data[(*at(i, r), slice(None), slice(None))].astype(jnp.float32)
            for slot in arrived:
                total = total + slot[there].astype(jnp.float32)
            if phase < 2:
                self.data[part][phase + 1][there] = total.astype(jnp.bfloat16)
            else:
                self.finish(part, total)

        over(rest, add)

    def relays(self):
        for part in range(3):
            self.relay(part, 0)

    def advance(self, phase):
        for part in range(3):
            self.close(part, phase)
            if phase < 2:
                self.open(part, phase + 1)

    def drain(self):
        for made in self.copies.values():
            made.wait_send()


NT = (((1,), (1,)), ((), ()))
TN = (((0,), (0,)), ((), ()))


def dot_nn(a, b):
    return jnp.dot(a, b, preferred_element_type=jnp.float32)


def dot_nt(a, b):
    return lax.dot_general(a, b, NT, preferred_element_type=jnp.float32)


def dot_tn(a, b):
    return lax.dot_general(a, b, TN, preferred_element_type=jnp.float32)


def gelu_both(x):
    bell = jnp.exp(-0.5 * (x * x))
    t = 1.0 / (1.0 + (0.3275911 / math.sqrt(2.0)) * jnp.abs(x))
    poly = t * (
        0.5 * 0.254829592
        + t * (-0.5 * 0.284496736 + t * (0.5 * 1.421413741 + t * (-0.5 * 1.453152027 + t * (0.5 * 1.061405429))))
    )
    tail = poly * bell
    share = jnp.where(x >= 0.0, 1.0 - tail, tail)
    return x * share, share + x * (bell * (1.0 / math.sqrt(2.0 * math.pi)))


def norm_back(objective_derivative, normal_hat, inverse):
    first = jnp.mean(objective_derivative, axis=-1, keepdims=True)
    second = jnp.mean(objective_derivative * normal_hat, axis=-1, keepdims=True)
    return inverse * (objective_derivative - first - normal_hat * second)


def normalised(values):
    wide = values.astype(jnp.float32)
    centre = wide - jnp.mean(wide, axis=-1, keepdims=True)
    inverse = lax.rsqrt(jnp.mean(centre * centre, axis=-1, keepdims=True) + EPS)
    return centre * inverse, inverse


def in_columns(count=4):
    return [slice(part * 256, part * 256 + 256) for part in range(count)]


def kernel(names, *refs):
    r = types.SimpleNamespace(**dict(zip(names, refs)))
    ring_scratch = refs[len(names) :]
    place = Place()
    member, space, core = place.member, place.space, place.core

    loads = [
        pltpu.make_async_copy(
            r.w_qkv_hbm.at[:, pl.ds(part * 1024, 1024)], r.w_qkv.at[:, pl.ds(part * 1024, 1024)], r.load_sems.at[part]
        )
        for part in range(3)
    ]
    loads.append(pltpu.make_async_copy(r.w_out_hbm, r.w_out, r.load_sems.at[3]))
    loads.append(pltpu.make_async_copy(r.w_hidden_hbm, r.w_hidden, r.load_sems.at[4]))
    loads.append(pltpu.make_async_copy(
        r.truth_hbm.at[pl.ds(pl.multiple_of(member * 128, 128), 128), :], r.truth, r.load_sems.at[5]
    ))
    for load in loads:
        load.start()

    above, below = (member, lax.rem(space + 1, 16)), (member, lax.rem(space + 15, 16))
    others = [
        lax.rem(place.y + 4 - back, 4) * 2 + lax.rem(member + turn, 2)
        for back, turn in ((0, 1), (1, 0), (1, 1), (2, 0), (2, 1), (3, 0), (3, 1))
    ]
    entry_barrier([above, below, place.partner, *place.neighbours(), *[(other, space) for other in others]])
    sent_copies = []

    def push(source, target, sems, i, device):
        made = pltpu.make_async_remote_copy(
            src_ref=source, dst_ref=target, send_sem=sems.at[(0, *i)], recv_sem=sems.at[(1, *i)],
            device_id=device, device_id_type=MESH,
        )
        made.start()
        sent_copies.append(made)
        return made

    halo_tokens = []
    for m in range(2):
        halo_tokens.append(push(
            r.tokens.at[pl.ds(m * 128 + 64, 64)], r.halo.at[m, pl.ds(0, 64)], r.token_sems, (0, m), above
        ))
        halo_tokens.append(push(
            r.tokens.at[pl.ds(m * 128, 64)], r.halo.at[m, pl.ds(64, 64)], r.token_sems, (1, m), below
        ))

    pair_count = [0]

    def pair(source, target):
        pair_count[0] += 1
        return push(source, target, r.pair_sems, (pair_count[0] - 1,), place.partner)

    for block in range(4):
        rows = slice(block * 64, block * 64 + 64)
        r.normed[rows, :] = normalised(r.tokens[rows, :])[0].astype(jnp.bfloat16)
    normed_here = pair(r.normed, r.normed_2)
    loads[0].wait()
    for columns in in_columns():
        r.queries[:, columns] = dot_nn(r.normed[...], r.w_qkv[:, columns]).astype(jnp.bfloat16)

    def push_edges(source, target, sems):
        made = []
        for m in range(2):
            made.append(push(source.at[pl.ds(m * 128 + 64, 64)], target.at[m, pl.ds(0, 64)], sems, (0, m), above))
            made.append(push(source.at[pl.ds(m * 128, 64)], target.at[m, pl.ds(64, 64)], sems, (1, m), below))
        return made

    queries_here = push_edges(r.queries, r.queries_h, r.query_sems)
    for part in range(2):
        loads[1 + part].wait()
        for n in range(4):
            at = slice(part * 1024 + n * 256, part * 1024 + n * 256 + 256)
            value = dot_nn(r.normed[...], r.w_qkv[:, slice(at.start + 1024, at.stop + 1024)]).astype(jnp.bfloat16)
            r.kv[0, 0:128, at] = value[:128]
            r.kv[1, 0:128, at] = value[128:]

    row = lax.broadcasted_iota(jnp.int32, (256, 256), 0) % 128
    key = lax.broadcasted_iota(jnp.int32, (256, 256), 1)
    offset = jnp.where(key < 128, key, jnp.where(key < 192, key - 192, key - 64))
    token = space * 128 + offset
    inside = (offset >= row - 64) & (offset <= row + 64) & (token >= 0) & (token < 2048)
    r.window[...] = jnp.where(inside, 1.0, 0.0)
    row = lax.broadcasted_iota(jnp.int32, (256, 128), 0) % 128
    key = lax.broadcasted_iota(jnp.int32, (256, 128), 1)
    offset = jnp.where(row < 64, row - 64, row + 64)
    token = space * 128 + offset
    inside = (key >= offset - 64) & (key <= offset + 64) & (token >= 0) & (token < 2048)
    r.window_h[...] = jnp.where(inside, 1.0, 0.0)
    for group, columns in enumerate(in_columns()):
        local = r.edge_token[:, columns] - space * 128
        weight = r.edge_weight[:, columns]
        places = lax.broadcasted_iota(jnp.int32, (128, 256), 0)
        matrix = jnp.zeros((128, 256), jnp.float32)
        for slot in range(3):
            matrix = matrix + jnp.where(local[slot : slot + 1] == places, weight[slot : slot + 1], 0.0)
        high = matrix.astype(jnp.bfloat16)
        both = jnp.concatenate([high, (matrix - high.astype(jnp.float32)).astype(jnp.bfloat16)], axis=0)
        r.edges_t[group] = both
        r.edges[group] = both.T

    def edge_keys(m):
        for made in halo_tokens[2 * m : 2 * m + 2]:
            made.wait_recv()
        edges_normed = normalised(r.halo[m])[0].astype(jnp.bfloat16)
        for n in range(8):
            at = slice(n * 256, n * 256 + 256)
            value = dot_nn(edges_normed, r.w_qkv[:, slice(at.start + 1024, at.stop + 1024)])
            r.kv[m, 128:256, at] = value.astype(jnp.bfloat16)

    first = lax.broadcasted_iota(jnp.int32, (128, 128), 1) < 64

    def stacked(value):
        zero = jnp.zeros_like(value)
        return jnp.concatenate([jnp.where(first, value, zero), jnp.where(first, zero, value)], axis=0)

    lane = lax.broadcasted_iota(jnp.int32, (256, 128), 1)
    r.scales[...] = jnp.zeros_like(r.scales)

    def attend(i, carry):
        m, n = i // 8, lax.rem(i, 8)
        start = pl.multiple_of(n * 128, 128)
        columns, values = pl.ds(start, 128), pl.ds(start + 1024, 128)
        token_rows = pl.ds(pl.multiple_of(m * 128, 128), 128)
        scores = dot_nt(stacked(r.queries[token_rows, columns]), r.kv[m, :, columns])
        expo = jnp.where(r.window[...] > 0.0, jnp.exp(scores * 0.125), 0.0)
        scale = 1.0 / jnp.sum(expo, axis=-1, keepdims=True)
        probs = expo * scale
        r.probs[i] = probs
        r.scales[...] = jnp.where(lane == i, scale, r.scales[...])
        result = dot_nn(probs.astype(jnp.bfloat16), r.kv[m, :, values])
        r.att[token_rows, columns] = jnp.where(first, result[:128], result[128:]).astype(jnp.bfloat16)
        return carry

    for m in range(2):
        edge_keys(m)
        lax.fori_loop(m * 8, m * 8 + 8, attend, 0, unroll=2)
    att_here = pair(r.att, r.att_2)
    edge_here = queries_here + push_edges(r.att, r.att_h, r.att_sems)
    for head in range(2):
        begin = head * 128
        edge_here.append(push(
            r.scales.at[pl.ds(begin + 64, 64)], r.scales_h.at[pl.ds(begin, 64)], r.scale_sems, (0, head), above
        ))
        edge_here.append(push(
            r.scales.at[pl.ds(begin, 64)], r.scales_h.at[pl.ds(begin + 64, 64)], r.scale_sems, (1, head), below
        ))
    loads[3].wait()
    for columns in in_columns():
        value = r.tokens[:, columns].astype(jnp.float32) + dot_nn(r.att[...], r.w_out[:, columns])
        r.states[:, columns] = value.astype(jnp.bfloat16)
    states_here = pair(r.states, r.states_2)
    loads[4].wait()
    for columns in in_columns():
        value = dot_nn(r.states[...], r.w_hidden[:, columns]).astype(jnp.bfloat16)
        for m in range(2):
            r.hidden[m, 0:128, columns] = value[m * 128 : m * 128 + 128]
            r.hidden[m, 128:256, columns] = value[m * 128 : m * 128 + 128]

    home = member // 2

    def give(source, target, i, to):
        return pltpu.make_async_remote_copy(
            src_ref=source.at[to], dst_ref=target.at[member], send_sem=r.member_sems.at[i, 0, to],
            recv_sem=r.member_sems.at[i, 1, member], device_id=(to, space), device_id_type=MESH,
        )

    def take(target, i, source):
        return pltpu.make_async_remote_copy(
            src_ref=target.at[source], dst_ref=target.at[source], send_sem=r.member_sems.at[i, 0, source],
            recv_sem=r.member_sems.at[i, 1, source], device_id=(source, space), device_id_type=MESH,
        )

    for n in range(4):
        group = lax.rem(home + 1 + n, 4)

        def forward(b, carry, group=group):
            forecast = jnp.zeros((256, 128), jnp.float32)
            for columns in in_columns():
                value, derivative = gelu_both(dot_nn(r.edges[group], r.hidden[b, :, columns]))
                value = value.astype(jnp.bfloat16)
                r.active[b, group, :, columns] = value
                r.slope[b, group, :, columns] = derivative.astype(jnp.bfloat16)
                forecast = forecast + dot_nn(value, r.readout[columns, :])
            r.sent[2 * group, b] = forecast[:128].astype(jnp.bfloat16)
            r.sent[2 * group + 1, b] = forecast[128:].astype(jnp.bfloat16)
            return carry

        lax.fori_loop(0, 2, forward, 0)
        if n < 3:
            give(r.sent, r.held, 0, 2 * group).start()
            give(r.sent, r.held, 0, 2 * group + 1).start()
        else:
            give(r.sent, r.held, 0, 2 * group + 1 - lax.rem(member, 2)).start()
            r.held[member] = r.sent[member]
    r.area_here[...] = jnp.broadcast_to(r.area[pl.ds(member, 1), :], (128, 128)).T
    loads[5].wait()

    def turn(source, target, begin):
        for columns in in_columns():
            target[columns, begin : begin + 256] = source[:, columns].T

    turn(r.states, r.states_t, 0)
    states_here.wait_recv()
    turn(r.states_2, r.states_t, 256)
    turn(r.att, r.att_t, 0)
    for other in others:
        take(r.held, 0, other).wait_recv()

    multiplier = math.sqrt(16 / 16384)
    eps_fair = (1.0 - ALPHA) / 16

    def score(block, carry):
        rows = pl.ds(pl.multiple_of(block * 16, 16), 16)
        whole = [r.held[m // 2, m % 2, rows, :].astype(jnp.float32) for m in range(16)]
        truth, area = r.truth[rows, :], r.area_here[rows, :]
        found = [[] for _ in range(16)]
        for half in (slice(0, 8), slice(8, 16)):
            values = [value[half] for value in whole]
            spread = [None] * 16
            for j in range(16):
                for k in range(j + 1, 16):
                    d = values[j] - values[k]
                    s = d * lax.rsqrt(d * d + DELTA * DELTA)
                    spread[j] = s if spread[j] is None else spread[j] + s
                    spread[k] = -s if spread[k] is None else spread[k] - s
            for j in range(16):
                d = values[j] - truth[half]
                s = d * lax.rsqrt(d * d + DELTA * DELTA)
                found[j].append(
                    multiplier * area[half] * (s / 16 - (1.0 - eps_fair) / (16 * 15) * spread[j])
                )
        for j in range(16):
            r.sent_back[j // 2, j % 2, rows, :] = jnp.concatenate(found[j], axis=0).astype(jnp.bfloat16)
        return carry

    lax.fori_loop(0, 8, score, 0)
    for other in others:
        give(r.sent_back, r.held_back, 1, other).start()
    r.held_back[member] = r.sent_back[member]

    att_here.wait_recv()
    turn(r.att_2, r.att_t, 256)
    turn(r.normed, r.normed_t, 0)
    normed_here.wait_recv()
    turn(r.normed_2, r.normed_t, 256)
    r.gathered[...] = jnp.zeros_like(r.gathered)
    r.turned[...] = jnp.zeros_like(r.turned)
    for n in range(4):
        group = lax.rem(home + n, 4)
        if n == 0:
            take(r.held_back, 1, 2 * group + 1 - lax.rem(member, 2)).wait_recv()
        else:
            take(r.held_back, 1, 2 * group).wait_recv()
            take(r.held_back, 1, 2 * group + 1).wait_recv()

        def backward(b, group=group):
            grad = jnp.concatenate([r.held_back[2 * group, b], r.held_back[2 * group + 1, b]], axis=0)
            grad_t = grad.T
            token_rows = pl.ds(b * 128, 128)
            for columns in in_columns():
                hidden = dot_nt(grad, r.readout[columns, :])
                grad_pre = (hidden * r.slope[b, group, :, columns].astype(jnp.float32)).astype(jnp.bfloat16)
                both = dot_nn(r.edges_t[group], grad_pre)
                r.gathered[token_rows, columns] += both[:128] + both[128:]
                r.turned[:, columns] += dot_nn(grad_t, r.active[b, group, :, columns])

        for b in range(2):
            backward(b)

    mine = pl.ds(pl.multiple_of(core * 512, 512), 512)
    other_half = pl.ds(pl.multiple_of((1 - core) * 512, 512), 512)
    high = r.gathered[...].astype(jnp.bfloat16)
    r.gather_b[...] = high
    gather_here = pair(r.gather_b.at[:, other_half], r.gather_2)
    r.readout_grad[...] = r.turned[...].T.astype(jnp.bfloat16)
    readout_here = pair(r.readout_grad, r.readout_2)
    low = (r.gathered[...] - high.astype(jnp.float32)).astype(jnp.bfloat16)
    for rows in in_columns():
        weights = r.w_hidden[rows, :]
        value = dot_nt(high, weights) + dot_nt(low, weights)
        r.grad_s[:, rows] = value
        r.grad_sb[:, rows] = value.astype(jnp.bfloat16)
    grad_s_here = pair(r.grad_sb.at[:, other_half], r.grad_s2)

    for rows in in_columns():
        r.grad_att[:, rows] = dot_nt(r.grad_sb[...], r.w_out[rows, :]).astype(jnp.bfloat16)
    edge_here += push_edges(r.grad_att, r.grad_att_h, r.grad_att_sems)

    def early_tile(tile, y, value):
        columns = slice(tile % 3 * 128, tile % 3 * 128 + 128)
        r.early_data[tile // 3, y, :, :, :, :, columns] = value.astype(jnp.bfloat16).reshape(2, 2, 4, 16, 128)

    gather_here.wait_recv()
    both = jnp.concatenate([r.gather_b[:, mine], r.gather_2[...]], axis=0)
    for y, rows in enumerate(in_columns()):
        value = dot_nn(r.states_t[rows, :], both)
        for tile in range(4):
            early_tile(tile, y, value[:, tile * 128 : tile * 128 + 128])
    readout_here.wait_recv()
    for y, rows in enumerate(in_columns()):
        early_tile(8, y, r.readout_grad[rows, :].astype(jnp.float32) + r.readout_2[rows, :].astype(jnp.float32))
    grad_s_here.wait_recv()
    both = jnp.concatenate([r.grad_sb[:, mine], r.grad_s2[...]], axis=0)
    for y, rows in enumerate(in_columns()):
        value = dot_nn(r.att_t[rows, :], both)
        for tile in range(4):
            early_tile(4 + tile, y, value[:, tile * 128 : tile * 128 + 128])

    def ring_sum(data, final, width, scratch):
        def finish(part, total):
            final[:, :, part * width : part * width + width] = total.reshape(2, 8, width)

        return RingSum(place, width, [data.at[part] for part in range(3)], scratch, finish)

    third = len(ring_scratch) // 3
    early = ring_sum(r.early_data, r.early_final, 384, ring_scratch[:third])
    late = [
        ring_sum(r.late_data.at[g], r.late_final.at[g], 256, ring_scratch[third * (1 + g) : third * (2 + g)])
        for g in range(2)
    ]
    for part in range(3):
        early.open(part, 0)

    def attend_back(i, carry):
        n, m = i // 2, lax.rem(i, 2)
        start = pl.multiple_of(n * 128, 128)
        columns, values = pl.ds(start, 128), pl.ds(start + 1024, 128)
        token_rows = pl.ds(pl.multiple_of(m * 128, 128), 128)
        turn_index = m * 8 + n
        queries = stacked(r.queries[token_rows, columns])
        grads = stacked(r.grad_att[token_rows, columns])
        att = r.att[token_rows, columns].astype(jnp.float32)
        inner = jnp.sum(grads.astype(jnp.float32) * jnp.concatenate([att, att], axis=0), axis=-1, keepdims=True)
        probs = r.probs[turn_index]
        dprob = dot_nt(grads, r.kv[m, :, values])
        dscore = (probs * (dprob - inner) * 0.125).astype(jnp.bfloat16)
        grad_q = dot_nn(dscore, r.kv[m, :, columns])
        r.grad_qkv[token_rows, columns] = jnp.where(first, grad_q[:128], grad_q[128:]).astype(jnp.bfloat16)

        queries_h = stacked(r.queries_h[m, :, columns])
        grads_h = stacked(r.grad_att_h[m, :, columns])
        att = r.att_h[m, :, columns].astype(jnp.float32)
        inner = jnp.sum(grads_h.astype(jnp.float32) * jnp.concatenate([att, att], axis=0), axis=-1, keepdims=True)
        scale = jnp.sum(jnp.where(lane == turn_index, r.scales_h[...], 0.0), axis=-1, keepdims=True)
        scores = dot_nt(queries_h, r.kv[m, 0:128, columns])
        probs_h = jnp.where(r.window_h[...] > 0.0, jnp.exp(scores * 0.125) * scale, 0.0)
        dprob = dot_nt(grads_h, r.kv[m, 0:128, values])
        dscore_h = (probs_h * (dprob - inner) * 0.125).astype(jnp.bfloat16)

        grad_k = dot_tn(
            jnp.concatenate([dscore[:, :128], dscore_h], axis=0), jnp.concatenate([queries, queries_h], axis=0)
        )
        grad_v = dot_tn(
            jnp.concatenate([probs[:, :128].astype(jnp.bfloat16), probs_h.astype(jnp.bfloat16)], axis=0),
            jnp.concatenate([grads, grads_h], axis=0),
        )
        r.grad_qkv[token_rows, values] = grad_k.astype(jnp.bfloat16)
        r.grad_qkv[token_rows, pl.ds(start + 2048, 128)] = grad_v.astype(jnp.bfloat16)
        return carry

    def own_columns(group, part, which):
        return pl.ds(pl.multiple_of(part * 1024 + group * 512 + which * 256, 256), 256)

    def swap(group):
        return [
            pair(r.grad_qkv.at[:, own_columns(group, part, 1 - core)], r.grad_qkv2.at[group, part])
            for part in range(3)
        ]

    def late_products(group, swaps):
        for part in range(3):
            swaps[part].wait_recv()
            both = jnp.concatenate(
                [r.grad_qkv[:, own_columns(group, part, core)], r.grad_qkv2[group, part]], axis=0
            )
            for y, rows in enumerate(in_columns()):
                value = dot_nn(r.normed_t[rows, :], both)
                r.late_data[group, part, y] = value.astype(jnp.bfloat16).reshape(2, 2, 4, 16, 256)
            late[group].open(part, 0)

    for made in edge_here:
        made.wait_recv()
    lax.fori_loop(0, 8, attend_back, 0)
    swaps = swap(0)
    early.relays()
    lax.fori_loop(8, 12, attend_back, 0)
    late_products(0, swaps)
    lax.fori_loop(12, 16, attend_back, 0)
    swaps = swap(1)
    early.advance(0)
    late[0].relays()
    late_products(1, swaps)

    def back_normed(part):
        rows = slice(part * 256, part * 256 + 256)
        r.grad_normed[:, rows] = dot_nt(r.grad_qkv[...], r.w_qkv[rows, :])

    def finals(i):
        source = (r.early_final, r.late_final.at[0], r.late_final.at[1])[i]
        target = (r.early_other, r.late_other.at[0], r.late_other.at[1])[i]
        return push(source.at[1 - core], target, r.final_sems, (i,), place.partner)

    back_normed(0)
    early.advance(1)
    back_normed(1)
    late[0].advance(0)
    back_normed(2)
    late[1].relays()
    back_normed(3)
    early.advance(2)
    final_sums = [finals(0)]
    for block in range(4):
        rows = slice(block * 64, block * 64 + 64)
        normal_hat, inverse = normalised(r.tokens[rows, :])
        back = norm_back(r.grad_normed[rows, :], normal_hat, inverse)
        r.grad_tokens[rows, :] = (r.grad_s[rows, :] + back).astype(jnp.bfloat16)
    late[0].advance(1)
    late[1].advance(0)
    late[0].advance(2)
    final_sums.append(finals(1))
    late[1].advance(1)

    yours = pl.ds(pl.multiple_of((1 - core) * 512, 512), 512)
    r.grad_hidden_w[:, mine] = r.early_final[core, :, :512]
    r.grad_out_w[:, mine] = r.early_final[core, :, 512:1024]
    r.grad_readout[...] = r.early_final[core, :, 1024:]
    final_sums[0].wait_recv()
    r.grad_hidden_w[:, yours] = r.early_other[:, :512]
    r.grad_out_w[:, yours] = r.early_other[:, 512:1024]

    def place_late(group):
        for part in range(3):
            at = slice(part * 256, part * 256 + 256)
            r.grad_qkv_w[:, own_columns(group, part, core)] = r.late_final[group, core, :, at]
            r.grad_qkv_w[:, own_columns(group, part, 1 - core)] = r.late_other[group, :, at]

    late[1].advance(2)
    final_sums.append(finals(2))
    final_sums[1].wait_recv()
    place_late(0)
    final_sums[2].wait_recv()
    place_late(1)
    for made in sent_copies:
        made.wait_send()
    for other in others:
        give(r.sent, r.held, 0, other).wait_send()
        give(r.sent_back, r.held_back, 1, other).wait_send()
    for sums in (early, *late):
        sums.drain()


def handed_on(*refs):
    count = len(refs) // 2
    for source, target in zip(refs[:count], refs[count:]):
        target[...] = source[...]


def on_device(
    tokens, w_qkv, w_out, w_hidden, decoder_readout_matrix, edge_token, edge_weight, truth_state, area
):
    vmem, anywhere = pl.BlockSpec(memory_space=pltpu.VMEM), pl.BlockSpec(memory_space=pl.ANY)
    dma = pltpu.SemaphoreType.DMA

    def b16(*shape):
        return pltpu.VMEM(shape, jnp.bfloat16)

    def f32(*shape):
        return pltpu.VMEM(shape, jnp.float32)

    inputs = {
        "tokens": (tokens.reshape(256, 1024), vmem),
        "w_qkv_hbm": (w_qkv, anywhere),
        "w_out_hbm": (w_out, anywhere),
        "w_hidden_hbm": (w_hidden, anywhere),
        "readout": (decoder_readout_matrix, vmem),
        "edge_token": (edge_token.T, vmem),
        "edge_weight": (edge_weight.T, vmem),
        "truth_hbm": (truth_state, anywhere),
        "area": (area.reshape(8, 128), vmem),
    }
    outputs = {
        "grad_tokens": jax.ShapeDtypeStruct((256, 1024), jnp.bfloat16),
        "grad_qkv_w": jax.ShapeDtypeStruct((8, 3072), jnp.float32),
        "grad_out_w": jax.ShapeDtypeStruct((8, 1024), jnp.float32),
        "grad_hidden_w": jax.ShapeDtypeStruct((8, 1024), jnp.float32),
        "grad_readout": jax.ShapeDtypeStruct((8, 128), jnp.float32),
    }
    scratch = {
        "w_qkv": b16(1024, 3072), "w_out": b16(1024, 1024), "w_hidden": b16(1024, 1024), "truth": f32(128, 128),
        "area_here": f32(128, 128), "halo": b16(2, 128, 1024), "normed": b16(256, 1024), "normed_2": b16(256, 1024),
        "queries": b16(256, 1024), "kv": b16(2, 256, 2048), "window": f32(256, 256), "window_h": f32(256, 128), "scales": f32(256, 128), "scales_h": f32(256, 128),
        "queries_h": b16(2, 128, 1024), "att_h": b16(2, 128, 1024), "grad_att_h": b16(2, 128, 1024),
        "states_t": b16(1024, 512), "att_t": b16(1024, 512), "normed_t": b16(1024, 512),
        "probs": f32(16, 256, 256),
        "att": b16(256, 1024), "att_2": b16(256, 1024), "states": b16(256, 1024), "states_2": b16(256, 1024),
        "hidden": b16(2, 256, 1024), "edges": b16(4, 256, 256), "edges_t": b16(4, 256, 256),
        "active": b16(2, 4, 256, 1024), "slope": b16(2, 4, 256, 1024),
        "sent": b16(8, 2, 128, 128), "held": b16(8, 2, 128, 128),
        "sent_back": b16(8, 2, 128, 128), "held_back": b16(8, 2, 128, 128), "turned": f32(128, 1024),
        "gathered": f32(256, 1024), "gather_b": b16(256, 1024), "gather_2": b16(256, 512),
        "grad_s": f32(256, 1024), "grad_sb": b16(256, 1024), "grad_s2": b16(256, 512), "grad_att": b16(256, 1024),
        "readout_grad": b16(1024, 128), "readout_2": b16(1024, 128), "grad_qkv": b16(256, 3072),
        "grad_qkv2": b16(2, 3, 256, 256), "grad_normed": f32(256, 1024),
        "early_data": b16(3, *FULL, 16, 384), "late_data": b16(2, 3, *FULL, 16, 256),
        "early_final": f32(2, 8, 1152), "late_final": f32(2, 2, 8, 768),
        "early_other": f32(8, 1152), "late_other": f32(2, 8, 768),
        "load_sems": dma((6,)), "token_sems": dma((2, 2, 2)), "pair_sems": dma((2, 12)), "query_sems": dma((2, 2, 2)),
        "att_sems": dma((2, 2, 2)), "scale_sems": dma((2, 2, 2)), "grad_att_sems": dma((2, 2, 2)),
        "member_sems": dma((2, 2, 8)), "final_sems": dma((2, 3)),
    }
    names = [*inputs, *outputs, *scratch]
    results = pl.pallas_call(
        functools.partial(kernel, names),
        out_shape=tuple(outputs.values()),
        in_specs=[spec for _, spec in inputs.values()],
        out_specs=[vmem] * len(outputs),
        scratch_shapes=[*scratch.values(), *sum_scratch(384), *sum_scratch(256), *sum_scratch(256)],
        compiler_params=pltpu.CompilerParams(
            collective_id=0, has_side_effects=True, vmem_limit_bytes=62 * 2**20
        ),
    )(*[value for value, _ in inputs.values()])
    results = pl.pallas_call(
        handed_on,
        out_shape=tuple(outputs.values()),
        in_specs=[vmem] * len(outputs),
        out_specs=[vmem] * len(outputs),
    )(*results)
    return (results[0].reshape(tokens.shape), *results[1:])


def solution(mesh):
    in_specs = (
        P("member", "space", None),
        P(),
        P(),
        P(),
        P(),
        P("space", None),
        P("space", None),
        P("space", None),
        P("space"),
    )
    out_specs = (
        P("member", "space", None),
        P(("member", "space"), None),
        P(("member", "space"), None),
        P(("member", "space"), None),
        P(("member", "space"), None),
    )
    return jax.shard_map(
        on_device, mesh=mesh, in_specs=in_specs, out_specs=out_specs, check_vma=False
    )
```

```python
import functools
import math
import types

import jax
import jax.numpy as jnp
from jax import lax
from jax.experimental import pallas as pl
from jax.experimental.pallas import tpu as pltpu
from jax.sharding import PartitionSpec as P

EPS = 1e-05
ALPHA = 0.95
DELTA = 0.1


MESH = pl.DeviceIdType.MESH


class Place:
    def __init__(self):
        member, space = lax.axis_index("member"), lax.axis_index("space")
        self.member, self.space = member, space
        self.y, z_lo = member // 2, member % 2
        z_hi = space // 8
        self.x, self.core = (space // 2) % 4, space % 2
        self.z = z_hi * 2 + z_lo
        self.partner = (member, space + 1 - 2 * self.core)

    def ring(self, axis):
        return {"x": self.x, "y": self.y, "z": self.z}[axis]

    def device(self, axis, j, core=None):
        core = self.core if core is None else core
        if axis == "x":
            return (self.member, (self.space // 8) * 8 + j * 2 + core)
        if axis == "y":
            return (j * 2 + self.member % 2, (self.space // 2) * 2 + core)
        return ((self.member // 2) * 2 + j % 2, (j // 2) * 8 + ((self.space % 8) // 2) * 2 + core)

    def neighbours(self):
        found = []
        for axis in "xyz":
            i = self.ring(axis)
            found += [self.device(axis, (i + 1) % 4), self.device(axis, (i + 3) % 4)]
        return found


def entry_barrier(devices):
    barrier = pltpu.get_barrier_semaphore()
    for device in devices:
        pl.semaphore_signal(barrier, inc=1, device_id=device, device_id_type=MESH)
    pl.semaphore_wait(barrier, len(devices))


ORDERS = (
    (
        ("x", (4, 2, 2), lambda j, r: (*r, j)),
        ("y", (2, 2), lambda j, r: (j, *r)),
        ("z", (), lambda j, r: (j % 2, j // 2)),
    ),
    (
        ("y", (2, 2, 4), lambda j, r: (j, *r)),
        ("z", (4,), lambda j, r: (j % 2, j // 2, *r)),
        ("x", (), lambda j, r: (j,)),
    ),
    (
        ("z", (4, 4), lambda j, r: (r[0], j % 2, j // 2, r[1])),
        ("x", (4,), lambda j, r: (r[0], j)),
        ("y", (), lambda j, r: (j,)),
    ),
)
FULL = (4, 2, 2, 4)


def first_columns(width):
    return width // 128 // 2 * 128


def sum_scratch(width):
    low = first_columns(width)
    shapes = []
    for order in ORDERS:
        (_, rest, _), (_, rest_1, _), _ = order
        for columns in (width, width, low, width - low, width):
            shapes.append(pltpu.VMEM((*rest, 16, columns), jnp.bfloat16))
        shapes += [pltpu.VMEM((*rest_1, 16, width), jnp.bfloat16)] * 3
        shapes.append(pltpu.VMEM((*rest_1, 2, 8, width), jnp.float32))
        shapes.append(pltpu.VMEM((4, 2, 8, width), jnp.float32))
    return shapes + [pltpu.SemaphoreType.DMA((60,)), pltpu.SemaphoreType.DMA((60,))]


def over(dims, body):
    if len(dims) <= 1:
        body((slice(None),) * len(dims))
        return
    count = math.prod(dims[:-1])

    def step(n, carry):
        index = []
        for size in reversed(dims[:-1]):
            index.insert(0, lax.rem(n, size))
            n = n // size
        body((*index, slice(None)))
        return carry

    lax.fori_loop(0, count, step, 0)


class RingSum:
    def __init__(self, place, width, parts, scratch, finish):
        self.place, self.width, self.low = place, width, first_columns(width)
        scratch = list(scratch)
        self.recv, self.send = scratch.pop(), scratch.pop()
        self.slots = []
        for _ in range(3):
            self.slots.append([])
            for phase in range(3):
                count = (5, 4, 1)[phase]
                self.slots[-1].append(scratch[:count])
                scratch = scratch[count:]
        self.data = [[part] for part in parts]
        for part in range(3):
            self.data[part] += [self.slots[part][0][4], self.slots[part][1][3]]
        self.finish = finish
        self.copies = {}

    def copy(self, part, phase, message, source, target, device):
        sem = part * 20 + (0, 6, 12)[phase] + message
        made = pltpu.make_async_remote_copy(
            src_ref=source, dst_ref=target, send_sem=self.send.at[sem], recv_sem=self.recv.at[sem],
            device_id=device, device_id_type=MESH,
        )
        made.start()
        self.copies[part, phase, message] = made

    def view(self, part, phase, j, low):
        _, rest, at = ORDERS[part][phase]
        columns = pl.ds(0, self.low) if low else pl.ds(self.low, self.width - self.low)
        return self.data[part][phase].at[(*at(j, (slice(None),) * len(rest)), slice(None), columns)]

    def around(self, part, phase):
        axis = ORDERS[part][phase][0]
        i = self.place.ring(axis)
        right, left = (i + 1) % 4, (i + 3) % 4
        return i, right, left, (i + 2) % 4, self.place.device(axis, right), self.place.device(axis, left)

    def open(self, part, phase):
        _, right, left, opposite, to_right, to_left = self.around(part, phase)
        if phase == 2:
            axis, _, at = ORDERS[part][2]
            i, core = self.place.ring(axis), self.place.core
            data, slots = self.data[part][2], self.slots[part][2][0]
            for step in (2, 1, 3, 0):
                j = (i + step) % 4
                for message, to in ((2 * step, core), (2 * step + 1, 1 - core)):
                    if message:
                        self.copy(
                            part, 2, message, data.at[(*at(j, ()), to)], slots.at[i, core],
                            self.place.device(axis, j, to),
                        )
            slots[i, core] = data[(*at(i, ()), core)]
            return
        if phase:
            axis, rest, at = ORDERS[part][phase]
            across = self.place.device(axis, opposite)
            for message, (j, to) in enumerate(((opposite, across), (right, to_right), (left, to_left))):
                source = self.data[part][phase].at[(*at(j, (slice(None),) * len(rest)),)]
                self.copy(part, phase, message, source, self.slots[part][phase][message], to)
            return
        from_left, from_right, relay_left, relay_right = self.slots[part][phase][:4]
        low, high = pl.ds(0, self.low), pl.ds(self.low, self.width - self.low)
        self.copy(part, phase, 0, self.view(part, phase, opposite, True), relay_left, to_right)
        self.copy(part, phase, 1, self.view(part, phase, opposite, False), relay_right, to_left)
        self.copy(part, phase, 2, self.view(part, phase, right, False), from_left.at[..., high], to_right)
        self.copy(part, phase, 3, self.view(part, phase, left, True), from_right.at[..., low], to_left)

    def relay(self, part, phase):
        _, right, left, _, to_right, to_left = self.around(part, phase)
        _, rest, at = ORDERS[part][phase]
        from_left, from_right, relay_left, relay_right = self.slots[part][phase][:4]
        low, high = pl.ds(0, self.low), pl.ds(self.low, self.width - self.low)
        data = self.data[part][phase]
        for message, j, columns, relayed in ((0, right, low, relay_left), (1, left, high, relay_right)):
            self.copies[part, phase, message].wait_recv()

            def add(r, j=j, columns=columns, relayed=relayed):
                here = (*at(j, r), slice(None), columns)
                there = (*r, slice(None), slice(None))
                both = data[here].astype(jnp.float32) + relayed[there].astype(jnp.float32)
                data[here] = both.astype(jnp.bfloat16)

            over(rest, add)
            if message == 0:
                self.copy(part, phase, 4, self.view(part, phase, right, True), from_left.at[..., low], to_right)
            else:
                self.copy(part, phase, 5, self.view(part, phase, left, False), from_right.at[..., high], to_left)

    def close(self, part, phase):
        i = self.around(part, phase)[0]
        _, rest, at = ORDERS[part][phase]
        if phase == 2:
            for message in range(1, 8):
                self.copies[part, 2, message].wait_recv()
            slots = self.slots[part][2][0]
            self.finish(part, (slots[0] + slots[1]) + (slots[2] + slots[3]))
            return
        arrived = self.slots[part][phase][: 3 if phase else 2]
        data = self.data[part][phase]
        for message in (0, 1, 2) if phase else (2, 3, 4, 5):
            self.copies[part, phase, message].wait_recv()

        def add(r):
            there = (*r, slice(None), slice(None))
            total = data[(*at(i, r), slice(None), slice(None))].astype(jnp.float32)
            for slot in arrived:
                total = total + slot[there].astype(jnp.float32)
            if phase == 0:
                self.data[part][1][there] = total.astype(jnp.bfloat16)
            else:
                halves = total.reshape(*total.shape[:-2], 2, 8, self.width)
                self.data[part][2][(*r, slice(None), slice(None), slice(None))] = halves

        over(rest, add)

    def relays(self):
        for part in range(3):
            self.relay(part, 0)

    def advance(self, phase):
        for part in range(3):
            self.close(part, phase)
            if phase < 2:
                self.open(part, phase + 1)

    def drain(self):
        for made in self.copies.values():
            made.wait_send()


NT = (((1,), (1,)), ((), ()))
TN = (((0,), (0,)), ((), ()))


def dot_nn(a, b):
    return jnp.dot(a, b, preferred_element_type=jnp.float32)


def dot_nt(a, b):
    return lax.dot_general(a, b, NT, preferred_element_type=jnp.float32)


def dot_tn(a, b):
    return lax.dot_general(a, b, TN, preferred_element_type=jnp.float32)


def gelu_both(x):
    bell = jnp.exp(-0.5 * (x * x))
    t = 1.0 / (1.0 + (0.3275911 / math.sqrt(2.0)) * jnp.abs(x))
    poly = t * (
        0.5 * 0.254829592
        + t * (-0.5 * 0.284496736 + t * (0.5 * 1.421413741 + t * (-0.5 * 1.453152027 + t * (0.5 * 1.061405429))))
    )
    tail = poly * bell
    share = jnp.where(x >= 0.0, 1.0 - tail, tail)
    return x * share, share + x * (bell * (1.0 / math.sqrt(2.0 * math.pi)))


def norm_back(objective_derivative, normal_hat, inverse):
    first = jnp.mean(objective_derivative, axis=-1, keepdims=True)
    second = jnp.mean(objective_derivative * normal_hat, axis=-1, keepdims=True)
    return inverse * (objective_derivative - first - normal_hat * second)


def normalised(values):
    wide = values.astype(jnp.float32)
    centre = wide - jnp.mean(wide, axis=-1, keepdims=True)
    inverse = lax.rsqrt(jnp.mean(centre * centre, axis=-1, keepdims=True) + EPS)
    return centre * inverse, inverse


def in_columns(count=4):
    return [slice(part * 256, part * 256 + 256) for part in range(count)]


def kernel(names, *refs):
    r = types.SimpleNamespace(**dict(zip(names, refs)))
    ring_scratch = refs[len(names) :]
    place = Place()
    member, space, core = place.member, place.space, place.core

    loads = [
        pltpu.make_async_copy(
            r.w_qkv_hbm.at[:, pl.ds(part * 1024, 1024)], r.w_qkv.at[:, pl.ds(part * 1024, 1024)], r.load_sems.at[part]
        )
        for part in range(3)
    ]
    loads.append(pltpu.make_async_copy(r.w_out_hbm, r.w_out, r.load_sems.at[3]))
    loads.append(pltpu.make_async_copy(r.w_hidden_hbm, r.w_hidden, r.load_sems.at[4]))
    loads.append(pltpu.make_async_copy(
        r.truth_hbm.at[pl.ds(pl.multiple_of(member * 128, 128), 128), :], r.truth, r.load_sems.at[5]
    ))
    for load in loads:
        load.start()

    above, below = (member, lax.rem(space + 1, 16)), (member, lax.rem(space + 15, 16))
    home = member // 4
    nearby = [home * 4 + lax.rem(member + k, 4) for k in range(1, 4)]
    others = nearby + [(1 - home) * 4 + lax.rem(member + k, 4) for k in range(4)]
    entry_barrier([above, below, place.partner, *place.neighbours(), *[(other, space) for other in others]])
    sent_copies = []

    def push(source, target, sems, i, device):
        made = pltpu.make_async_remote_copy(
            src_ref=source, dst_ref=target, send_sem=sems.at[(0, *i)], recv_sem=sems.at[(1, *i)],
            device_id=device, device_id_type=MESH,
        )
        made.start()
        sent_copies.append(made)
        return made

    halo_tokens = []
    for m in range(2):
        halo_tokens.append(push(
            r.tokens.at[pl.ds(m * 128 + 64, 64)], r.halo.at[m, pl.ds(0, 64)], r.token_sems, (0, m), above
        ))
        halo_tokens.append(push(
            r.tokens.at[pl.ds(m * 128, 64)], r.halo.at[m, pl.ds(64, 64)], r.token_sems, (1, m), below
        ))

    pair_count = [0]

    def pair(source, target):
        pair_count[0] += 1
        return push(source, target, r.pair_sems, (pair_count[0] - 1,), place.partner)

    for block in range(4):
        rows = slice(block * 64, block * 64 + 64)
        r.normed[rows, :] = normalised(r.tokens[rows, :])[0].astype(jnp.bfloat16)
    normed_here = pair(r.normed, r.normed_2)
    loads[0].wait()
    for columns in in_columns():
        r.queries[:, columns] = dot_nn(r.normed[...], r.w_qkv[:, columns]).astype(jnp.bfloat16)

    def push_edges(source, target, sems):
        made = []
        for m in range(2):
            made.append(push(source.at[pl.ds(m * 128 + 64, 64)], target.at[m, pl.ds(0, 64)], sems, (0, m), above))
            made.append(push(source.at[pl.ds(m * 128, 64)], target.at[m, pl.ds(64, 64)], sems, (1, m), below))
        return made

    queries_here = push_edges(r.queries, r.queries_h, r.query_sems)
    for part in range(2):
        loads[1 + part].wait()
        for n in range(4):
            at = slice(part * 1024 + n * 256, part * 1024 + n * 256 + 256)
            value = dot_nn(r.normed[...], r.w_qkv[:, slice(at.start + 1024, at.stop + 1024)]).astype(jnp.bfloat16)
            r.kv[0, 0:128, at] = value[:128]
            r.kv[1, 0:128, at] = value[128:]

    row = lax.broadcasted_iota(jnp.int32, (256, 256), 0) % 128
    key = lax.broadcasted_iota(jnp.int32, (256, 256), 1)
    offset = jnp.where(key < 128, key, jnp.where(key < 192, key - 192, key - 64))
    token = space * 128 + offset
    inside = (offset >= row - 64) & (offset <= row + 64) & (token >= 0) & (token < 2048)
    r.window[...] = jnp.where(inside, 1.0, 0.0)
    row = lax.broadcasted_iota(jnp.int32, (256, 128), 0) % 128
    key = lax.broadcasted_iota(jnp.int32, (256, 128), 1)
    offset = jnp.where(row < 64, row - 64, row + 64)
    token = space * 128 + offset
    inside = (key >= offset - 64) & (key <= offset + 64) & (token >= 0) & (token < 2048)
    r.window_h[...] = jnp.where(inside, 1.0, 0.0)
    for group, columns in enumerate(in_columns()):
        local = r.edge_token[:, columns] - space * 128
        weight = r.edge_weight[:, columns]
        places = lax.broadcasted_iota(jnp.int32, (128, 256), 0)
        matrix = jnp.zeros((128, 256), jnp.float32)
        for slot in range(3):
            matrix = matrix + jnp.where(local[slot : slot + 1] == places, weight[slot : slot + 1], 0.0)
        high = matrix.astype(jnp.bfloat16)
        both = jnp.concatenate([high, (matrix - high.astype(jnp.float32)).astype(jnp.bfloat16)], axis=0)
        turned = both.T
        for i in range(2):
            owner = 2 * group + i
            for half in range(2):
                begin = i * 128 + half * 64
                r.edges[half, owner // 4, owner % 4 * 64 : owner % 4 * 64 + 64, :] = turned[begin : begin + 64]
    for half in range(2):
        for quad in range(2):
            r.edges_t[half, quad] = r.edges[half, quad].T

    def edge_keys(m):
        for made in halo_tokens[2 * m : 2 * m + 2]:
            made.wait_recv()
        edges_normed = normalised(r.halo[m])[0].astype(jnp.bfloat16)
        for n in range(8):
            at = slice(n * 256, n * 256 + 256)
            value = dot_nn(edges_normed, r.w_qkv[:, slice(at.start + 1024, at.stop + 1024)])
            r.kv[m, 128:256, at] = value.astype(jnp.bfloat16)

    first = lax.broadcasted_iota(jnp.int32, (128, 128), 1) < 64

    def stacked(value):
        zero = jnp.zeros_like(value)
        return jnp.concatenate([jnp.where(first, value, zero), jnp.where(first, zero, value)], axis=0)

    lane = lax.broadcasted_iota(jnp.int32, (256, 128), 1)
    r.scales[...] = jnp.zeros_like(r.scales)

    def attend(i, carry):
        m, n = i // 8, lax.rem(i, 8)
        start = pl.multiple_of(n * 128, 128)
        columns, values = pl.ds(start, 128), pl.ds(start + 1024, 128)
        token_rows = pl.ds(pl.multiple_of(m * 128, 128), 128)
        scores = dot_nt(stacked(r.queries[token_rows, columns]), r.kv[m, :, columns])
        expo = jnp.where(r.window[...] > 0.0, jnp.exp(scores * 0.125), 0.0)
        scale = 1.0 / jnp.sum(expo, axis=-1, keepdims=True)
        probs = expo * scale
        r.probs[i] = probs
        r.scales[...] = jnp.where(lane == i, scale, r.scales[...])
        result = dot_nn(probs.astype(jnp.bfloat16), r.kv[m, :, values])
        r.att[token_rows, columns] = jnp.where(first, result[:128], result[128:]).astype(jnp.bfloat16)
        return carry

    for m in range(2):
        edge_keys(m)
        lax.fori_loop(m * 8, m * 8 + 8, attend, 0, unroll=2)
    att_here = pair(r.att, r.att_2)
    edge_here = queries_here + push_edges(r.att, r.att_h, r.att_sems)
    for head in range(2):
        begin = head * 128
        edge_here.append(push(
            r.scales.at[pl.ds(begin + 64, 64)], r.scales_h.at[pl.ds(begin, 64)], r.scale_sems, (0, head), above
        ))
        edge_here.append(push(
            r.scales.at[pl.ds(begin, 64)], r.scales_h.at[pl.ds(begin + 64, 64)], r.scale_sems, (1, head), below
        ))
    loads[3].wait()
    for columns in in_columns():
        value = r.tokens[:, columns].astype(jnp.float32) + dot_nn(r.att[...], r.w_out[:, columns])
        r.states[:, columns] = value.astype(jnp.bfloat16)
    states_here = pair(r.states, r.states_2)
    loads[4].wait()
    for columns in in_columns():
        value = dot_nn(r.states[...], r.w_hidden[:, columns]).astype(jnp.bfloat16)
        for m in range(2):
            r.hidden[m, 0:128, columns] = value[m * 128 : m * 128 + 128]
            r.hidden[m, 128:256, columns] = value[m * 128 : m * 128 + 128]

    def give(source, target, i, half, to):
        rows = pl.ds(half * 64, 64)
        return pltpu.make_async_remote_copy(
            src_ref=source.at[to, :, rows], dst_ref=target.at[member, :, rows],
            send_sem=r.member_sems.at[i, half, 0, to], recv_sem=r.member_sems.at[i, half, 1, member],
            device_id=(to, space), device_id_type=MESH,
        )

    def take(target, i, half, source):
        rows = pl.ds(half * 64, 64)
        return pltpu.make_async_remote_copy(
            src_ref=target.at[source, :, rows], dst_ref=target.at[source, :, rows],
            send_sem=r.member_sems.at[i, half, 0, source], recv_sem=r.member_sems.at[i, half, 1, source],
            device_id=(source, space), device_id_type=MESH,
        )

    for half in range(2):
        rows = slice(half * 64, half * 64 + 64)
        for n in range(2):
            quad = 1 - home if n == 0 else home

            def forward(b, carry, half=half, quad=quad, rows=rows):
                forecast = jnp.zeros((256, 128), jnp.float32)
                for columns in in_columns():
                    value, derivative = gelu_both(dot_nn(r.edges[half, quad], r.hidden[b, :, columns]))
                    value = value.astype(jnp.bfloat16)
                    r.active[b, half, quad, :, columns] = value
                    r.slope[b, half, quad, :, columns] = derivative.astype(jnp.bfloat16)
                    forecast = forecast + dot_nn(value, r.readout[columns, :])
                for i in range(4):
                    r.sent[4 * quad + i, b, rows] = forecast[i * 64 : i * 64 + 64].astype(jnp.bfloat16)
                return carry

            lax.fori_loop(0, 2, forward, 0)
            for to in others[3:] if n == 0 else nearby:
                give(r.sent, r.held, 0, half, to).start()
        r.held[member, :, rows] = r.sent[member, :, rows]
    r.area_here[...] = jnp.broadcast_to(r.area[pl.ds(member, 1), :], (128, 128)).T
    loads[5].wait()

    def turn(source, target, begin):
        for columns in in_columns():
            target[columns, begin : begin + 256] = source[:, columns].T

    turn(r.states, r.states_t, 0)
    states_here.wait_recv()
    turn(r.states_2, r.states_t, 256)
    turn(r.att, r.att_t, 0)

    multiplier = math.sqrt(16 / 16384)
    eps_fair = (1.0 - ALPHA) / 16

    def score(block, carry):
        rows = pl.ds(pl.multiple_of(block * 16, 16), 16)
        whole = [r.held[m // 2, m % 2, rows, :].astype(jnp.float32) for m in range(16)]
        truth, area = r.truth[rows, :], r.area_here[rows, :]
        found = [[] for _ in range(16)]
        for half in (slice(0, 8), slice(8, 16)):
            values = [value[half] for value in whole]
            spread = [None] * 16
            for j in range(16):
                for k in range(j + 1, 16):
                    d = values[j] - values[k]
                    s = d * lax.rsqrt(d * d + DELTA * DELTA)
                    spread[j] = s if spread[j] is None else spread[j] + s
                    spread[k] = -s if spread[k] is None else spread[k] - s
            for j in range(16):
                d = values[j] - truth[half]
                s = d * lax.rsqrt(d * d + DELTA * DELTA)
                found[j].append(
                    multiplier * area[half] * (s / 16 - (1.0 - eps_fair) / (16 * 15) * spread[j])
                )
        for j in range(16):
            r.sent_back[j // 2, j % 2, rows, :] = jnp.concatenate(found[j], axis=0).astype(jnp.bfloat16)
        return carry

    for half in range(2):
        rows = slice(half * 64, half * 64 + 64)
        for other in others:
            take(r.held, 0, half, other).wait_recv()
        lax.fori_loop(half * 4, half * 4 + 4, score, 0)
        for other in others:
            give(r.sent_back, r.held_back, 1, half, other).start()
        r.held_back[member, :, rows] = r.sent_back[member, :, rows]
        if half == 0:
            att_here.wait_recv()
            turn(r.att_2, r.att_t, 256)
            turn(r.normed, r.normed_t, 0)
    normed_here.wait_recv()
    turn(r.normed_2, r.normed_t, 256)
    r.gathered[...] = jnp.zeros_like(r.gathered)
    r.turned[...] = jnp.zeros_like(r.turned)
    for half, n in ((0, 0), (0, 1), (1, 0), (1, 1)):
        quad = home if n == 0 else 1 - home
        for other in nearby if n == 0 else others[3:]:
            take(r.held_back, 1, half, other).wait_recv()

        def backward(b, half=half, quad=quad):
            rows = slice(half * 64, half * 64 + 64)
            grad = jnp.concatenate([r.held_back[4 * quad + i, b, rows] for i in range(4)], axis=0)
            grad_t = grad.T
            token_rows = pl.ds(b * 128, 128)
            for columns in in_columns():
                hidden = dot_nt(grad, r.readout[columns, :])
                grad_pre = (hidden * r.slope[b, half, quad, :, columns].astype(jnp.float32)).astype(jnp.bfloat16)
                both = dot_nn(r.edges_t[half, quad], grad_pre)
                r.gathered[token_rows, columns] += both[:128] + both[128:]
                r.turned[:, columns] += dot_nn(grad_t, r.active[b, half, quad, :, columns])

        for b in range(2):
            backward(b)

    mine = pl.ds(pl.multiple_of(core * 512, 512), 512)
    other_half = pl.ds(pl.multiple_of((1 - core) * 512, 512), 512)
    high = r.gathered[...].astype(jnp.bfloat16)
    r.gather_b[...] = high
    gather_here = pair(r.gather_b.at[:, other_half], r.gather_2)
    r.readout_grad[...] = r.turned[...].T.astype(jnp.bfloat16)
    readout_here = pair(r.readout_grad, r.readout_2)
    low = (r.gathered[...] - high.astype(jnp.float32)).astype(jnp.bfloat16)
    for rows in in_columns():
        weights = r.w_hidden[rows, :]
        value = dot_nt(high, weights) + dot_nt(low, weights)
        r.grad_s[:, rows] = value
        r.grad_sb[:, rows] = value.astype(jnp.bfloat16)
    grad_s_here = pair(r.grad_sb.at[:, other_half], r.grad_s2)

    for rows in in_columns():
        r.grad_att[:, rows] = dot_nt(r.grad_sb[...], r.w_out[rows, :]).astype(jnp.bfloat16)
    edge_here += push_edges(r.grad_att, r.grad_att_h, r.grad_att_sems)

    def early_tile(tile, y, value):
        columns = slice(tile % 3 * 128, tile % 3 * 128 + 128)
        r.early_data[tile // 3, y, :, :, :, :, columns] = value.astype(jnp.bfloat16).reshape(2, 2, 4, 16, 128)

    gather_here.wait_recv()
    both = jnp.concatenate([r.gather_b[:, mine], r.gather_2[...]], axis=0)
    for y, rows in enumerate(in_columns()):
        value = dot_nn(r.states_t[rows, :], both)
        for tile in range(4):
            early_tile(tile, y, value[:, tile * 128 : tile * 128 + 128])
    readout_here.wait_recv()
    for y, rows in enumerate(in_columns()):
        early_tile(8, y, r.readout_grad[rows, :].astype(jnp.float32) + r.readout_2[rows, :].astype(jnp.float32))
    grad_s_here.wait_recv()
    both = jnp.concatenate([r.grad_sb[:, mine], r.grad_s2[...]], axis=0)
    for y, rows in enumerate(in_columns()):
        value = dot_nn(r.att_t[rows, :], both)
        for tile in range(4):
            early_tile(4 + tile, y, value[:, tile * 128 : tile * 128 + 128])

    def ring_sum(data, final, width, scratch):
        def finish(part, total):
            final[:, :, part * width : part * width + width] = total

        return RingSum(place, width, [data.at[part] for part in range(3)], scratch, finish)

    third = len(ring_scratch) // 3
    early = ring_sum(r.early_data, r.early_final, 384, ring_scratch[:third])
    late = [
        ring_sum(r.late_data.at[g], r.late_final.at[g], 256, ring_scratch[third * (1 + g) : third * (2 + g)])
        for g in range(2)
    ]
    for part in range(3):
        early.open(part, 0)

    def attend_back(i, carry):
        n, m = i // 2, lax.rem(i, 2)
        start = pl.multiple_of(n * 128, 128)
        columns, values = pl.ds(start, 128), pl.ds(start + 1024, 128)
        token_rows = pl.ds(pl.multiple_of(m * 128, 128), 128)
        turn_index = m * 8 + n
        queries = stacked(r.queries[token_rows, columns])
        grads = stacked(r.grad_att[token_rows, columns])
        att = r.att[token_rows, columns].astype(jnp.float32)
        inner = jnp.sum(grads.astype(jnp.float32) * jnp.concatenate([att, att], axis=0), axis=-1, keepdims=True)
        probs = r.probs[turn_index]
        dprob = dot_nt(grads, r.kv[m, :, values])
        dscore = (probs * (dprob - inner) * 0.125).astype(jnp.bfloat16)
        grad_q = dot_nn(dscore, r.kv[m, :, columns])
        r.grad_qkv[token_rows, columns] = jnp.where(first, grad_q[:128], grad_q[128:]).astype(jnp.bfloat16)

        local = pl.multiple_of(lax.rem(n, 4) * 128, 128)
        r.gathered[token_rows, pl.ds(local, 128)] = dot_tn(dscore[:, :128], queries)
        r.gathered[token_rows, pl.ds(local + 512, 128)] = dot_tn(probs[:, :128].astype(jnp.bfloat16), grads)
        return carry

    def attend_back_edges(i, carry):
        n, m = i // 2, lax.rem(i, 2)
        start = pl.multiple_of(n * 128, 128)
        columns, values = pl.ds(start, 128), pl.ds(start + 1024, 128)
        token_rows = pl.ds(pl.multiple_of(m * 128, 128), 128)
        queries_h = stacked(r.queries_h[m, :, columns])
        grads_h = stacked(r.grad_att_h[m, :, columns])
        att = r.att_h[m, :, columns].astype(jnp.float32)
        inner = jnp.sum(grads_h.astype(jnp.float32) * jnp.concatenate([att, att], axis=0), axis=-1, keepdims=True)
        scale = jnp.sum(jnp.where(lane == m * 8 + n, r.scales_h[...], 0.0), axis=-1, keepdims=True)
        scores = dot_nt(queries_h, r.kv[m, 0:128, columns])
        probs_h = jnp.where(r.window_h[...] > 0.0, jnp.exp(scores * 0.125) * scale, 0.0)
        dprob = dot_nt(grads_h, r.kv[m, 0:128, values])
        dscore_h = (probs_h * (dprob - inner) * 0.125).astype(jnp.bfloat16)
        local = pl.multiple_of(lax.rem(n, 4) * 128, 128)
        grad_k = r.gathered[token_rows, pl.ds(local, 128)] + dot_tn(dscore_h, queries_h)
        grad_v = r.gathered[token_rows, pl.ds(local + 512, 128)] + dot_tn(probs_h.astype(jnp.bfloat16), grads_h)
        r.grad_qkv[token_rows, values] = grad_k.astype(jnp.bfloat16)
        r.grad_qkv[token_rows, pl.ds(start + 2048, 128)] = grad_v.astype(jnp.bfloat16)
        return carry

    def own_columns(group, part, which):
        return pl.ds(pl.multiple_of(part * 1024 + group * 512 + which * 256, 256), 256)

    def swap(group):
        return [
            pair(r.grad_qkv.at[:, own_columns(group, part, 1 - core)], r.grad_qkv2.at[group, part])
            for part in range(3)
        ]

    def late_products(group, swaps):
        for part in range(3):
            swaps[part].wait_recv()
            both = jnp.concatenate(
                [r.grad_qkv[:, own_columns(group, part, core)], r.grad_qkv2[group, part]], axis=0
            )
            for y, rows in enumerate(in_columns()):
                value = dot_nn(r.normed_t[rows, :], both)
                r.late_data[group, part, y] = value.astype(jnp.bfloat16).reshape(2, 2, 4, 16, 256)
            late[group].open(part, 0)

    lax.fori_loop(0, 8, attend_back, 0, unroll=2)
    for made in edge_here:
        made.wait_recv()
    lax.fori_loop(0, 8, attend_back_edges, 0, unroll=2)
    swaps = swap(0)
    early.relays()
    lax.fori_loop(8, 16, attend_back, 0, unroll=2)
    late_products(0, swaps)
    lax.fori_loop(8, 16, attend_back_edges, 0, unroll=2)
    swaps = swap(1)
    early.advance(0)
    late[0].relays()
    late_products(1, swaps)

    def back_normed(part):
        rows = slice(part * 256, part * 256 + 256)
        r.gathered[:, rows] = dot_nt(r.grad_qkv[...], r.w_qkv[rows, :])

    back_normed(0)
    early.advance(1)
    back_normed(1)
    late[0].advance(0)
    back_normed(2)
    late[1].relays()
    back_normed(3)
    early.advance(2)
    for block in range(4):
        rows = slice(block * 64, block * 64 + 64)
        normal_hat, inverse = normalised(r.tokens[rows, :])
        back = norm_back(r.gathered[rows, :], normal_hat, inverse)
        r.grad_tokens[rows, :] = (r.grad_s[rows, :] + back).astype(jnp.bfloat16)
    late[0].advance(1)
    late[1].advance(0)
    late[0].advance(2)
    late[1].advance(1)

    for half in range(2):
        at = slice(half * 512, half * 512 + 512)
        r.grad_hidden_w[:, at] = r.early_final[half, :, :512]
        r.grad_out_w[:, at] = r.early_final[half, :, 512:1024]
    r.grad_readout[...] = r.early_final[0, :, 1024:]
    late[1].advance(2)
    for group in range(2):
        for part in range(3):
            for half in range(2):
                begin = part * 1024 + group * 512 + half * 256
                r.grad_qkv_w[:, begin : begin + 256] = r.late_final[group, half, :, part * 256 : part * 256 + 256]
    for made in sent_copies:
        made.wait_send()
    for other in others:
        for half in range(2):
            give(r.sent, r.held, 0, half, other).wait_send()
            give(r.sent_back, r.held_back, 1, half, other).wait_send()
    for sums in (early, *late):
        sums.drain()


def handed_on(*refs):
    count = len(refs) // 2
    for source, target in zip(refs[:count], refs[count:]):
        target[...] = source[...]


def on_device(
    tokens, w_qkv, w_out, w_hidden, decoder_readout_matrix, edge_token, edge_weight, truth_state, area
):
    vmem, anywhere = pl.BlockSpec(memory_space=pltpu.VMEM), pl.BlockSpec(memory_space=pl.ANY)
    dma = pltpu.SemaphoreType.DMA

    def b16(*shape):
        return pltpu.VMEM(shape, jnp.bfloat16)

    def f32(*shape):
        return pltpu.VMEM(shape, jnp.float32)

    inputs = {
        "tokens": (tokens.reshape(256, 1024), vmem),
        "w_qkv_hbm": (w_qkv, anywhere),
        "w_out_hbm": (w_out, anywhere),
        "w_hidden_hbm": (w_hidden, anywhere),
        "readout": (decoder_readout_matrix, vmem),
        "edge_token": (edge_token.T, vmem),
        "edge_weight": (edge_weight.T, vmem),
        "truth_hbm": (truth_state, anywhere),
        "area": (area.reshape(8, 128), vmem),
    }
    outputs = {
        "grad_tokens": jax.ShapeDtypeStruct((256, 1024), jnp.bfloat16),
        "grad_qkv_w": jax.ShapeDtypeStruct((8, 3072), jnp.float32),
        "grad_out_w": jax.ShapeDtypeStruct((8, 1024), jnp.float32),
        "grad_hidden_w": jax.ShapeDtypeStruct((8, 1024), jnp.float32),
        "grad_readout": jax.ShapeDtypeStruct((8, 128), jnp.float32),
    }
    scratch = {
        "w_qkv": b16(1024, 3072), "w_out": b16(1024, 1024), "w_hidden": b16(1024, 1024), "truth": f32(128, 128),
        "area_here": f32(128, 128), "halo": b16(2, 128, 1024), "normed": b16(256, 1024), "normed_2": b16(256, 1024),
        "queries": b16(256, 1024), "kv": b16(2, 256, 2048), "window": f32(256, 256), "window_h": f32(256, 128), "scales": f32(256, 128), "scales_h": f32(256, 128),
        "queries_h": b16(2, 128, 1024), "att_h": b16(2, 128, 1024), "grad_att_h": b16(2, 128, 1024),
        "states_t": b16(1024, 512), "att_t": b16(1024, 512), "normed_t": b16(1024, 512),
        "probs": f32(16, 256, 256),
        "att": b16(256, 1024), "att_2": b16(256, 1024), "states": b16(256, 1024), "states_2": b16(256, 1024),
        "hidden": b16(2, 256, 1024), "edges": b16(2, 2, 256, 256), "edges_t": b16(2, 2, 256, 256),
        "active": b16(2, 2, 2, 256, 1024), "slope": b16(2, 2, 2, 256, 1024),
        "sent": b16(8, 2, 128, 128), "held": b16(8, 2, 128, 128),
        "sent_back": b16(8, 2, 128, 128), "held_back": b16(8, 2, 128, 128), "turned": f32(128, 1024),
        "gathered": f32(256, 1024), "gather_b": b16(256, 1024), "gather_2": b16(256, 512),
        "grad_s": f32(256, 1024), "grad_sb": b16(256, 1024), "grad_s2": b16(256, 512), "grad_att": b16(256, 1024),
        "readout_grad": b16(1024, 128), "readout_2": b16(1024, 128), "grad_qkv": b16(256, 3072),
        "grad_qkv2": b16(2, 3, 256, 256),
        "early_data": b16(3, *FULL, 16, 384), "late_data": b16(2, 3, *FULL, 16, 256),
        "early_final": f32(2, 8, 1152), "late_final": f32(2, 2, 8, 768),
        "load_sems": dma((6,)), "token_sems": dma((2, 2, 2)), "pair_sems": dma((2, 12)), "query_sems": dma((2, 2, 2)),
        "att_sems": dma((2, 2, 2)), "scale_sems": dma((2, 2, 2)), "grad_att_sems": dma((2, 2, 2)),
        "member_sems": dma((2, 2, 2, 8)),
    }
    names = [*inputs, *outputs, *scratch]
    results = pl.pallas_call(
        functools.partial(kernel, names),
        out_shape=tuple(outputs.values()),
        in_specs=[spec for _, spec in inputs.values()],
        out_specs=[vmem] * len(outputs),
        scratch_shapes=[*scratch.values(), *sum_scratch(384), *sum_scratch(256), *sum_scratch(256)],
        compiler_params=pltpu.CompilerParams(
            collective_id=0, has_side_effects=True, vmem_limit_bytes=62 * 2**20
        ),
    )(*[value for value, _ in inputs.values()])
    results = pl.pallas_call(
        handed_on,
        out_shape=tuple(outputs.values()),
        in_specs=[vmem] * len(outputs),
        out_specs=[vmem] * len(outputs),
    )(*results)
    return (results[0].reshape(tokens.shape), *results[1:])


def solution(mesh):
    in_specs = (
        P("member", "space", None),
        P(),
        P(),
        P(),
        P(),
        P("space", None),
        P("space", None),
        P("space", None),
        P("space"),
    )
    out_specs = (
        P("member", "space", None),
        P(("member", "space"), None),
        P(("member", "space"), None),
        P(("member", "space"), None),
        P(("member", "space"), None),
    )
    return jax.shard_map(
        on_device, mesh=mesh, in_specs=in_specs, out_specs=out_specs, check_vma=False
    )
```

```python
import functools
import math
import types

import jax
import jax.numpy as jnp
from jax import lax
from jax.experimental import pallas as pl
from jax.experimental.pallas import tpu as pltpu
from jax.sharding import PartitionSpec as P

EPS = 1e-05
ALPHA = 0.95
DELTA = 0.1


MESH = pl.DeviceIdType.MESH


class Place:
    def __init__(self):
        member, space = lax.axis_index("member"), lax.axis_index("space")
        self.member, self.space = member, space
        self.y, z_lo = member // 2, member % 2
        z_hi = space // 8
        self.x, self.core = (space // 2) % 4, space % 2
        self.z = z_hi * 2 + z_lo
        self.partner = (member, space + 1 - 2 * self.core)

    def ring(self, axis):
        return {"x": self.x, "y": self.y, "z": self.z}[axis]

    def device(self, axis, j, core=None):
        core = self.core if core is None else core
        if axis == "x":
            return (self.member, (self.space // 8) * 8 + j * 2 + core)
        if axis == "y":
            return (j * 2 + self.member % 2, (self.space // 2) * 2 + core)
        return ((self.member // 2) * 2 + j % 2, (j // 2) * 8 + ((self.space % 8) // 2) * 2 + core)

    def neighbours(self):
        found = []
        for axis in "xyz":
            i = self.ring(axis)
            found += [self.device(axis, (i + 1) % 4), self.device(axis, (i + 3) % 4)]
        return found


def entry_barrier(devices):
    barrier = pltpu.get_barrier_semaphore()
    for device in devices:
        pl.semaphore_signal(barrier, inc=1, device_id=device, device_id_type=MESH)
    pl.semaphore_wait(barrier, len(devices))


ORDERS = (
    (
        ("x", (4, 2, 2), lambda j, r: (*r, j)),
        ("y", (2, 2), lambda j, r: (j, *r)),
        ("z", (), lambda j, r: (j % 2, j // 2)),
    ),
    (
        ("y", (2, 2, 4), lambda j, r: (j, *r)),
        ("z", (4,), lambda j, r: (j % 2, j // 2, *r)),
        ("x", (), lambda j, r: (j,)),
    ),
    (
        ("z", (4, 4), lambda j, r: (r[0], j % 2, j // 2, r[1])),
        ("x", (4,), lambda j, r: (r[0], j)),
        ("y", (), lambda j, r: (j,)),
    ),
)
FULL = (4, 2, 2, 4)


def first_columns(width):
    return width // 128 // 2 * 128


def sum_scratch(width):
    low = first_columns(width)
    shapes = []
    for order in ORDERS:
        (_, rest, _), (_, rest_1, _), _ = order
        for columns in (width, width, low, width - low, width):
            shapes.append(pltpu.VMEM((*rest, 16, columns), jnp.bfloat16))
        shapes += [pltpu.VMEM((*rest_1, 16, width), jnp.bfloat16)] * 3
        shapes.append(pltpu.VMEM((*rest_1, 2, 8, width), jnp.float32))
        shapes.append(pltpu.VMEM((4, 2, 8, width), jnp.float32))
    return shapes + [pltpu.SemaphoreType.DMA((60,)), pltpu.SemaphoreType.DMA((60,))]


def over(dims, body):
    if len(dims) <= 1:
        body((slice(None),) * len(dims))
        return
    count = math.prod(dims[:-1])

    def step(n, carry):
        index = []
        for size in reversed(dims[:-1]):
            index.insert(0, lax.rem(n, size))
            n = n // size
        body((*index, slice(None)))
        return carry

    lax.fori_loop(0, count, step, 0)


class RingSum:
    def __init__(self, place, width, parts, scratch, finish):
        self.place, self.width, self.low = place, width, first_columns(width)
        scratch = list(scratch)
        self.recv, self.send = scratch.pop(), scratch.pop()
        self.slots = []
        for _ in range(3):
            self.slots.append([])
            for phase in range(3):
                count = (5, 4, 1)[phase]
                self.slots[-1].append(scratch[:count])
                scratch = scratch[count:]
        self.data = [[part] for part in parts]
        for part in range(3):
            self.data[part] += [self.slots[part][0][4], self.slots[part][1][3]]
        self.finish = finish
        self.copies = {}

    def copy(self, part, phase, message, source, target, device):
        sem = part * 20 + (0, 6, 12)[phase] + message
        made = pltpu.make_async_remote_copy(
            src_ref=source, dst_ref=target, send_sem=self.send.at[sem], recv_sem=self.recv.at[sem],
            device_id=device, device_id_type=MESH,
        )
        made.start()
        self.copies[part, phase, message] = made

    def view(self, part, phase, j, low):
        _, rest, at = ORDERS[part][phase]
        columns = pl.ds(0, self.low) if low else pl.ds(self.low, self.width - self.low)
        return self.data[part][phase].at[(*at(j, (slice(None),) * len(rest)), slice(None), columns)]

    def around(self, part, phase):
        axis = ORDERS[part][phase][0]
        i = self.place.ring(axis)
        right, left = (i + 1) % 4, (i + 3) % 4
        return i, right, left, (i + 2) % 4, self.place.device(axis, right), self.place.device(axis, left)

    def open(self, part, phase):
        _, right, left, opposite, to_right, to_left = self.around(part, phase)
        if phase == 2:
            axis, _, at = ORDERS[part][2]
            i, core = self.place.ring(axis), self.place.core
            data, slots = self.data[part][2], self.slots[part][2][0]
            for step in (2, 1, 3, 0):
                j = (i + step) % 4
                for message, to in ((2 * step, core), (2 * step + 1, 1 - core)):
                    if message:
                        self.copy(
                            part, 2, message, data.at[(*at(j, ()), to)], slots.at[i, core],
                            self.place.device(axis, j, to),
                        )
            slots[i, core] = data[(*at(i, ()), core)]
            return
        if phase:
            axis, rest, at = ORDERS[part][phase]
            across = self.place.device(axis, opposite)
            for message, (j, to) in enumerate(((opposite, across), (right, to_right), (left, to_left))):
                source = self.data[part][phase].at[(*at(j, (slice(None),) * len(rest)),)]
                self.copy(part, phase, message, source, self.slots[part][phase][message], to)
            return
        from_left, from_right, relay_left, relay_right = self.slots[part][phase][:4]
        low, high = pl.ds(0, self.low), pl.ds(self.low, self.width - self.low)
        self.copy(part, phase, 0, self.view(part, phase, opposite, True), relay_left, to_right)
        self.copy(part, phase, 1, self.view(part, phase, opposite, False), relay_right, to_left)
        self.copy(part, phase, 2, self.view(part, phase, right, False), from_left.at[..., high], to_right)
        self.copy(part, phase, 3, self.view(part, phase, left, True), from_right.at[..., low], to_left)

    def relay(self, part, phase):
        _, right, left, _, to_right, to_left = self.around(part, phase)
        _, rest, at = ORDERS[part][phase]
        from_left, from_right, relay_left, relay_right = self.slots[part][phase][:4]
        low, high = pl.ds(0, self.low), pl.ds(self.low, self.width - self.low)
        data = self.data[part][phase]
        for message, j, columns, relayed in ((0, right, low, relay_left), (1, left, high, relay_right)):
            self.copies[part, phase, message].wait_recv()

            def add(r, j=j, columns=columns, relayed=relayed):
                here = (*at(j, r), slice(None), columns)
                there = (*r, slice(None), slice(None))
                both = data[here].astype(jnp.float32) + relayed[there].astype(jnp.float32)
                data[here] = both.astype(jnp.bfloat16)

            over(rest, add)
            if message == 0:
                self.copy(part, phase, 4, self.view(part, phase, right, True), from_left.at[..., low], to_right)
            else:
                self.copy(part, phase, 5, self.view(part, phase, left, False), from_right.at[..., high], to_left)

    def close(self, part, phase):
        i = self.around(part, phase)[0]
        _, rest, at = ORDERS[part][phase]
        if phase == 2:
            for message in range(1, 8):
                self.copies[part, 2, message].wait_recv()
            slots = self.slots[part][2][0]
            self.finish(part, (slots[0] + slots[1]) + (slots[2] + slots[3]))
            return
        arrived = self.slots[part][phase][: 3 if phase else 2]
        data = self.data[part][phase]
        for message in (0, 1, 2) if phase else (2, 3, 4, 5):
            self.copies[part, phase, message].wait_recv()

        def add(r):
            there = (*r, slice(None), slice(None))
            total = data[(*at(i, r), slice(None), slice(None))].astype(jnp.float32)
            for slot in arrived:
                total = total + slot[there].astype(jnp.float32)
            if phase == 0:
                self.data[part][1][there] = total.astype(jnp.bfloat16)
            else:
                halves = total.reshape(*total.shape[:-2], 2, 8, self.width)
                self.data[part][2][(*r, slice(None), slice(None), slice(None))] = halves

        over(rest, add)

    def relays(self):
        for part in range(3):
            self.relay(part, 0)

    def advance(self, phase):
        for part in range(3):
            self.close(part, phase)
            if phase < 2:
                self.open(part, phase + 1)

    def drain(self):
        for made in self.copies.values():
            made.wait_send()


NT = (((1,), (1,)), ((), ()))
TN = (((0,), (0,)), ((), ()))


def dot_nn(a, b):
    return jnp.dot(a, b, preferred_element_type=jnp.float32)


def dot_nt(a, b):
    return lax.dot_general(a, b, NT, preferred_element_type=jnp.float32)


def dot_tn(a, b):
    return lax.dot_general(a, b, TN, preferred_element_type=jnp.float32)


def gelu_both(x):
    bell = jnp.exp(-0.5 * (x * x))
    t = 1.0 / (1.0 + (0.3275911 / math.sqrt(2.0)) * jnp.abs(x))
    poly = t * (
        0.5 * 0.254829592
        + t * (-0.5 * 0.284496736 + t * (0.5 * 1.421413741 + t * (-0.5 * 1.453152027 + t * (0.5 * 1.061405429))))
    )
    tail = poly * bell
    share = jnp.where(x >= 0.0, 1.0 - tail, tail)
    return x * share, share + x * (bell * (1.0 / math.sqrt(2.0 * math.pi)))


def norm_back(objective_derivative, normal_hat, inverse):
    first = jnp.mean(objective_derivative, axis=-1, keepdims=True)
    second = jnp.mean(objective_derivative * normal_hat, axis=-1, keepdims=True)
    return inverse * (objective_derivative - first - normal_hat * second)


def normalised(values):
    wide = values.astype(jnp.float32)
    centre = wide - jnp.mean(wide, axis=-1, keepdims=True)
    inverse = lax.rsqrt(jnp.mean(centre * centre, axis=-1, keepdims=True) + EPS)
    return centre * inverse, inverse


def in_columns(count=4):
    return [slice(part * 256, part * 256 + 256) for part in range(count)]


def kernel(names, *refs):
    r = types.SimpleNamespace(**dict(zip(names, refs)))
    ring_scratch = refs[len(names) :]
    place = Place()
    member, space, core = place.member, place.space, place.core

    loads = [
        pltpu.make_async_copy(
            r.w_qkv_hbm.at[:, pl.ds(part * 1024, 1024)], r.w_qkv.at[:, pl.ds(part * 1024, 1024)], r.load_sems.at[part]
        )
        for part in range(3)
    ]
    loads.append(pltpu.make_async_copy(r.w_out_hbm, r.w_out, r.load_sems.at[3]))
    loads.append(pltpu.make_async_copy(r.w_hidden_hbm, r.w_hidden, r.load_sems.at[4]))
    loads.append(pltpu.make_async_copy(
        r.truth_hbm.at[pl.ds(pl.multiple_of(member * 128, 128), 128), :], r.truth, r.load_sems.at[5]
    ))
    for load in loads:
        load.start()

    above, below = (member, lax.rem(space + 1, 16)), (member, lax.rem(space + 15, 16))
    home = member // 4
    nearby = [home * 4 + lax.rem(member + k, 4) for k in range(1, 4)]
    others = nearby + [(1 - home) * 4 + lax.rem(member + k, 4) for k in range(4)]
    entry_barrier([above, below, place.partner, *place.neighbours(), *[(other, space) for other in others]])
    sent_copies = []

    def push(source, target, sems, i, device):
        made = pltpu.make_async_remote_copy(
            src_ref=source, dst_ref=target, send_sem=sems.at[(0, *i)], recv_sem=sems.at[(1, *i)],
            device_id=device, device_id_type=MESH,
        )
        made.start()
        sent_copies.append(made)
        return made

    halo_tokens = []
    for m in range(2):
        halo_tokens.append(push(
            r.tokens.at[pl.ds(m * 128 + 64, 64)], r.halo.at[m, pl.ds(0, 64)], r.token_sems, (0, m), above
        ))
        halo_tokens.append(push(
            r.tokens.at[pl.ds(m * 128, 64)], r.halo.at[m, pl.ds(64, 64)], r.token_sems, (1, m), below
        ))

    pair_count = [0]

    def pair(source, target):
        pair_count[0] += 1
        return push(source, target, r.pair_sems, (pair_count[0] - 1,), place.partner)

    for block in range(4):
        rows = slice(block * 64, block * 64 + 64)
        r.normed[rows, :] = normalised(r.tokens[rows, :])[0].astype(jnp.bfloat16)
    normed_here = pair(r.normed, r.normed_2)
    loads[0].wait()
    for columns in in_columns():
        r.queries[:, columns] = dot_nn(r.normed[...], r.w_qkv[:, columns]).astype(jnp.bfloat16)

    def push_edges(source, target, sems):
        made = []
        for m in range(2):
            made.append(push(source.at[pl.ds(m * 128 + 64, 64)], target.at[m, pl.ds(0, 64)], sems, (0, m), above))
            made.append(push(source.at[pl.ds(m * 128, 64)], target.at[m, pl.ds(64, 64)], sems, (1, m), below))
        return made

    queries_here = push_edges(r.queries, r.queries_h, r.query_sems)
    for part in range(2):
        loads[1 + part].wait()
        for n in range(4):
            at = slice(part * 1024 + n * 256, part * 1024 + n * 256 + 256)
            value = dot_nn(r.normed[...], r.w_qkv[:, slice(at.start + 1024, at.stop + 1024)]).astype(jnp.bfloat16)
            r.kv[0, 0:128, at] = value[:128]
            r.kv[1, 0:128, at] = value[128:]

    row = lax.broadcasted_iota(jnp.int32, (256, 256), 0) % 128
    key = lax.broadcasted_iota(jnp.int32, (256, 256), 1)
    offset = jnp.where(key < 128, key, jnp.where(key < 192, key - 192, key - 64))
    token = space * 128 + offset
    inside = (offset >= row - 64) & (offset <= row + 64) & (token >= 0) & (token < 2048)
    r.window[...] = jnp.where(inside, 1.0, 0.0)
    row = lax.broadcasted_iota(jnp.int32, (256, 128), 0) % 128
    key = lax.broadcasted_iota(jnp.int32, (256, 128), 1)
    offset = jnp.where(row < 64, row - 64, row + 64)
    token = space * 128 + offset
    inside = (key >= offset - 64) & (key <= offset + 64) & (token >= 0) & (token < 2048)
    r.window_h[...] = jnp.where(inside, 1.0, 0.0)
    for group, columns in enumerate(in_columns()):
        local = r.edge_token[:, columns] - space * 128
        weight = r.edge_weight[:, columns]
        places = lax.broadcasted_iota(jnp.int32, (128, 256), 0)
        matrix = jnp.zeros((128, 256), jnp.float32)
        for slot in range(3):
            matrix = matrix + jnp.where(local[slot : slot + 1] == places, weight[slot : slot + 1], 0.0)
        high = matrix.astype(jnp.bfloat16)
        both = jnp.concatenate([high, (matrix - high.astype(jnp.float32)).astype(jnp.bfloat16)], axis=0)
        turned = both.T
        for i in range(2):
            owner = 2 * group + i
            for half in range(2):
                begin = i * 128 + half * 64
                r.edges[half, owner // 4, owner % 4 * 64 : owner % 4 * 64 + 64, :] = turned[begin : begin + 64]
    for half in range(2):
        for quad in range(2):
            r.edges_t[half, quad] = r.edges[half, quad].T

    def edge_keys(m):
        for made in halo_tokens[2 * m : 2 * m + 2]:
            made.wait_recv()
        edges_normed = normalised(r.halo[m])[0].astype(jnp.bfloat16)
        for n in range(8):
            at = slice(n * 256, n * 256 + 256)
            value = dot_nn(edges_normed, r.w_qkv[:, slice(at.start + 1024, at.stop + 1024)])
            r.kv[m, 128:256, at] = value.astype(jnp.bfloat16)

    first = lax.broadcasted_iota(jnp.int32, (128, 128), 1) < 64

    def stacked(value):
        zero = jnp.zeros_like(value)
        return jnp.concatenate([jnp.where(first, value, zero), jnp.where(first, zero, value)], axis=0)

    lane = lax.broadcasted_iota(jnp.int32, (256, 128), 1)
    r.scales[...] = jnp.zeros_like(r.scales)

    def attend(i, carry):
        m, n = i // 8, lax.rem(i, 8)
        start = pl.multiple_of(n * 128, 128)
        columns, values = pl.ds(start, 128), pl.ds(start + 1024, 128)
        token_rows = pl.ds(pl.multiple_of(m * 128, 128), 128)
        scores = dot_nt(stacked(r.queries[token_rows, columns]), r.kv[m, :, columns])
        expo = jnp.where(r.window[...] > 0.0, jnp.exp(scores * 0.125), 0.0)
        scale = 1.0 / jnp.sum(expo, axis=-1, keepdims=True)
        probs = expo * scale
        r.probs[i] = probs
        r.scales[...] = jnp.where(lane == i, scale, r.scales[...])
        result = dot_nn(probs.astype(jnp.bfloat16), r.kv[m, :, values])
        r.att[token_rows, columns] = jnp.where(first, result[:128], result[128:]).astype(jnp.bfloat16)
        return carry

    for m in range(2):
        edge_keys(m)
        lax.fori_loop(m * 8, m * 8 + 8, attend, 0, unroll=8)
    att_here = pair(r.att, r.att_2)
    edge_here = queries_here + push_edges(r.att, r.att_h, r.att_sems)
    for head in range(2):
        begin = head * 128
        edge_here.append(push(
            r.scales.at[pl.ds(begin + 64, 64)], r.scales_h.at[pl.ds(begin, 64)], r.scale_sems, (0, head), above
        ))
        edge_here.append(push(
            r.scales.at[pl.ds(begin, 64)], r.scales_h.at[pl.ds(begin + 64, 64)], r.scale_sems, (1, head), below
        ))
    loads[3].wait()
    for columns in in_columns():
        value = r.tokens[:, columns].astype(jnp.float32) + dot_nn(r.att[...], r.w_out[:, columns])
        r.states[:, columns] = value.astype(jnp.bfloat16)
    states_here = pair(r.states, r.states_2)
    loads[4].wait()
    for columns in in_columns():
        value = dot_nn(r.states[...], r.w_hidden[:, columns]).astype(jnp.bfloat16)
        for m in range(2):
            r.hidden[m, 0:128, columns] = value[m * 128 : m * 128 + 128]
            r.hidden[m, 128:256, columns] = value[m * 128 : m * 128 + 128]

    def give(source, target, i, half, to):
        rows = pl.ds(half * 64, 64)
        return pltpu.make_async_remote_copy(
            src_ref=source.at[to, :, rows], dst_ref=target.at[member, :, rows],
            send_sem=r.member_sems.at[i, half, 0, to], recv_sem=r.member_sems.at[i, half, 1, member],
            device_id=(to, space), device_id_type=MESH,
        )

    def take(target, i, half, source):
        rows = pl.ds(half * 64, 64)
        return pltpu.make_async_remote_copy(
            src_ref=target.at[source, :, rows], dst_ref=target.at[source, :, rows],
            send_sem=r.member_sems.at[i, half, 0, source], recv_sem=r.member_sems.at[i, half, 1, source],
            device_id=(source, space), device_id_type=MESH,
        )

    for half in range(2):
        rows = slice(half * 64, half * 64 + 64)
        for n in range(2):
            quad = 1 - home if n == 0 else home

            def forward(b, carry, half=half, quad=quad, rows=rows):
                forecast = jnp.zeros((256, 128), jnp.float32)
                for columns in in_columns():
                    value, derivative = gelu_both(dot_nn(r.edges[half, quad], r.hidden[b, :, columns]))
                    value = value.astype(jnp.bfloat16)
                    r.active[b, half, quad, :, columns] = value
                    r.slope[b, half, quad, :, columns] = derivative.astype(jnp.bfloat16)
                    forecast = forecast + dot_nn(value, r.readout[columns, :])
                for i in range(4):
                    r.sent[4 * quad + i, b, rows] = forecast[i * 64 : i * 64 + 64].astype(jnp.bfloat16)
                return carry

            lax.fori_loop(0, 2, forward, 0, unroll=2)
            for to in others[3:] if n == 0 else nearby:
                give(r.sent, r.held, 0, half, to).start()
        r.held[member, :, rows] = r.sent[member, :, rows]
    r.area_here[...] = jnp.broadcast_to(r.area[pl.ds(member, 1), :], (128, 128)).T
    loads[5].wait()

    def turn(source, target, begin):
        for columns in in_columns():
            target[columns, begin : begin + 256] = source[:, columns].T

    turn(r.states, r.states_t, 0)
    states_here.wait_recv()
    turn(r.states_2, r.states_t, 256)
    turn(r.att, r.att_t, 0)

    multiplier = math.sqrt(16 / 16384)
    eps_fair = (1.0 - ALPHA) / 16

    def score(block, carry):
        rows = pl.ds(pl.multiple_of(block * 16, 16), 16)
        whole = [r.held[m // 2, m % 2, rows, :].astype(jnp.float32) for m in range(16)]
        truth, area = r.truth[rows, :], r.area_here[rows, :]
        found = [[] for _ in range(16)]
        for half in (slice(0, 8), slice(8, 16)):
            values = [value[half] for value in whole]
            spread = [None] * 16
            for j in range(16):
                for k in range(j + 1, 16):
                    d = values[j] - values[k]
                    s = d * lax.rsqrt(d * d + DELTA * DELTA)
                    spread[j] = s if spread[j] is None else spread[j] + s
                    spread[k] = -s if spread[k] is None else spread[k] - s
            for j in range(16):
                d = values[j] - truth[half]
                s = d * lax.rsqrt(d * d + DELTA * DELTA)
                found[j].append(
                    multiplier * area[half] * (s / 16 - (1.0 - eps_fair) / (16 * 15) * spread[j])
                )
        for j in range(16):
            r.sent_back[j // 2, j % 2, rows, :] = jnp.concatenate(found[j], axis=0).astype(jnp.bfloat16)
        return carry

    for half in range(2):
        rows = slice(half * 64, half * 64 + 64)
        for other in others:
            take(r.held, 0, half, other).wait_recv()
        lax.fori_loop(half * 4, half * 4 + 4, score, 0, unroll=2)
        for other in others:
            give(r.sent_back, r.held_back, 1, half, other).start()
        r.held_back[member, :, rows] = r.sent_back[member, :, rows]
        if half == 0:
            att_here.wait_recv()
            turn(r.att_2, r.att_t, 256)
            turn(r.normed, r.normed_t, 0)
    normed_here.wait_recv()
    turn(r.normed_2, r.normed_t, 256)
    r.gathered[...] = jnp.zeros_like(r.gathered)
    r.turned[...] = jnp.zeros_like(r.turned)
    for half, n in ((0, 0), (0, 1), (1, 0), (1, 1)):
        quad = home if n == 0 else 1 - home
        for other in nearby if n == 0 else others[3:]:
            take(r.held_back, 1, half, other).wait_recv()

        def backward(b, half=half, quad=quad):
            rows = slice(half * 64, half * 64 + 64)
            grad = jnp.concatenate([r.held_back[4 * quad + i, b, rows] for i in range(4)], axis=0)
            grad_t = grad.T
            token_rows = pl.ds(b * 128, 128)
            for columns in in_columns():
                hidden = dot_nt(grad, r.readout[columns, :])
                grad_pre = (hidden * r.slope[b, half, quad, :, columns].astype(jnp.float32)).astype(jnp.bfloat16)
                both = dot_nn(r.edges_t[half, quad], grad_pre)
                r.gathered[token_rows, columns] += both[:128] + both[128:]
                r.turned[:, columns] += dot_nn(grad_t, r.active[b, half, quad, :, columns])

        for b in range(2):
            backward(b)

    mine = pl.ds(pl.multiple_of(core * 512, 512), 512)
    other_half = pl.ds(pl.multiple_of((1 - core) * 512, 512), 512)
    high = r.gathered[...].astype(jnp.bfloat16)
    r.gather_b[...] = high
    gather_here = pair(r.gather_b.at[:, other_half], r.gather_2)
    r.readout_grad[...] = r.turned[...].T.astype(jnp.bfloat16)
    readout_here = pair(r.readout_grad, r.readout_2)
    low = (r.gathered[...] - high.astype(jnp.float32)).astype(jnp.bfloat16)
    stack = jnp.concatenate([high, low], axis=0)
    for rows in in_columns():
        value = dot_nt(stack, r.w_hidden[rows, :])
        value = value[:256] + value[256:]
        r.grad_s[:, rows] = value
        r.grad_sb[:, rows] = value.astype(jnp.bfloat16)
    grad_s_here = pair(r.grad_sb.at[:, other_half], r.grad_s2)

    for rows in in_columns():
        r.grad_att[:, rows] = dot_nt(r.grad_sb[...], r.w_out[rows, :]).astype(jnp.bfloat16)
    edge_here += push_edges(r.grad_att, r.grad_att_h, r.grad_att_sems)

    def early_tile(tile, y, value):
        columns = slice(tile % 3 * 128, tile % 3 * 128 + 128)
        r.early_data[tile // 3, y, :, :, :, :, columns] = value.astype(jnp.bfloat16).reshape(2, 2, 4, 16, 128)

    gather_here.wait_recv()
    both = jnp.concatenate([r.gather_b[:, mine], r.gather_2[...]], axis=0)
    for y, rows in enumerate(in_columns()):
        value = dot_nn(r.states_t[rows, :], both)
        for tile in range(4):
            early_tile(tile, y, value[:, tile * 128 : tile * 128 + 128])
    readout_here.wait_recv()
    for y, rows in enumerate(in_columns()):
        early_tile(8, y, r.readout_grad[rows, :].astype(jnp.float32) + r.readout_2[rows, :].astype(jnp.float32))
    grad_s_here.wait_recv()
    both = jnp.concatenate([r.grad_sb[:, mine], r.grad_s2[...]], axis=0)
    for y, rows in enumerate(in_columns()):
        value = dot_nn(r.att_t[rows, :], both)
        for tile in range(4):
            early_tile(4 + tile, y, value[:, tile * 128 : tile * 128 + 128])

    def ring_sum(data, final, width, scratch):
        def finish(part, total):
            final[:, :, part * width : part * width + width] = total

        return RingSum(place, width, [data.at[part] for part in range(3)], scratch, finish)

    third = len(ring_scratch) // 3
    early = ring_sum(r.early_data, r.early_final, 384, ring_scratch[:third])
    late = [
        ring_sum(r.late_data.at[g], r.late_final.at[g], 256, ring_scratch[third * (1 + g) : third * (2 + g)])
        for g in range(2)
    ]
    for part in range(3):
        early.open(part, 0)

    def attend_back(i, carry):
        n, m = i // 2, lax.rem(i, 2)
        start = pl.multiple_of(n * 128, 128)
        columns, values = pl.ds(start, 128), pl.ds(start + 1024, 128)
        token_rows = pl.ds(pl.multiple_of(m * 128, 128), 128)
        turn_index = m * 8 + n
        queries = stacked(r.queries[token_rows, columns])
        grads = stacked(r.grad_att[token_rows, columns])
        att = r.att[token_rows, columns].astype(jnp.float32)
        inner = jnp.sum(grads.astype(jnp.float32) * jnp.concatenate([att, att], axis=0), axis=-1, keepdims=True)
        probs = r.probs[turn_index]
        dprob = dot_nt(grads, r.kv[m, :, values])
        dscore = (probs * (dprob - inner) * 0.125).astype(jnp.bfloat16)
        grad_q = dot_nn(dscore, r.kv[m, :, columns])
        r.grad_qkv[token_rows, columns] = jnp.where(first, grad_q[:128], grad_q[128:]).astype(jnp.bfloat16)

        local = pl.multiple_of(lax.rem(n, 4) * 128, 128)
        r.gathered[token_rows, pl.ds(local, 128)] = dot_tn(dscore[:, :128], queries)
        r.gathered[token_rows, pl.ds(local + 512, 128)] = dot_tn(probs[:, :128].astype(jnp.bfloat16), grads)
        return carry

    def attend_back_edges(i, carry):
        n, m = i // 2, lax.rem(i, 2)
        start = pl.multiple_of(n * 128, 128)
        columns, values = pl.ds(start, 128), pl.ds(start + 1024, 128)
        token_rows = pl.ds(pl.multiple_of(m * 128, 128), 128)
        queries_h = stacked(r.queries_h[m, :, columns])
        grads_h = stacked(r.grad_att_h[m, :, columns])
        att = r.att_h[m, :, columns].astype(jnp.float32)
        inner = jnp.sum(grads_h.astype(jnp.float32) * jnp.concatenate([att, att], axis=0), axis=-1, keepdims=True)
        scale = jnp.sum(jnp.where(lane == m * 8 + n, r.scales_h[...], 0.0), axis=-1, keepdims=True)
        scores = dot_nt(queries_h, r.kv[m, 0:128, columns])
        probs_h = jnp.where(r.window_h[...] > 0.0, jnp.exp(scores * 0.125) * scale, 0.0)
        dprob = dot_nt(grads_h, r.kv[m, 0:128, values])
        dscore_h = (probs_h * (dprob - inner) * 0.125).astype(jnp.bfloat16)
        local = pl.multiple_of(lax.rem(n, 4) * 128, 128)
        grad_k = r.gathered[token_rows, pl.ds(local, 128)] + dot_tn(dscore_h, queries_h)
        grad_v = r.gathered[token_rows, pl.ds(local + 512, 128)] + dot_tn(probs_h.astype(jnp.bfloat16), grads_h)
        r.grad_qkv[token_rows, values] = grad_k.astype(jnp.bfloat16)
        r.grad_qkv[token_rows, pl.ds(start + 2048, 128)] = grad_v.astype(jnp.bfloat16)
        return carry

    def own_columns(group, part, which):
        return pl.ds(pl.multiple_of(part * 1024 + group * 512 + which * 256, 256), 256)

    def swap(group):
        return [
            pair(r.grad_qkv.at[:, own_columns(group, part, 1 - core)], r.grad_qkv2.at[group, part])
            for part in range(3)
        ]

    def late_products(group, swaps):
        for part in range(3):
            swaps[part].wait_recv()
            both = jnp.concatenate(
                [r.grad_qkv[:, own_columns(group, part, core)], r.grad_qkv2[group, part]], axis=0
            )
            for y, rows in enumerate(in_columns()):
                value = dot_nn(r.normed_t[rows, :], both)
                r.late_data[group, part, y] = value.astype(jnp.bfloat16).reshape(2, 2, 4, 16, 256)
            late[group].open(part, 0)

    lax.fori_loop(0, 8, attend_back, 0, unroll=8)
    for made in edge_here:
        made.wait_recv()
    lax.fori_loop(0, 8, attend_back_edges, 0, unroll=8)
    swaps = swap(0)
    early.relays()
    lax.fori_loop(8, 16, attend_back, 0, unroll=8)
    late_products(0, swaps)
    lax.fori_loop(8, 16, attend_back_edges, 0, unroll=8)
    swaps = swap(1)
    early.advance(0)
    late[0].relays()
    late_products(1, swaps)

    def back_normed(part):
        rows = slice(part * 256, part * 256 + 256)
        r.gathered[:, rows] = dot_nt(r.grad_qkv[...], r.w_qkv[rows, :])

    back_normed(0)
    early.advance(1)
    back_normed(1)
    late[0].advance(0)
    back_normed(2)
    late[1].relays()
    back_normed(3)
    early.advance(2)
    for block in range(4):
        rows = slice(block * 64, block * 64 + 64)
        normal_hat, inverse = normalised(r.tokens[rows, :])
        back = norm_back(r.gathered[rows, :], normal_hat, inverse)
        r.grad_tokens[rows, :] = (r.grad_s[rows, :] + back).astype(jnp.bfloat16)
    late[0].advance(1)
    late[1].advance(0)
    late[0].advance(2)
    late[1].advance(1)

    for half in range(2):
        at = slice(half * 512, half * 512 + 512)
        r.grad_hidden_w[:, at] = r.early_final[half, :, :512]
        r.grad_out_w[:, at] = r.early_final[half, :, 512:1024]
    r.grad_readout[...] = r.early_final[0, :, 1024:]
    late[1].advance(2)
    for group in range(2):
        for part in range(3):
            for half in range(2):
                begin = part * 1024 + group * 512 + half * 256
                r.grad_qkv_w[:, begin : begin + 256] = r.late_final[group, half, :, part * 256 : part * 256 + 256]
    for made in sent_copies:
        made.wait_send()
    for other in others:
        for half in range(2):
            give(r.sent, r.held, 0, half, other).wait_send()
            give(r.sent_back, r.held_back, 1, half, other).wait_send()
    for sums in (early, *late):
        sums.drain()


def handed_on(*refs):
    count = len(refs) // 2
    for source, target in zip(refs[:count], refs[count:]):
        target[...] = source[...]


def on_device(
    tokens, w_qkv, w_out, w_hidden, decoder_readout_matrix, edge_token, edge_weight, truth_state, area
):
    vmem, anywhere = pl.BlockSpec(memory_space=pltpu.VMEM), pl.BlockSpec(memory_space=pl.ANY)
    dma = pltpu.SemaphoreType.DMA

    def b16(*shape):
        return pltpu.VMEM(shape, jnp.bfloat16)

    def f32(*shape):
        return pltpu.VMEM(shape, jnp.float32)

    inputs = {
        "tokens": (tokens.reshape(256, 1024), vmem),
        "w_qkv_hbm": (w_qkv, anywhere),
        "w_out_hbm": (w_out, anywhere),
        "w_hidden_hbm": (w_hidden, anywhere),
        "readout": (decoder_readout_matrix, vmem),
        "edge_token": (edge_token.T, vmem),
        "edge_weight": (edge_weight.T, vmem),
        "truth_hbm": (truth_state, anywhere),
        "area": (area.reshape(8, 128), vmem),
    }
    outputs = {
        "grad_tokens": jax.ShapeDtypeStruct((256, 1024), jnp.bfloat16),
        "grad_qkv_w": jax.ShapeDtypeStruct((8, 3072), jnp.float32),
        "grad_out_w": jax.ShapeDtypeStruct((8, 1024), jnp.float32),
        "grad_hidden_w": jax.ShapeDtypeStruct((8, 1024), jnp.float32),
        "grad_readout": jax.ShapeDtypeStruct((8, 128), jnp.float32),
    }
    scratch = {
        "w_qkv": b16(1024, 3072), "w_out": b16(1024, 1024), "w_hidden": b16(1024, 1024), "truth": f32(128, 128),
        "area_here": f32(128, 128), "halo": b16(2, 128, 1024), "normed": b16(256, 1024), "normed_2": b16(256, 1024),
        "queries": b16(256, 1024), "kv": b16(2, 256, 2048), "window": f32(256, 256), "window_h": f32(256, 128), "scales": f32(256, 128), "scales_h": f32(256, 128),
        "queries_h": b16(2, 128, 1024), "att_h": b16(2, 128, 1024), "grad_att_h": b16(2, 128, 1024),
        "states_t": b16(1024, 512), "att_t": b16(1024, 512), "normed_t": b16(1024, 512),
        "probs": f32(16, 256, 256),
        "att": b16(256, 1024), "att_2": b16(256, 1024), "states": b16(256, 1024), "states_2": b16(256, 1024),
        "hidden": b16(2, 256, 1024), "edges": b16(2, 2, 256, 256), "edges_t": b16(2, 2, 256, 256),
        "active": b16(2, 2, 2, 256, 1024), "slope": b16(2, 2, 2, 256, 1024),
        "sent": b16(8, 2, 128, 128), "held": b16(8, 2, 128, 128),
        "sent_back": b16(8, 2, 128, 128), "held_back": b16(8, 2, 128, 128), "turned": f32(128, 1024),
        "gathered": f32(256, 1024), "gather_b": b16(256, 1024), "gather_2": b16(256, 512),
        "grad_s": f32(256, 1024), "grad_sb": b16(256, 1024), "grad_s2": b16(256, 512), "grad_att": b16(256, 1024),
        "readout_grad": b16(1024, 128), "readout_2": b16(1024, 128), "grad_qkv": b16(256, 3072),
        "grad_qkv2": b16(2, 3, 256, 256),
        "early_data": b16(3, *FULL, 16, 384), "late_data": b16(2, 3, *FULL, 16, 256),
        "early_final": f32(2, 8, 1152), "late_final": f32(2, 2, 8, 768),
        "load_sems": dma((6,)), "token_sems": dma((2, 2, 2)), "pair_sems": dma((2, 12)), "query_sems": dma((2, 2, 2)),
        "att_sems": dma((2, 2, 2)), "scale_sems": dma((2, 2, 2)), "grad_att_sems": dma((2, 2, 2)),
        "member_sems": dma((2, 2, 2, 8)),
    }
    names = [*inputs, *outputs, *scratch]
    results = pl.pallas_call(
        functools.partial(kernel, names),
        out_shape=tuple(outputs.values()),
        in_specs=[spec for _, spec in inputs.values()],
        out_specs=[vmem] * len(outputs),
        scratch_shapes=[*scratch.values(), *sum_scratch(384), *sum_scratch(256), *sum_scratch(256)],
        compiler_params=pltpu.CompilerParams(
            collective_id=0, has_side_effects=True, vmem_limit_bytes=62 * 2**20
        ),
    )(*[value for value, _ in inputs.values()])
    results = pl.pallas_call(
        handed_on,
        out_shape=tuple(outputs.values()),
        in_specs=[vmem] * len(outputs),
        out_specs=[vmem] * len(outputs),
    )(*results)
    return (results[0].reshape(tokens.shape), *results[1:])


def solution(mesh):
    in_specs = (
        P("member", "space", None),
        P(),
        P(),
        P(),
        P(),
        P("space", None),
        P("space", None),
        P("space", None),
        P("space"),
    )
    out_specs = (
        P("member", "space", None),
        P(("member", "space"), None),
        P(("member", "space"), None),
        P(("member", "space"), None),
        P(("member", "space"), None),
    )
    return jax.shard_map(
        on_device, mesh=mesh, in_specs=in_specs, out_specs=out_specs, check_vma=False
    )
```
